32 devices in a mesh: lat: 4 (over x, core), lon: 8 (over z, y).
Axes of the slice: x: 2, y: 2, z: 4, core: 2. Of those that a mesh axis runs over, the one named last changes fastest.
Arguments:
- pre_act: bfloat16 [256, 256, 256], P('lat', 'lon'), may hold values from -8 to 8
- cotangent: bfloat16 [256, 256, 256], P('lat', 'lon'), may hold values from -6 to 6
- spec_weight: float32 [128, 2, 256], replicated, may hold values from -3 to 3
- disco_weight: bfloat16 [3, 256, 256], replicated, may hold values from -0.375 to 0.375
- disco_filter: float32 [3, 256, 5, 5], replicated, may hold values from -0.6 to 0.6
- support: int32 [256, 5], replicated, may hold values from 0 to 2
Outputs:
- grad_input: bfloat16 [256, 256, 256], P('lat', 'lon')
The draws below stay inside these ranges and needn't reach their ends.
All inputs are finite; a program needn't handle non-finite values.
Results may differ from the reference program's by a relative error of at most 0.007.
Values may be sent and summed in bfloat16 or wider, within the bound.
No kernel may reach another device: no remote copies, remote signals or barrier semaphores. Data moves between devices by JAX's collectives and lax.ppermute only.
A program may use at most 192 MiB of HBM per device.

```python
import math
import jax
import jax.numpy as jnp
from jax import lax

C = 256
KERNELS = 3
REACH = 2
TAPS = 5
NLAT = 256
NLON = 256
MODES = 128


def draw_support(key, part):
    base_key = jax.random.fold_in(key, 11)
    key_one, key_two, key_three = jax.random.split(base_key, 3)
    reaches = jax.random.randint(key_one, (NLAT, TAPS), 0, REACH + 1)
    high_row = jax.random.randint(key_two, (), 0, NLAT)
    low_row = jax.random.randint(key_three, (), 0, NLAT)
    reaches = reaches.at[high_row, 0].set(REACH)
    reaches = reaches.at[low_row, TAPS - 1].set(0)
    return reaches.astype(jnp.int32)


def level_of(stream_key, dims, pieces, low, top_value):
    def one(axis_at, parts):
        draws = jax.random.uniform(jax.random.fold_in(jax.random.fold_in(stream_key, 6), axis_at), (parts,), jnp.float32, low / len(pieces), top_value / len(pieces))
        return jnp.repeat(jnp.exp(draws), dims[axis_at] // parts).reshape((-1,) + (1,) * (len(dims) - axis_at - 1))

    gain = one(*pieces[0])
    for cut in pieces[1:]:
        gain = gain * one(*cut)
    return gain


def gaussian(key, extent, width, bound, pieces=(), kind=jnp.bfloat16):
    gain = level_of(key, extent, pieces, -0.22, 0.18) if pieces else 1.0
    array = jax.random.normal(key, extent, jnp.float32) * width * gain
    return jnp.minimum(jnp.maximum(array, -bound), bound).astype(kind)


def setup_inputs(seed: int = 0) -> dict:
    key_list = jax.random.split(jax.random.key(seed), 7)
    pre_act = gaussian(key_list[0], (NLAT, NLON, C), 1.5, 8.0, ((0, 4), (1, 8)))
    cotangent = gaussian(key_list[1], (NLAT, NLON, C), 1.0, 6.0, ((0, 4), (1, 8)))
    spec_weight = gaussian(key_list[2], (MODES, 2, C), 0.5, 3.0, (), jnp.float32)
    disco_weight = gaussian(key_list[3], (KERNELS, C, C), C ** -0.5, 0.375)
    disco_filter = gaussian(key_list[4], (KERNELS, NLAT, TAPS, TAPS), 0.12, 0.6, (), jnp.float32)
    support = draw_support(jax.random.fold_in(key_list[6], 71), 0)
    return dict(pre_act=pre_act, cotangent=cotangent, spec_weight=spec_weight, disco_weight=disco_weight, disco_filter=disco_filter, support=support)


def legendre(orders, colatitude, degrees):
    order_vals = orders.astype(jnp.float32)[:, None]
    cosine = jnp.cos(colatitude)[None, :]
    sine_vals = jnp.sin(colatitude)[None, :]
    log_start = 0.5 * jnp.log((2.0 * order_vals + 1.0) / (4.0 * math.pi)) + 0.5 * (lax.lgamma(2.0 * order_vals + 1.0) - order_vals * math.log(4.0) - 2.0 * lax.lgamma(order_vals + 1.0)) + order_vals * jnp.log(sine_vals)
    zero_rows = jnp.zeros(log_start.shape, jnp.float32)

    def advance(state_triple, degree):
        latest, earlier, log_scale = state_triple
        deg_val = degree.astype(jnp.float32)
        upper_term = jnp.maximum(4.0 * deg_val * deg_val - 1.0, 0.0)
        lower_term = jnp.maximum(deg_val * deg_val - order_vals * order_vals, 1.0)
        coef_a = jnp.sqrt(upper_term / lower_term)
        prev_deg = deg_val - 1.0
        coef_b = jnp.sqrt(jnp.maximum(prev_deg * prev_deg - order_vals * order_vals, 0.0) / jnp.maximum(4.0 * prev_deg * prev_deg - 1.0, 1.0))
        recurred = coef_a * (cosine * latest - coef_b * earlier)
        magnitude = jnp.maximum(jnp.abs(recurred), jnp.abs(latest))
        divisor = jnp.where(magnitude > 10000.0, magnitude, 1.0)
        before = deg_val < order_vals
        at_start = deg_val == order_vals
        new_latest = jnp.where(before, 0.0, jnp.where(at_start, 1.0, recurred / divisor))
        new_earlier = jnp.where(before | at_start, 0.0, latest / divisor)
        new_scale = jnp.where(before, 0.0, jnp.where(at_start, log_start, log_scale + jnp.log(divisor)))
        fresh = jnp.where(before, 0.0, new_latest * jnp.exp(new_scale))
        return ((new_latest, new_earlier, new_scale), fresh)
    _, stacked = lax.scan(advance, (zero_rows, zero_rows, zero_rows), jnp.arange(degrees, dtype=jnp.int32))
    return jnp.transpose(stacked, (1, 0, 2))

def fourier_tables(order_list, points):
    grid_pos = jnp.arange(points, dtype=jnp.int32)
    product = grid_pos[:, None] * order_list[None, :] % points
    angles = 2.0 * math.pi / points * product.astype(jnp.float32)
    factor = jnp.where(order_list == 0, 1.0, 2.0).astype(jnp.float32)[None, :]
    forward = jnp.stack([factor * jnp.cos(angles), -factor * jnp.sin(angles)], axis=2)
    inverse = jnp.stack([jnp.cos(angles), -jnp.sin(angles)], axis=2)
    forward = forward.reshape(points, -1).astype(jnp.bfloat16)
    inverse = jnp.transpose(inverse, (1, 2, 0)).reshape(-1, points).astype(jnp.bfloat16)
    return (forward, inverse)

def gelu_slope(pre_values):
    normal_cdf = 0.5 * (1.0 + lax.erf(pre_values * (1.0 / math.sqrt(2.0))))
    density = jnp.exp(-0.5 * pre_values * pre_values) * (1.0 / math.sqrt(2.0 * math.pi))
    return normal_cdf + pre_values * density

def spectral_mix(legendre_tab, coeffs, weights):
    analysed = jnp.einsum('kli,iktc->lktc', legendre_tab.astype(jnp.float32), coeffs.astype(jnp.float32))
    real_w = weights[:, 0, :][:, None, :]
    imag_w = weights[:, 1, :][:, None, :]
    real_b = analysed[:, :, 0, :]
    imag_b = analysed[:, :, 1, :]
    mixed = jnp.stack([real_w * real_b + imag_w * imag_b, real_w * imag_b - imag_w * real_b], axis=2).astype(jnp.bfloat16)
    return jnp.einsum('kli,lktc->iktc', legendre_tab.astype(jnp.float32), mixed.astype(jnp.float32)).astype(jnp.bfloat16)

def reference(pre_act, cotangent, spec_weight, disco_weight, disco_filter, support):
    grad_pre = (cotangent.astype(jnp.float32) * gelu_slope(pre_act.astype(jnp.float32))).astype(jnp.bfloat16)
    order_list = jnp.arange(MODES, dtype=jnp.int32)
    forward, inverse = fourier_tables(order_list, NLON)
    coeffs = jnp.einsum('ijc,jn->inc', grad_pre.astype(jnp.float32), forward.astype(jnp.float32)).astype(jnp.bfloat16)
    block_len = math.gcd(MODES, 16)
    block_count = MODES // block_len
    blocks = jnp.transpose(coeffs.reshape(NLAT, block_count, block_len, 2, C), (1, 0, 2, 3, 4))
    colatitude = math.pi / NLAT * (jnp.arange(NLAT, dtype=jnp.float32) + 0.5)

    def one_block(packed):
        block_idx, block_coeffs = packed
        orders = block_idx * block_len + jnp.arange(block_len, dtype=jnp.int32)
        legendre_tab = legendre(orders, colatitude, MODES).astype(jnp.bfloat16)
        return spectral_mix(legendre_tab, block_coeffs, spec_weight)
    synth_all = lax.map(one_block, (jnp.arange(block_count, dtype=jnp.int32), blocks))
    synth_all = jnp.transpose(synth_all, (1, 0, 2, 3, 4)).reshape(NLAT, 2 * MODES, C)
    quad_weight = 2.0 * math.pi / NLON * (math.pi / NLAT) * jnp.sin(colatitude)
    spectral = (jnp.einsum('inc,nj->ijc', synth_all.astype(jnp.float32), inverse.astype(jnp.float32)) * quad_weight[:, None, None]).astype(jnp.bfloat16)
    mixed_in = jnp.einsum('ijo,kco->ijkc', grad_pre.astype(jnp.float32), disco_weight.astype(jnp.float32)).astype(jnp.bfloat16)
    lon_wrapped = jnp.concatenate([mixed_in[:, NLON - REACH:], mixed_in, mixed_in[:, :REACH]], axis=1)
    padded = jnp.pad(lon_wrapped, ((REACH, REACH), (0, 0), (0, 0), (0, 0)))
    offsets = jnp.arange(TAPS, dtype=jnp.int32) - REACH
    allowed = (jnp.abs(offsets)[None, None, :] <= support[:, :, None]).astype(jnp.float32)
    tap_coef = jnp.pad(disco_filter * allowed[None], ((0, 0), (REACH, REACH), (0, 0), (0, 0)))
    result_sum = spectral.astype(jnp.float32)
    for lat_tap in range(TAPS):
        for lon_tap in range(TAPS):
            row_off = 2 * REACH - lat_tap
            col_off = 2 * REACH - lon_tap
            for kernel in range(KERNELS):
                tap_w = tap_coef[kernel, row_off:row_off + NLAT, lat_tap, lon_tap]
                shifted = padded[row_off:row_off + NLAT, col_off:col_off + NLON, kernel, :].astype(jnp.float32)
                result_sum = result_sum + tap_w[:, None, None] * shifted
    return result_sum.astype(jnp.bfloat16)
```

```python
import functools
import math

import jax
import jax.numpy as jnp
import numpy as np
from jax import lax
from jax.experimental import pallas as pl
from jax.experimental.pallas import tpu as pltpu
from jax.sharding import PartitionSpec as P

REACH = 2
TAPS = 2 * REACH + 1
LANES = 128
F32 = jnp.float32
BF16 = jnp.bfloat16
VMEM_LIMIT = 56 * 1024 * 1024


def params():
    return pltpu.CompilerParams(vmem_limit_bytes=VMEM_LIMIT)


def gelu_slope(pre_values):
    normal_cdf = 0.5 * (1.0 + lax.erf(pre_values * (1.0 / math.sqrt(2.0))))
    density = jnp.exp(-0.5 * pre_values * pre_values) * (1.0 / math.sqrt(2.0 * math.pi))
    return normal_cdf + pre_values * density


def grad_kernel(flip_ref, pre_ref, cot_ref, grad_ref, send_ref, rows_scr, chan_scr, *, group, q_count):
    step = pl.program_id(0)
    rows, cols, channels = pre_ref.shape
    flip = flip_ref[0]
    for row in range(rows):
        pre = pre_ref[row].astype(F32)
        grad = (cot_ref[row].astype(F32) * gelu_slope(pre)).astype(BF16)
        grad_ref[row] = grad
        rows_scr[row] = grad.astype(F32)
    for block in range(rows // group):
        q_index = step * (rows // group) + block
        q_out = jnp.where(flip == 1, q_count - 1 - q_index, q_index)
        parts = []
        for r in range(group):
            source = block * group + jnp.where(flip == 1, group - 1 - r, r)
            parts.append(rows_scr[source])
        stacked = jnp.concatenate(parts, axis=0)
        for tile in range(channels // LANES):
            turned = stacked[:, tile * LANES : (tile + 1) * LANES].T
            chan_scr[pl.ds(tile * LANES * q_count + q_out, LANES, stride=q_count), :] = turned

    @pl.when(step == pl.num_programs(0) - 1)
    def _():
        for dest in range(send_ref.shape[0]):
            count = send_ref.shape[1]
            send_ref[dest] = chan_scr[dest * count : (dest + 1) * count, :].astype(BF16)


def gradient(pre_act, cotangent, flip, devices, group):
    rows, cols, channels = pre_act.shape
    q_count = rows // group
    steps = 4
    block = (rows // steps, cols, channels)
    spec = pl.BlockSpec(block, lambda i: (i, 0, 0))
    send = (devices, channels // devices * q_count, LANES)
    return pl.pallas_call(
        functools.partial(grad_kernel, group=group, q_count=q_count),
        grid=(steps,),
        in_specs=[pl.BlockSpec(memory_space=pltpu.SMEM), spec, spec],
        out_specs=[spec, pl.BlockSpec(send, lambda i: (0, 0, 0))],
        out_shape=[
            jax.ShapeDtypeStruct(pre_act.shape, BF16),
            jax.ShapeDtypeStruct(send, BF16),
        ],
        scratch_shapes=[
            pltpu.VMEM(block, F32),
            pltpu.VMEM((channels * q_count, LANES), F32),
        ],
        compiler_params=params(),
        name="gradient",
    )(flip, pre_act, cotangent)


def legendre_kernel(cos_ref, start_ref, table_ref, scr, *, degrees, span):
    orders = table_ref.shape[0]
    groups = orders // 8
    first = pl.program_id(0) * orders
    cosine = jnp.broadcast_to(cos_ref[...], (8, LANES))
    sub = lax.broadcasted_iota(jnp.int32, (8, LANES), 0)
    order_vals = [(first + 8 * g + sub).astype(F32) for g in range(groups)]
    squares = [order * order for order in order_vals]
    zero = jnp.zeros((8, LANES), F32)

    def chunk(index, state):
        latest, earlier, scale = (list(part) for part in state)
        factor = [jnp.exp(value) for value in scale]
        for step in range(span):
            degree = index * span + step
            deg_val = degree.astype(F32)
            square = deg_val * deg_val
            prev = (deg_val - 1.0) * (deg_val - 1.0)
            upper = jnp.full((8, LANES), jnp.maximum(4.0 * square - 1.0, 0.0))
            lower = jnp.full((8, LANES), jnp.maximum(4.0 * prev - 1.0, 1.0))
            for g in range(groups):
                coef_a = jnp.sqrt(upper / jnp.maximum(square - squares[g], 1.0))
                coef_b = jnp.sqrt(jnp.maximum(prev - squares[g], 0.0) / lower)
                value = coef_a * (cosine * latest[g] - coef_b * earlier[g])
                value = jnp.where(order_vals[g] == deg_val, 1.0, value)
                earlier[g] = latest[g]
                latest[g] = value
                scr[pl.ds(g * 8 * degrees + degree, 8, stride=degrees), :] = value * factor[g]
        for g in range(groups):
            large = jnp.maximum(jnp.abs(latest[g]), jnp.abs(earlier[g])) > 2.0**20
            shrink = jnp.where(large, 2.0**-40, 1.0)
            latest[g] = latest[g] * shrink
            earlier[g] = earlier[g] * shrink
            scale[g] = scale[g] + jnp.where(large, 40.0 * math.log(2.0), 0.0)
        return (tuple(latest), tuple(earlier), tuple(scale))

    starts = tuple(start_ref[8 * g : 8 * g + 8, :] for g in range(groups))
    zeros = (zero,) * groups
    lax.fori_loop(0, degrees // span, chunk, (zeros, zeros, starts))
    for order in range(orders):
        table_ref[order] = scr[order * degrees : (order + 1) * degrees, :].astype(BF16)


def legendre(cosine, start, degrees):
    orders, points = start.shape
    block = math.gcd(orders, 32)
    return pl.pallas_call(
        functools.partial(legendre_kernel, degrees=degrees, span=8),
        grid=(orders // block, points // LANES),
        in_specs=[
            pl.BlockSpec((1, LANES), lambda i, j: (0, j)),
            pl.BlockSpec((block, LANES), lambda i, j: (i, j)),
        ],
        out_specs=pl.BlockSpec((block, degrees, LANES), lambda i, j: (i, 0, j)),
        out_shape=jax.ShapeDtypeStruct((orders, degrees, points), BF16),
        scratch_shapes=[pltpu.VMEM((block * degrees, LANES), F32)],
        compiler_params=params(),
        cost_estimate=pl.CostEstimate(
            flops=40 * orders * degrees * points,
            bytes_accessed=2 * orders * degrees * points,
            transcendentals=0,
        ),
        name="legendre",
    )(cosine, start)


def spectral_kernel(
    recv_ref, forward_ref, inverse_ref, table_ref, weight_ref, quad_ref, back_ref,
    grid_scr, even_scr, odd_scr, north_scr, south_scr, *, group, q_count, unroll,
):
    step = pl.program_id(0)
    bands, sectors = recv_ref.shape[:2]
    local, lats, lons = grid_scr.shape
    orders_here, degrees, half = table_ref.shape
    tiles = half // LANES
    modes = forward_ref.shape[0]
    orders = modes // 2
    band_rows = group * q_count
    width = LANES // group
    lane_group = lax.broadcasted_iota(jnp.int32, (q_count, LANES), 1) // width

    def place(band, r):
        if band < bands // 2:
            return band * band_rows + r * q_count
        return lats // 2 + (bands - 1 - band) * band_rows + r * q_count

    def rolled(value, places):
        shift = places * width % LANES
        return value if shift == 0 else pltpu.roll(value, shift, 1)

    @pl.when(step == 0)
    def _():
        for chan in range(local):
            at = chan * q_count
            for band in range(bands):
                for unit in range(sectors // group):
                    pieces = [
                        recv_ref[band, unit * group + k, at : at + q_count, :].astype(F32)
                        for k in range(group)
                    ]
                    for r in range(group):
                        value = rolled(pieces[0], -r)
                        for k in range(1, group):
                            value = jnp.where(lane_group == k, rolled(pieces[k], k - r), value)
                        row = place(band, r)
                        grid_scr[chan, row : row + q_count, unit * LANES : (unit + 1) * LANES] = (
                            value.astype(BF16)
                        )
            spectrum = lax.dot_general(
                forward_ref[...], grid_scr[chan], (((1,), (1,)), ((), ())), preferred_element_type=F32
            )
            for tile in range(tiles):
                north = spectrum[:, tile * LANES : (tile + 1) * LANES]
                south = spectrum[:, half + tile * LANES : half + (tile + 1) * LANES]
                even_scr[tile, chan * modes : (chan + 1) * modes, :] = north + south
                odd_scr[tile, chan * modes : (chan + 1) * modes, :] = north - south

    def lines(scr, tile, mode):
        if local == 1:
            return (tile, pl.ds(mode, 1), slice(None))
        return (tile, pl.ds(mode, local, stride=modes), slice(None))

    def load(scr, mode):
        parts = [scr[lines(scr, tile, mode)] for tile in range(tiles)]
        return parts[0] if tiles == 1 else jnp.concatenate(parts, axis=1)

    degree_lane = lax.broadcasted_iota(jnp.int32, (local, degrees), 1)
    real_w = weight_ref[0]
    imag_w = weight_ref[1]
    quad = quad_ref[...]

    def one_order(index):
        order = step * orders_here + index
        table = table_ref[index]
        even = (degree_lane + order) % 2 == 0
        stacked = jnp.concatenate(
            [
                load(even_scr, order),
                load(even_scr, orders + order),
                load(odd_scr, order),
                load(odd_scr, orders + order),
            ],
            axis=0,
        ).astype(BF16)
        analysed = lax.dot_general(
            stacked, table, (((1,), (1,)), ((), ())), preferred_element_type=F32
        )
        real_a = jnp.where(even, analysed[0:local], analysed[2 * local : 3 * local])
        imag_a = jnp.where(even, analysed[local : 2 * local], analysed[3 * local : 4 * local])
        real_m = real_w * real_a + imag_w * imag_a
        imag_m = real_w * imag_a - imag_w * real_a
        mixed = jnp.concatenate(
            [
                jnp.where(even, real_m, 0.0),
                jnp.where(even, imag_m, 0.0),
                jnp.where(even, 0.0, real_m),
                jnp.where(even, 0.0, imag_m),
            ],
            axis=0,
        ).astype(BF16)
        synth = jnp.dot(mixed, table, preferred_element_type=F32) * quad
        for part in range(2):
            even_part = synth[part * local : (part + 1) * local]
            odd_part = synth[(2 + part) * local : (3 + part) * local]
            for tile in range(tiles):
                lanes = slice(tile * LANES, (tile + 1) * LANES)
                where = lines(north_scr, tile, part * orders + order)
                north_scr[where] = even_part[:, lanes] + odd_part[:, lanes]
                south_scr[where] = even_part[:, lanes] - odd_part[:, lanes]

    def several(index, carry):
        for inner in range(unroll):
            one_order(index * unroll + inner)
        return carry

    lax.fori_loop(0, orders_here // unroll, several, 0)

    @pl.when(step == pl.num_programs(0) - 1)
    def _():
        for chan in range(local):
            rows = slice(chan * modes, (chan + 1) * modes)
            profile = jnp.concatenate(
                [scr[tile, rows, :].astype(BF16) for scr in (north_scr, south_scr) for tile in range(tiles)],
                axis=1,
            )
            field = lax.dot_general(
                profile, inverse_ref[...], (((0,), (0,)), ((), ())), preferred_element_type=F32
            )
            at = chan * q_count
            for band in range(bands):
                for unit in range(sectors // group):
                    pieces = []
                    for r in range(group):
                        row = place(band, r)
                        pieces.append(field[row : row + q_count, unit * LANES : (unit + 1) * LANES])
                    for k in range(group):
                        value = rolled(pieces[0], -k)
                        for r in range(1, group):
                            value = jnp.where(lane_group == r, rolled(pieces[r], r - k), value)
                        back_ref[band, unit * group + k, at : at + q_count, :] = value.astype(BF16)


def spectral(received, forward, inverse, table, weights, quad, group):
    bands, sectors, rows, _ = received.shape
    local = weights.shape[1]
    q_count = rows // local
    orders, degrees, half = table.shape
    lons = forward.shape[1]
    block = max(1, min(orders, 2**19 // (degrees * half)))
    tiles = half // LANES

    def whole(shape):
        return pl.BlockSpec(shape, lambda i: (0,) * len(shape))

    lines = pltpu.VMEM((tiles, local * forward.shape[0], LANES), F32)
    return pl.pallas_call(
        functools.partial(spectral_kernel, group=group, q_count=q_count, unroll=math.gcd(block, 8)),
        grid=(orders // block,),
        in_specs=[
            whole(received.shape),
            whole(forward.shape),
            whole(inverse.shape),
            pl.BlockSpec((block, degrees, half), lambda i: (i, 0, 0)),
            whole(weights.shape),
            whole(quad.shape),
        ],
        out_specs=whole(received.shape),
        out_shape=jax.ShapeDtypeStruct(received.shape, BF16),
        scratch_shapes=[pltpu.VMEM((local, 2 * half, lons), BF16), lines, lines, lines, lines],
        compiler_params=params(),
        name="spectral",
    )(received, forward, inverse, table, weights, quad)


def disco_kernel(tap_ref, grad_ref, low_ref, high_ref, left_ref, right_ref, mix_ref, out_ref, padded, taps_scr):
    step = pl.program_id(0)
    rows, cols, channels = grad_ref.shape
    rows_here = out_ref.shape[0]
    kernels = mix_ref.shape[0]
    halves = channels // LANES
    origin = 8

    @pl.when(step == 0)
    def _():
        for half in range(halves):
            lanes = slice(half * LANES, (half + 1) * LANES)
            padded[half, REACH : REACH + rows, origin : origin + cols, :] = grad_ref[:, :, lanes].astype(F32)
            padded[half, 0:REACH, origin : origin + cols, :] = low_ref[:, :, lanes].astype(F32)
            padded[half, REACH + rows :, origin : origin + cols, :] = high_ref[:, :, lanes].astype(F32)
            for side in range(REACH):
                padded[half, :, origin - REACH + side, :] = left_ref[side, :, lanes].astype(F32)
                padded[half, :, origin + cols + side, :] = right_ref[side, :, lanes].astype(F32)

    def one_row(row, carry):
        for half in range(halves):
            sums = [jnp.zeros((cols, LANES), F32) for _ in range(kernels)]
            for lat_tap in range(TAPS):
                source = step * rows_here + row + 2 * REACH - lat_tap
                for lon_tap in range(TAPS):
                    start = origin + REACH - lon_tap
                    slab = padded[half, source, start : start + cols, :]
                    for kernel in range(kernels):
                        tap = tap_ref[source, (kernel * TAPS + lat_tap) * TAPS + lon_tap]
                        sums[kernel] = sums[kernel] + tap * slab
            for kernel in range(kernels):
                taps_scr[kernel, row, :, half * LANES : (half + 1) * LANES] = sums[kernel].astype(BF16)
        return carry

    lax.fori_loop(0, rows_here, one_row, 0)
    total = None
    for kernel in range(kernels):
        flat = taps_scr[kernel].reshape(rows_here * cols, channels)
        term = lax.dot_general(
            flat, mix_ref[kernel], (((1,), (1,)), ((), ())), preferred_element_type=F32
        )
        total = term if total is None else total + term
    out_ref[...] = total.reshape(rows_here, cols, channels)


def disco(taps, grad, low, high, left, right, mix):
    rows, cols, channels = grad.shape
    kernels = mix.shape[0]
    steps = 4

    def whole(shape):
        return pl.BlockSpec(shape, lambda i: (0,) * len(shape))

    return pl.pallas_call(
        disco_kernel,
        grid=(steps,),
        in_specs=[pl.BlockSpec(memory_space=pltpu.SMEM)]
        + [whole(value.shape) for value in (grad, low, high, left, right, mix)],
        out_specs=pl.BlockSpec((rows // steps, cols, channels), lambda i: (i, 0, 0)),
        out_shape=jax.ShapeDtypeStruct(grad.shape, F32),
        scratch_shapes=[
            pltpu.VMEM((channels // LANES, rows + 2 * REACH, cols + 16, LANES), F32),
            pltpu.VMEM((kernels, rows // steps, cols, channels), BF16),
        ],
        compiler_params=params(),
        cost_estimate=pl.CostEstimate(
            flops=1000 * rows * cols * channels, bytes_accessed=8 * rows * cols * channels, transcendentals=0
        ),
        name="disco",
    )(taps, grad, low, high, left, right, mix)


def combine_kernel(flip_ref, back_ref, disco_ref, out_ref, chan_scr, *, group, q_count):
    step = pl.program_id(0)
    rows, cols, channels = out_ref.shape
    flip = flip_ref[0]

    @pl.when(step == 0)
    def _():
        count = back_ref.shape[1]
        for source in range(back_ref.shape[0]):
            chan_scr[source * count : (source + 1) * count, :] = back_ref[source].astype(F32)

    for block in range(rows // group):
        q_index = step * (rows // group) + block
        q_from = jnp.where(flip == 1, q_count - 1 - q_index, q_index)
        turned = jnp.concatenate(
            [
                chan_scr[pl.ds(tile * LANES * q_count + q_from, LANES, stride=q_count), :].T
                for tile in range(channels // LANES)
            ],
            axis=1,
        )
        for r in range(group):
            row = block * group + jnp.where(flip == 1, group - 1 - r, r)
            out_ref[row] = (disco_ref[row] + turned[r * cols : (r + 1) * cols]).astype(BF16)


def combine(back, local_part, flip, group):
    rows, cols, channels = local_part.shape
    q_count = rows // group
    steps = 4
    spec = pl.BlockSpec((rows // steps, cols, channels), lambda i: (i, 0, 0))
    return pl.pallas_call(
        functools.partial(combine_kernel, group=group, q_count=q_count),
        grid=(steps,),
        in_specs=[pl.BlockSpec(memory_space=pltpu.SMEM), pl.BlockSpec(back.shape, lambda i: (0, 0, 0)), spec],
        out_specs=spec,
        out_shape=jax.ShapeDtypeStruct(local_part.shape, BF16),
        scratch_shapes=[pltpu.VMEM((channels * q_count, LANES), F32)],
        compiler_params=params(),
        name="combine",
    )(flip, back, local_part)


def neighbours(axis, block_low, block_high):
    count = lax.axis_size(axis)
    forward = [(i, (i + 1) % count) for i in range(count)]
    backward = [(target, source) for source, target in forward]
    return (lax.ppermute(block_low, axis, forward), lax.ppermute(block_high, axis, backward))


def fourier_tables(order_count, points):
    order_list = jnp.arange(order_count, dtype=jnp.int32)[:, None]
    grid_pos = jnp.arange(points, dtype=jnp.int32)[None, :]
    angles = 2.0 * math.pi / points * (grid_pos * order_list % points).astype(F32)
    factor = jnp.where(order_list == 0, 1.0, 2.0).astype(F32)
    inverse = jnp.concatenate([jnp.cos(angles), -jnp.sin(angles)], axis=0)
    forward = jnp.concatenate([factor, factor], axis=0) * inverse
    return (forward.astype(BF16), inverse.astype(BF16))


def shards(pre_act, cotangent, spec_weight, disco_weight, disco_filter, support):
    lat_rows, lon_cols, channels = pre_act.shape
    lat_count = lax.axis_size("lat")
    lon_count = lax.axis_size("lon")
    devices = lat_count * lon_count
    band_index = lax.axis_index("lat")
    device_id = band_index * lon_count + lax.axis_index("lon")
    total_lat = lat_rows * lat_count
    total_lon = lon_cols * lon_count
    mode_count = spec_weight.shape[0]
    local = channels // devices
    group = LANES // lon_cols
    q_count = lat_rows // group
    flip = (2 * band_index >= lat_count).astype(jnp.int32).reshape(1)

    grad_pre, to_send = gradient(pre_act, cotangent, flip, devices, group)
    received = lax.all_to_all(to_send, ("lat", "lon"), 0, 0, tiled=True)

    low, high = neighbours("lat", grad_pre[-REACH:], grad_pre[:REACH])
    west = jnp.concatenate([part[:, :REACH] for part in (low, grad_pre, high)], axis=0)
    east = jnp.concatenate([part[:, -REACH:] for part in (low, grad_pre, high)], axis=0)
    left, right = neighbours("lon", jnp.transpose(east, (1, 0, 2)), jnp.transpose(west, (1, 0, 2)))

    lane = np.arange(total_lat // 2)
    lats = lane // lat_rows * lat_rows + lane % q_count * group + lane % lat_rows // q_count
    colatitude = math.pi / total_lat * (jnp.asarray(lats, F32) + 0.5)[None, :]
    order_vals = jnp.arange(mode_count, dtype=F32)[:, None]
    start = (
        0.5 * jnp.log((2.0 * order_vals + 1.0) / (4.0 * math.pi))
        + 0.5
        * (
            lax.lgamma(2.0 * order_vals + 1.0)
            - order_vals * math.log(4.0)
            - 2.0 * lax.lgamma(order_vals + 1.0)
        )
        + order_vals * jnp.log(jnp.sin(colatitude))
    )
    table = legendre(jnp.cos(colatitude), start, mode_count)
    forward, inverse = fourier_tables(mode_count, total_lon)
    quad = 2.0 * math.pi / total_lon * (math.pi / total_lat) * jnp.sin(colatitude)
    weights = jnp.transpose(
        lax.dynamic_slice_in_dim(spec_weight, device_id * local, local, 2), (1, 2, 0)
    )
    offsets = jnp.arange(TAPS, dtype=jnp.int32) - REACH
    allowed = (jnp.abs(offsets)[None, None, :] <= support[:, :, None]).astype(F32)
    tap_coef = jnp.pad(disco_filter * allowed[None], ((0, 0), (REACH, REACH), (0, 0), (0, 0)))
    tap_coef = lax.dynamic_slice_in_dim(tap_coef, band_index * lat_rows, lat_rows + 2 * REACH, 1)
    taps = jnp.transpose(tap_coef, (1, 0, 2, 3)).reshape(lat_rows + 2 * REACH, -1)

    blocks = received.reshape(lat_count, lon_count, local * q_count, LANES)
    back = spectral(blocks, forward, inverse, table, weights, quad, group)
    back, taps = lax.optimization_barrier((back, taps))
    returned = lax.all_to_all(
        back.reshape(devices, local * q_count, LANES), ("lat", "lon"), 0, 0, tiled=True
    )
    local_part = disco(taps, grad_pre, low, high, left, right, disco_weight)
    return combine(returned, local_part, flip, group)


def solution(mesh):
    return jax.shard_map(
        shards,
        mesh=mesh,
        in_specs=(P("lat", "lon", None), P("lat", "lon", None), P(), P(), P(), P()),
        out_specs=P("lat", "lon", None),
        check_vma=False,
    )
```

```python
import functools
import math

import jax
import jax.numpy as jnp
import numpy as np
from jax import lax
from jax.experimental import pallas as pl
from jax.experimental.pallas import tpu as pltpu
from jax.sharding import PartitionSpec as P

REACH = 2
TAPS = 2 * REACH + 1
LANES = 128
F32 = jnp.float32
BF16 = jnp.bfloat16
MIB = 1024 * 1024


def params(limit):
    return pltpu.CompilerParams(vmem_limit_bytes=limit)


def gelu_slope(pre_values):
    normal_cdf = 0.5 * (1.0 + lax.erf(pre_values * (1.0 / math.sqrt(2.0))))
    density = jnp.exp(-0.5 * pre_values * pre_values) * (1.0 / math.sqrt(2.0 * math.pi))
    return normal_cdf + pre_values * density


def grad_kernel(
    flip_ref, pre_ref, cot_ref, grad_ref, send_ref, first_ref, last_ref, rows_scr, chan_scr, *, group, q_count
):
    step = pl.program_id(0)
    rows, cols, channels = pre_ref.shape
    flip = flip_ref[0]
    for row in range(rows):
        pre = pre_ref[row].astype(F32)
        grad = (cot_ref[row].astype(F32) * gelu_slope(pre)).astype(BF16)
        grad_ref[row] = grad
        rows_scr[row] = grad.astype(F32)
    for block in range(rows // group):
        q_index = step * (rows // group) + block
        q_out = jnp.where(flip == 1, q_count - 1 - q_index, q_index)
        parts = []
        for r in range(group):
            source = block * group + jnp.where(flip == 1, group - 1 - r, r)
            parts.append(rows_scr[source])
        stacked = jnp.concatenate(parts, axis=0)
        for tile in range(channels // LANES):
            turned = stacked[:, tile * LANES : (tile + 1) * LANES].T
            chan_scr[pl.ds(tile * LANES * q_count + q_out, LANES, stride=q_count), :] = turned

    @pl.when(step == 0)
    def _():
        first_ref[...] = grad_ref[:REACH]

    @pl.when(step == pl.num_programs(0) - 1)
    def _():
        last_ref[...] = grad_ref[rows - REACH :]
        for dest in range(send_ref.shape[0]):
            count = send_ref.shape[1]
            send_ref[dest] = chan_scr[dest * count : (dest + 1) * count, :].astype(BF16)


def gradient(pre_act, cotangent, flip, devices, group):
    rows, cols, channels = pre_act.shape
    q_count = rows // group
    steps = 4
    block = (rows // steps, cols, channels)
    spec = pl.BlockSpec(block, lambda i: (i, 0, 0))
    send = (devices, channels // devices * q_count, LANES)
    edge = (REACH, cols, channels)
    return pl.pallas_call(
        functools.partial(grad_kernel, group=group, q_count=q_count),
        grid=(steps,),
        in_specs=[pl.BlockSpec(memory_space=pltpu.SMEM), spec, spec],
        out_specs=[spec, pl.BlockSpec(send, lambda i: (0, 0, 0))] + [pl.BlockSpec(edge, lambda i: (0, 0, 0))] * 2,
        out_shape=[jax.ShapeDtypeStruct(shape, BF16) for shape in (pre_act.shape, send, edge, edge)],
        scratch_shapes=[
            pltpu.VMEM(block, F32),
            pltpu.VMEM((channels * q_count, LANES), F32),
        ],
        compiler_params=params(60 * MIB),
        name="gradient",
    )(flip, pre_act, cotangent)


def legendre_kernel(norm_ref, cos_ref, start_ref, *refs, degrees, span):
    scr = refs[-1]
    table_ref = refs[0]
    orders = table_ref.shape[0]
    groups = orders // 8
    first = pl.program_id(0) * orders
    cosine = jnp.broadcast_to(cos_ref[...], (8, LANES))
    sub = lax.broadcasted_iota(jnp.int32, (8, LANES), 0)
    order_vals = [(first + 8 * g + sub).astype(F32) for g in range(groups)]
    squares = [order * order for order in order_vals]
    zero = jnp.zeros((8, LANES), F32)

    def chunk(index, state):
        latest, earlier, coef_b, scale = (list(part) for part in state)
        factor = [jnp.exp(value) for value in scale]
        for step in range(span):
            degree = index * span + step
            deg_val = degree.astype(F32)
            norm = norm_ref[0, degree]
            inverse_norm = norm_ref[1, degree]
            for g in range(groups):
                gap = jnp.maximum(deg_val * deg_val - squares[g], 1.0)
                root = lax.rsqrt(gap)
                value = (root * norm) * (cosine * latest[g] - coef_b[g] * earlier[g])
                value = jnp.where(order_vals[g] == deg_val, 1.0, value)
                coef_b[g] = gap * root * inverse_norm
                earlier[g] = latest[g]
                latest[g] = value
                scr[pl.ds(g * 8 * degrees + degree, 8, stride=degrees), :] = value * factor[g]
        for g in range(groups):
            large = jnp.maximum(jnp.abs(latest[g]), jnp.abs(earlier[g])) > 2.0**20
            shrink = jnp.where(large, 2.0**-40, 1.0)
            latest[g] = latest[g] * shrink
            earlier[g] = earlier[g] * shrink
            scale[g] = scale[g] + jnp.where(large, 40.0 * math.log(2.0), 0.0)
        return (tuple(latest), tuple(earlier), tuple(coef_b), tuple(scale))

    starts = tuple(start_ref[8 * g : 8 * g + 8, :] for g in range(groups))
    zeros = (zero,) * groups
    lax.fori_loop(0, degrees // span, chunk, (zeros, zeros, zeros, starts))
    for order in range(orders):
        values = scr[order * degrees : (order + 1) * degrees, :]
        table_ref[order] = values.astype(BF16)
        for turned_ref in refs[1:-1]:
            turned_ref[order] = values.T.astype(BF16)


def legendre(norms, cosine, start, both):
    orders, points = start.shape
    degrees = norms.shape[1]
    block = math.gcd(orders, 32)
    return pl.pallas_call(
        functools.partial(legendre_kernel, degrees=degrees, span=8),
        grid=(orders // block, points // LANES),
        in_specs=[
            pl.BlockSpec(memory_space=pltpu.SMEM),
            pl.BlockSpec((1, LANES), lambda i, j: (0, j)),
            pl.BlockSpec((block, LANES), lambda i, j: (i, j)),
        ],
        out_specs=[
            pl.BlockSpec((block, degrees, LANES), lambda i, j: (i, 0, j)),
            pl.BlockSpec((block, LANES, degrees), lambda i, j: (i, j, 0)),
        ][: 1 + both],
        out_shape=[
            jax.ShapeDtypeStruct((orders, degrees, points), BF16),
            jax.ShapeDtypeStruct((orders, points, degrees), BF16),
        ][: 1 + both],
        scratch_shapes=[pltpu.VMEM((block * degrees, LANES), F32)],
        compiler_params=params(56 * MIB),
        cost_estimate=pl.CostEstimate(
            flops=40 * orders * degrees * points,
            bytes_accessed=4 * orders * degrees * points,
            transcendentals=0,
        ),
        name="legendre",
    )(norms, cosine, start)


def spectral_kernel(
    from_ref, forward_ref, inverse_ref, weight_ref, quad_ref, *refs, group, q_count, unroll
):
    *tables, back_ref, recv_ref, grid_scr, even_scr, odd_scr, north_scr, south_scr, copied = refs
    table_ref = tables[0]
    step = pl.program_id(0)
    bands, sectors = recv_ref.shape[:2]
    local, lats, lons = grid_scr.shape
    orders_here, degrees, half = table_ref.shape
    tiles = half // LANES
    modes = forward_ref.shape[0]
    orders = modes // 2
    band_rows = group * q_count
    width = LANES // group
    lane_group = lax.broadcasted_iota(jnp.int32, (q_count, LANES), 1) // width

    def place(band, r):
        if band < bands // 2:
            return band * band_rows + r * q_count
        return lats // 2 + (bands - 1 - band) * band_rows + r * q_count

    def rolled(value, places):
        shift = places * width % LANES
        return value if shift == 0 else pltpu.roll(value, shift, 1)

    @pl.when(step == 0)
    def _():
        copy = pltpu.make_async_copy(from_ref, recv_ref, copied)
        copy.start()
        copy.wait()
        for chan in range(local):
            at = chan * q_count
            for band in range(bands):
                for unit in range(sectors // group):
                    pieces = [
                        recv_ref[band, unit * group + k, at : at + q_count, :].astype(F32)
                        for k in range(group)
                    ]
                    for r in range(group):
                        value = rolled(pieces[0], -r)
                        for k in range(1, group):
                            value = jnp.where(lane_group == k, rolled(pieces[k], k - r), value)
                        row = place(band, r)
                        grid_scr[chan, row : row + q_count, unit * LANES : (unit + 1) * LANES] = (
                            value.astype(BF16)
                        )
            spectrum = lax.dot_general(
                forward_ref[...], grid_scr[chan], (((1,), (1,)), ((), ())), preferred_element_type=F32
            )
            for tile in range(tiles):
                north = spectrum[:, tile * LANES : (tile + 1) * LANES]
                south = spectrum[:, half + tile * LANES : half + (tile + 1) * LANES]
                even_scr[tile, chan * modes : (chan + 1) * modes, :] = north + south
                odd_scr[tile, chan * modes : (chan + 1) * modes, :] = north - south

    def lines(scr, tile, mode):
        if local == 1:
            return (tile, pl.ds(mode, 1), slice(None))
        return (tile, pl.ds(mode, local, stride=modes), slice(None))

    def load(scr, mode):
        parts = [scr[lines(scr, tile, mode)] for tile in range(tiles)]
        return parts[0] if tiles == 1 else jnp.concatenate(parts, axis=1)

    degree_lane = lax.broadcasted_iota(jnp.int32, (local, degrees), 1)
    real_w = weight_ref[0]
    imag_w = weight_ref[1]
    quad = quad_ref[...]

    def one_order(index):
        order = step * orders_here + index
        table = table_ref[index]
        even = (degree_lane + order) % 2 == 0
        stacked = jnp.concatenate(
            [
                load(even_scr, order),
                load(even_scr, orders + order),
                load(odd_scr, order),
                load(odd_scr, orders + order),
            ],
            axis=0,
        ).astype(BF16)
        if len(tables) == 2:
            analysed = jnp.dot(stacked, tables[1][index], preferred_element_type=F32)
        else:
            analysed = lax.dot_general(
                stacked, table, (((1,), (1,)), ((), ())), preferred_element_type=F32
            )
        real_a = jnp.where(even, analysed[0:local], analysed[2 * local : 3 * local])
        imag_a = jnp.where(even, analysed[local : 2 * local], analysed[3 * local : 4 * local])
        real_m = real_w * real_a + imag_w * imag_a
        imag_m = real_w * imag_a - imag_w * real_a
        mixed = jnp.concatenate(
            [
                jnp.where(even, real_m, 0.0),
                jnp.where(even, imag_m, 0.0),
                jnp.where(even, 0.0, real_m),
                jnp.where(even, 0.0, imag_m),
            ],
            axis=0,
        ).astype(BF16)
        synth = jnp.dot(mixed, table, preferred_element_type=F32) * quad
        for part in range(2):
            even_part = synth[part * local : (part + 1) * local]
            odd_part = synth[(2 + part) * local : (3 + part) * local]
            for tile in range(tiles):
                lanes = slice(tile * LANES, (tile + 1) * LANES)
                where = lines(north_scr, tile, part * orders + order)
                north_scr[where] = even_part[:, lanes] + odd_part[:, lanes]
                south_scr[where] = even_part[:, lanes] - odd_part[:, lanes]

    def several(index, carry):
        for inner in range(unroll):
            one_order(index * unroll + inner)
        return carry

    lax.fori_loop(0, orders_here // unroll, several, 0)

    @pl.when(step == pl.num_programs(0) - 1)
    def _():
        for chan in range(local):
            rows = slice(chan * modes, (chan + 1) * modes)
            profile = jnp.concatenate(
                [scr[tile, rows, :].astype(BF16) for scr in (north_scr, south_scr) for tile in range(tiles)],
                axis=1,
            )
            field = lax.dot_general(
                profile, inverse_ref[...], (((0,), (0,)), ((), ())), preferred_element_type=F32
            )
            at = chan * q_count
            for band in range(bands):
                for unit in range(sectors // group):
                    pieces = []
                    for r in range(group):
                        row = place(band, r)
                        pieces.append(field[row : row + q_count, unit * LANES : (unit + 1) * LANES])
                    for k in range(group):
                        value = rolled(pieces[0], -k)
                        for r in range(1, group):
                            value = jnp.where(lane_group == r, rolled(pieces[r], r - k), value)
                        back_ref[band, unit * group + k, at : at + q_count, :] = value.astype(BF16)


def spectral(received, forward, inverse, tables, weights, quad, group):
    bands, sectors, rows, _ = received.shape
    local = weights.shape[1]
    q_count = rows // local
    orders, degrees, half = tables[0].shape
    lons = forward.shape[1]
    block = max(1, min(orders, 2**19 // (degrees * half)))
    tiles = half // LANES

    def whole(shape):
        return pl.BlockSpec(shape, lambda i: (0,) * len(shape))

    lines = pltpu.VMEM((tiles, local * forward.shape[0], LANES), F32)
    return pl.pallas_call(
        functools.partial(spectral_kernel, group=group, q_count=q_count, unroll=math.gcd(block, 8)),
        grid=(orders // block,),
        in_specs=[
            pl.BlockSpec(memory_space=pl.ANY),
            whole(forward.shape),
            whole(inverse.shape),
            whole(weights.shape),
            whole(quad.shape),
        ]
        + [pl.BlockSpec((block,) + table.shape[1:], lambda i: (i, 0, 0)) for table in tables],
        out_specs=whole(received.shape),
        out_shape=jax.ShapeDtypeStruct(received.shape, BF16),
        scratch_shapes=[
            pltpu.VMEM(received.shape, BF16),
            pltpu.VMEM((local, 2 * half, lons), BF16),
            lines,
            lines,
            lines,
            lines,
            pltpu.SemaphoreType.DMA,
        ],
        compiler_params=params(50 * MIB),
        name="spectral",
    )(received, forward, inverse, weights, quad, *tables)


def disco_kernel(tap_ref, grad_ref, low_ref, high_ref, left_ref, right_ref, mix_ref, out_ref, padded, taps_scr):
    step = pl.program_id(0)
    rows, cols, channels = grad_ref.shape
    rows_here = out_ref.shape[0]
    kernels = mix_ref.shape[0]
    halves = channels // LANES
    origin = 8

    @pl.when(step == 0)
    def _():
        for half in range(halves):
            lanes = slice(half * LANES, (half + 1) * LANES)
            padded[half, REACH : REACH + rows, origin : origin + cols, :] = grad_ref[:, :, lanes].astype(F32)
            padded[half, 0:REACH, origin : origin + cols, :] = low_ref[:, :, lanes].astype(F32)
            padded[half, REACH + rows :, origin : origin + cols, :] = high_ref[:, :, lanes].astype(F32)
            for side in range(REACH):
                padded[half, :, origin - REACH + side, :] = left_ref[side, :, lanes].astype(F32)
                padded[half, :, origin + cols + side, :] = right_ref[side, :, lanes].astype(F32)

    def one_row(row, carry):
        for half in range(halves):
            sums = [jnp.zeros((cols, LANES), F32) for _ in range(kernels)]
            for lat_tap in range(TAPS):
                source = step * rows_here + row + 2 * REACH - lat_tap
                for lon_tap in range(TAPS):
                    start = origin + REACH - lon_tap
                    slab = padded[half, source, start : start + cols, :]
                    for kernel in range(kernels):
                        tap = tap_ref[source, (kernel * TAPS + lat_tap) * TAPS + lon_tap]
                        sums[kernel] = sums[kernel] + tap * slab
            for kernel in range(kernels):
                taps_scr[kernel, row, :, half * LANES : (half + 1) * LANES] = sums[kernel].astype(BF16)
        return carry

    lax.fori_loop(0, rows_here, one_row, 0)
    total = None
    for kernel in range(kernels):
        flat = taps_scr[kernel].reshape(rows_here * cols, channels)
        term = lax.dot_general(
            flat, mix_ref[kernel], (((1,), (1,)), ((), ())), preferred_element_type=F32
        )
        total = term if total is None else total + term
    out_ref[...] = total.reshape(rows_here, cols, channels)


def disco(taps, grad, low, high, left, right, mix):
    rows, cols, channels = grad.shape
    kernels = mix.shape[0]
    steps = 4

    def whole(shape):
        return pl.BlockSpec(shape, lambda i: (0,) * len(shape))

    return pl.pallas_call(
        disco_kernel,
        grid=(steps,),
        in_specs=[pl.BlockSpec(memory_space=pltpu.SMEM)]
        + [whole(value.shape) for value in (grad, low, high, left, right, mix)],
        out_specs=pl.BlockSpec((rows // steps, cols, channels), lambda i: (i, 0, 0)),
        out_shape=jax.ShapeDtypeStruct(grad.shape, F32),
        scratch_shapes=[
            pltpu.VMEM((channels // LANES, rows + 2 * REACH, cols + 16, LANES), F32),
            pltpu.VMEM((kernels, rows // steps, cols, channels), BF16),
        ],
        compiler_params=params(14 * MIB),
        cost_estimate=pl.CostEstimate(
            flops=1000 * rows * cols * channels, bytes_accessed=8 * rows * cols * channels, transcendentals=0
        ),
        name="disco",
    )(taps, grad, low, high, left, right, mix)


def combine_kernel(flip_ref, from_ref, disco_ref, out_ref, back_ref, chan_scr, copied, *, group, q_count):
    step = pl.program_id(0)
    rows, cols, channels = out_ref.shape
    flip = flip_ref[0]

    @pl.when(step == 0)
    def _():
        copy = pltpu.make_async_copy(from_ref, back_ref, copied)
        copy.start()
        copy.wait()
        count = back_ref.shape[1]
        for source in range(back_ref.shape[0]):
            chan_scr[source * count : (source + 1) * count, :] = back_ref[source].astype(F32)

    for block in range(rows // group):
        q_index = step * (rows // group) + block
        q_from = jnp.where(flip == 1, q_count - 1 - q_index, q_index)
        turned = jnp.concatenate(
            [
                chan_scr[pl.ds(tile * LANES * q_count + q_from, LANES, stride=q_count), :].T
                for tile in range(channels // LANES)
            ],
            axis=1,
        )
        for r in range(group):
            row = block * group + jnp.where(flip == 1, group - 1 - r, r)
            out_ref[row] = (disco_ref[row] + turned[r * cols : (r + 1) * cols]).astype(BF16)


def combine(back, local_part, flip, group):
    rows, cols, channels = local_part.shape
    q_count = rows // group
    steps = 4
    spec = pl.BlockSpec((rows // steps, cols, channels), lambda i: (i, 0, 0))
    return pl.pallas_call(
        functools.partial(combine_kernel, group=group, q_count=q_count),
        grid=(steps,),
        in_specs=[pl.BlockSpec(memory_space=pltpu.SMEM), pl.BlockSpec(memory_space=pl.ANY), spec],
        out_specs=spec,
        out_shape=jax.ShapeDtypeStruct(local_part.shape, BF16),
        scratch_shapes=[
            pltpu.VMEM(back.shape, BF16),
            pltpu.VMEM((channels * q_count, LANES), F32),
            pltpu.SemaphoreType.DMA,
        ],
        compiler_params=params(10 * MIB),
        name="combine",
    )(flip, back, local_part)


def neighbours(axis, block_low, block_high):
    count = lax.axis_size(axis)
    forward = [(i, (i + 1) % count) for i in range(count)]
    backward = [(target, source) for source, target in forward]
    return (lax.ppermute(block_low, axis, forward), lax.ppermute(block_high, axis, backward))


def fourier_tables(order_count, points):
    order_list = jnp.arange(order_count, dtype=jnp.int32)[:, None]
    grid_pos = jnp.arange(points, dtype=jnp.int32)[None, :]
    angles = 2.0 * math.pi / points * (grid_pos * order_list % points).astype(F32)
    factor = jnp.where(order_list == 0, 1.0, 2.0).astype(F32)
    inverse = jnp.concatenate([jnp.cos(angles), -jnp.sin(angles)], axis=0)
    forward = jnp.concatenate([factor, factor], axis=0) * inverse
    return (forward.astype(BF16), inverse.astype(BF16))


def shards(pre_act, cotangent, spec_weight, disco_weight, disco_filter, support):
    lat_rows, lon_cols, channels = pre_act.shape
    lat_count = lax.axis_size("lat")
    lon_count = lax.axis_size("lon")
    devices = lat_count * lon_count
    band_index = lax.axis_index("lat")
    device_id = band_index * lon_count + lax.axis_index("lon")
    total_lat = lat_rows * lat_count
    total_lon = lon_cols * lon_count
    mode_count = spec_weight.shape[0]
    local = channels // devices
    group = LANES // lon_cols
    q_count = lat_rows // group
    flip = (2 * band_index >= lat_count).astype(jnp.int32).reshape(1)

    grad_pre, to_send, first_rows, last_rows = gradient(pre_act, cotangent, flip, devices, group)
    received = lax.all_to_all(to_send, ("lat", "lon"), 0, 0, tiled=True)

    lane = np.arange(total_lat // 2)
    lats = lane // lat_rows * lat_rows + lane % q_count * group + lane % lat_rows // q_count
    colatitude = math.pi / total_lat * (jnp.asarray(lats, F32) + 0.5)[None, :]
    order_vals = jnp.arange(mode_count, dtype=F32)[:, None]
    start = (
        0.5 * jnp.log((2.0 * order_vals + 1.0) / (4.0 * math.pi))
        + 0.5
        * (
            lax.lgamma(2.0 * order_vals + 1.0)
            - order_vals * math.log(4.0)
            - 2.0 * lax.lgamma(order_vals + 1.0)
        )
        + order_vals * jnp.log(jnp.sin(colatitude))
    )
    degree_norm = jnp.sqrt(jnp.maximum(4.0 * jnp.square(jnp.arange(mode_count, dtype=F32)) - 1.0, 1.0))
    norms = jnp.stack([degree_norm, 1.0 / degree_norm])
    both = mode_count * mode_count * total_lat < 2**25
    tables = legendre(norms, jnp.cos(colatitude), start, both)
    low, high = neighbours("lat", last_rows, first_rows)
    west = jnp.concatenate([part[:, :REACH] for part in (low, grad_pre, high)], axis=0)
    east = jnp.concatenate([part[:, -REACH:] for part in (low, grad_pre, high)], axis=0)
    left, right = neighbours("lon", jnp.transpose(east, (1, 0, 2)), jnp.transpose(west, (1, 0, 2)))
    forward, inverse = fourier_tables(mode_count, total_lon)
    quad = 2.0 * math.pi / total_lon * (math.pi / total_lat) * jnp.sin(colatitude)
    weights = jnp.transpose(
        lax.dynamic_slice_in_dim(spec_weight, device_id * local, local, 2), (1, 2, 0)
    )
    offsets = jnp.arange(TAPS, dtype=jnp.int32) - REACH
    allowed = (jnp.abs(offsets)[None, None, :] <= support[:, :, None]).astype(F32)
    tap_coef = jnp.pad(disco_filter * allowed[None], ((0, 0), (REACH, REACH), (0, 0), (0, 0)))
    tap_coef = lax.dynamic_slice_in_dim(tap_coef, band_index * lat_rows, lat_rows + 2 * REACH, 1)
    taps = jnp.transpose(tap_coef, (1, 0, 2, 3)).reshape(lat_rows + 2 * REACH, -1)

    received, low, high, left, right = lax.optimization_barrier((received, low, high, left, right))
    blocks = received.reshape(lat_count, lon_count, local * q_count, LANES)
    back = spectral(blocks, forward, inverse, tables, weights, quad, group)
    back, taps = lax.optimization_barrier((back, taps))
    returned = lax.all_to_all(
        back.reshape(devices, local * q_count, LANES), ("lat", "lon"), 0, 0, tiled=True
    )
    local_part = disco(taps, grad_pre, low, high, left, right, disco_weight)
    return combine(returned, local_part, flip, group)


def solution(mesh):
    return jax.shard_map(
        shards,
        mesh=mesh,
        in_specs=(P("lat", "lon", None), P("lat", "lon", None), P(), P(), P(), P()),
        out_specs=P("lat", "lon", None),
        check_vma=False,
    )
```

```python
import functools
import math

import jax
import jax.numpy as jnp
import numpy as np
from jax import lax
from jax.experimental import pallas as pl
from jax.experimental.pallas import tpu as pltpu
from jax.sharding import PartitionSpec as P

REACH = 2
TAPS = 2 * REACH + 1
LANES = 128
PAD = 8
CHUNKS = 4
F32 = jnp.float32
BF16 = jnp.bfloat16
MIB = 1024 * 1024


def params(limit):
    return pltpu.CompilerParams(vmem_limit_bytes=limit)


def gelu_slope(pre_values):
    normal_cdf = 0.5 * (1.0 + lax.erf(pre_values * (1.0 / math.sqrt(2.0))))
    density = jnp.exp(-0.5 * pre_values * pre_values) * (1.0 / math.sqrt(2.0 * math.pi))
    return normal_cdf + pre_values * density


def grad_kernel(
    flip_ref, pre_hbm, cot_hbm, grad_hbm, send_hbm, first_ref, last_ref, west_ref, east_ref,
    pre_ref, cot_ref, grad_ref, send_ref, rows_scr, chan_scr, in_sems, out_sems, *, group, q_count,
):
    rows, cols, channels = pre_ref.shape
    part = rows // CHUNKS
    flip = flip_ref[0]

    def fetch(chunk):
        at = pl.ds(chunk * part, part)
        return [
            pltpu.make_async_copy(pre_hbm.at[at], pre_ref.at[at], in_sems.at[0, chunk]),
            pltpu.make_async_copy(cot_hbm.at[at], cot_ref.at[at], in_sems.at[1, chunk]),
        ]

    def keep(chunk):
        at = pl.ds(chunk * part, part)
        return pltpu.make_async_copy(grad_ref.at[at], grad_hbm.at[at], out_sems.at[0, chunk])

    def send(chunk):
        count = send_ref.shape[0] // CHUNKS
        at = pl.ds(chunk * count, count)
        return pltpu.make_async_copy(send_ref.at[at], send_hbm.at[at], out_sems.at[1, chunk])

    for chunk in range(CHUNKS):
        for copy in fetch(chunk):
            copy.start()
    for chunk in range(CHUNKS):
        for copy in fetch(chunk):
            copy.wait()
        for row in range(chunk * part, (chunk + 1) * part):
            grad = (cot_ref[row].astype(F32) * gelu_slope(pre_ref[row].astype(F32))).astype(BF16)
            grad_ref[row] = grad
            rows_scr[row] = grad.astype(F32)
        keep(chunk).start()
        for q_index in range(chunk * part // group, (chunk + 1) * part // group):
            q_out = jnp.where(flip == 1, q_count - 1 - q_index, q_index)
            slabs = []
            for r in range(group):
                slabs.append(rows_scr[q_index * group + jnp.where(flip == 1, group - 1 - r, r)])
            stacked = jnp.concatenate(slabs, axis=0)
            for tile in range(channels // LANES):
                turned = stacked[:, tile * LANES : (tile + 1) * LANES].T
                chan_scr[pl.ds(tile * LANES * q_count + q_out, LANES, stride=q_count), :] = turned
    dests, count = send_ref.shape[:2]
    for chunk in range(CHUNKS):
        for dest in range(chunk * dests // CHUNKS, (chunk + 1) * dests // CHUNKS):
            send_ref[dest] = chan_scr[dest * count : (dest + 1) * count, :].astype(BF16)
        send(chunk).start()
    for row in range(REACH):
        first_ref[row * cols : (row + 1) * cols, :] = grad_ref[row]
        last_ref[row * cols : (row + 1) * cols, :] = grad_ref[rows - REACH + row]
    for side in range(REACH):
        west_ref[side * rows : (side + 1) * rows, :] = rows_scr[:, side, :].astype(BF16)
        east_ref[side * rows : (side + 1) * rows, :] = rows_scr[:, cols - REACH + side, :].astype(BF16)
    for chunk in range(CHUNKS):
        keep(chunk).wait()
        send(chunk).wait()


def gradient(pre_act, cotangent, flip, devices, group):
    rows, cols, channels = pre_act.shape
    q_count = rows // group
    send = (devices, channels // devices * q_count, LANES)
    edges = [(REACH * cols, channels)] * 2 + [(REACH * rows, channels)] * 2
    anywhere = pl.BlockSpec(memory_space=pl.ANY)
    vmem = pl.BlockSpec(memory_space=pltpu.VMEM)
    return pl.pallas_call(
        functools.partial(grad_kernel, group=group, q_count=q_count),
        in_specs=[pl.BlockSpec(memory_space=pltpu.SMEM), anywhere, anywhere],
        out_specs=[anywhere, anywhere] + [vmem] * 4,
        out_shape=[jax.ShapeDtypeStruct(shape, BF16) for shape in (pre_act.shape, send, *edges)],
        scratch_shapes=[
            pltpu.VMEM(pre_act.shape, BF16),
            pltpu.VMEM(pre_act.shape, BF16),
            pltpu.VMEM(pre_act.shape, BF16),
            pltpu.VMEM(send, BF16),
            pltpu.VMEM(pre_act.shape, F32),
            pltpu.VMEM((channels * q_count, LANES), F32),
            pltpu.SemaphoreType.DMA((2, CHUNKS)),
            pltpu.SemaphoreType.DMA((2, CHUNKS)),
        ],
        compiler_params=params(60 * MIB),
        name="gradient",
    )(flip, pre_act, cotangent)


def legendre_kernel(norm_ref, cos_ref, start_ref, *refs, degrees, span):
    scr = refs[-1]
    pitch = degrees + PAD
    table_ref = refs[0]
    orders = table_ref.shape[0]
    groups = orders // 8
    first = pl.program_id(0) * orders
    cosine = jnp.broadcast_to(cos_ref[...], (8, LANES))
    sub = lax.broadcasted_iota(jnp.int32, (8, LANES), 0)
    order_vals = [(first + 8 * g + sub).astype(F32) for g in range(groups)]
    squares = [order * order for order in order_vals]
    zero = jnp.zeros((8, LANES), F32)

    def chunk(index, state):
        latest, earlier, coef_b, scale = (list(part) for part in state)
        factor = [jnp.exp(value) for value in scale]
        for step in range(span):
            degree = index * span + step
            deg_val = degree.astype(F32)
            norm = norm_ref[0, degree]
            inverse_norm = norm_ref[1, degree]
            for g in range(groups):
                gap = jnp.maximum(deg_val * deg_val - squares[g], 1.0)
                root = lax.rsqrt(gap)
                value = (root * norm) * (cosine * latest[g] - coef_b[g] * earlier[g])
                value = jnp.where(order_vals[g] == deg_val, 1.0, value)
                coef_b[g] = gap * root * inverse_norm
                earlier[g] = latest[g]
                latest[g] = value
                scr[pl.ds(g * 8 * pitch + degree, 8, stride=pitch), :] = value * factor[g]
        for g in range(groups):
            large = jnp.maximum(jnp.abs(latest[g]), jnp.abs(earlier[g])) > 2.0**20
            shrink = jnp.where(large, 2.0**-40, 1.0)
            latest[g] = latest[g] * shrink
            earlier[g] = earlier[g] * shrink
            scale[g] = scale[g] + jnp.where(large, 40.0 * math.log(2.0), 0.0)
        return (tuple(latest), tuple(earlier), tuple(coef_b), tuple(scale))

    starts = tuple(start_ref[8 * g : 8 * g + 8, :] for g in range(groups))
    zeros = (zero,) * groups
    lax.fori_loop(0, degrees // span, chunk, (zeros, zeros, zeros, starts))
    for order in range(orders):
        values = scr[order * pitch : order * pitch + degrees, :]
        table_ref[order] = values.astype(BF16)
        for turned_ref in refs[1:-1]:
            turned_ref[order] = values.T.astype(BF16)


def legendre(norms, cosine, start, both):
    orders, points = start.shape
    degrees = norms.shape[1]
    block = math.gcd(orders, 32)
    return pl.pallas_call(
        functools.partial(legendre_kernel, degrees=degrees, span=8),
        grid=(orders // block, points // LANES),
        in_specs=[
            pl.BlockSpec(memory_space=pltpu.SMEM),
            pl.BlockSpec((1, LANES), lambda i, j: (0, j)),
            pl.BlockSpec((block, LANES), lambda i, j: (i, j)),
        ],
        out_specs=[
            pl.BlockSpec((block, degrees, LANES), lambda i, j: (i, 0, j)),
            pl.BlockSpec((block, LANES, degrees), lambda i, j: (i, j, 0)),
        ][: 1 + both],
        out_shape=[
            jax.ShapeDtypeStruct((orders, degrees, points), BF16),
            jax.ShapeDtypeStruct((orders, points, degrees), BF16),
        ][: 1 + both],
        scratch_shapes=[pltpu.VMEM((block * (degrees + PAD), LANES), F32)],
        compiler_params=params(56 * MIB),
        cost_estimate=pl.CostEstimate(
            flops=40 * orders * degrees * points,
            bytes_accessed=4 * orders * degrees * points,
            transcendentals=0,
        ),
        name="legendre",
    )(norms, cosine, start)


def spectral_kernel(
    recv_hbm, forward_ref, inverse_ref, weight_ref, quad_ref, *refs, group, q_count, unroll, count
):
    tables = refs[:count]
    back_hbm, recv_ref, back_ref, grid_scr, even_scr, odd_scr, north_scr, south_scr = refs[count : count + 8]
    slots = refs[count + 8 : 2 * count + 8]
    recv_sem, table_sems, back_sems = refs[2 * count + 8 :]
    bands, sectors = recv_ref.shape[:2]
    local, lats, lons = grid_scr.shape
    slot_count, orders_here, degrees, half = slots[0].shape
    tiles = half // LANES
    modes = forward_ref.shape[0]
    orders = modes // 2
    blocks = orders // orders_here
    pitch = modes + PAD
    band_rows = group * q_count
    width = LANES // group
    lane_group = lax.broadcasted_iota(jnp.int32, (q_count, LANES), 1) // width

    def fetch(block, slot):
        at = pl.ds(block * orders_here, orders_here)
        return [
            pltpu.make_async_copy(table.at[at], ring.at[slot], table_sems.at[kind, slot])
            for kind, (table, ring) in enumerate(zip(tables, slots))
        ]

    def give(chan):
        at = pl.ds(chan * q_count, q_count)
        return pltpu.make_async_copy(back_ref.at[:, :, at], back_hbm.at[:, :, at], back_sems.at[chan])

    def place(band, r):
        if band < bands // 2:
            return band * band_rows + r * q_count
        return lats // 2 + (bands - 1 - band) * band_rows + r * q_count

    def rolled(value, places):
        shift = places * width % LANES
        return value if shift == 0 else pltpu.roll(value, shift, 1)

    receive = pltpu.make_async_copy(recv_hbm, recv_ref, recv_sem)
    receive.start()
    for block in range(slot_count):
        for copy in fetch(block, block):
            copy.start()
    receive.wait()

    for chan in range(local):
        at = chan * q_count
        for band in range(bands):
            for unit in range(sectors // group):
                pieces = [
                    recv_ref[band, unit * group + k, at : at + q_count, :].astype(F32) for k in range(group)
                ]
                for r in range(group):
                    value = rolled(pieces[0], -r)
                    for k in range(1, group):
                        value = jnp.where(lane_group == k, rolled(pieces[k], k - r), value)
                    row = place(band, r)
                    grid_scr[chan, row : row + q_count, unit * LANES : (unit + 1) * LANES] = value.astype(BF16)
        spectrum = lax.dot_general(
            forward_ref[...], grid_scr[chan], (((1,), (1,)), ((), ())), preferred_element_type=F32
        )
        for tile in range(tiles):
            north = spectrum[:, tile * LANES : (tile + 1) * LANES]
            south = spectrum[:, half + tile * LANES : half + (tile + 1) * LANES]
            even_scr[tile, chan * pitch : chan * pitch + modes, :] = north + south
            odd_scr[tile, chan * pitch : chan * pitch + modes, :] = north - south

    def lines(tile, mode):
        if local == 1:
            return (tile, pl.ds(mode, 1), slice(None))
        return (tile, pl.ds(mode, local, stride=pitch), slice(None))

    def load(scr, mode):
        parts = [scr[lines(tile, mode)] for tile in range(tiles)]
        return parts[0] if tiles == 1 else jnp.concatenate(parts, axis=1)

    degree_lane = lax.broadcasted_iota(jnp.int32, (local, degrees), 1)
    real_w = weight_ref[0]
    imag_w = weight_ref[1]
    quad = quad_ref[...]

    def one_order(slot, order, index):
        table = slots[0][slot, index]
        even = (degree_lane + order) % 2 == 0
        stacked = jnp.concatenate(
            [
                load(even_scr, order),
                load(even_scr, orders + order),
                load(odd_scr, order),
                load(odd_scr, orders + order),
            ],
            axis=0,
        ).astype(BF16)
        if count == 2:
            analysed = jnp.dot(stacked, slots[1][slot, index], preferred_element_type=F32)
        else:
            analysed = lax.dot_general(
                stacked, table, (((1,), (1,)), ((), ())), preferred_element_type=F32
            )
        real_a = jnp.where(even, analysed[0:local], analysed[2 * local : 3 * local])
        imag_a = jnp.where(even, analysed[local : 2 * local], analysed[3 * local : 4 * local])
        real_m = real_w * real_a + imag_w * imag_a
        imag_m = real_w * imag_a - imag_w * real_a
        mixed = jnp.concatenate(
            [
                jnp.where(even, real_m, 0.0),
                jnp.where(even, imag_m, 0.0),
                jnp.where(even, 0.0, real_m),
                jnp.where(even, 0.0, imag_m),
            ],
            axis=0,
        ).astype(BF16)
        synth = jnp.dot(mixed, table, preferred_element_type=F32) * quad
        for part in range(2):
            even_part = synth[part * local : (part + 1) * local]
            odd_part = synth[(2 + part) * local : (3 + part) * local]
            for tile in range(tiles):
                lanes = slice(tile * LANES, (tile + 1) * LANES)
                where = lines(tile, part * orders + order)
                north_scr[where] = even_part[:, lanes] + odd_part[:, lanes]
                south_scr[where] = even_part[:, lanes] - odd_part[:, lanes]

    def one_block(block, carry):
        slot = block % slot_count
        for copy in fetch(block, slot):
            copy.wait()

        def several(index, inner_carry):
            for inner in range(unroll):
                at = index * unroll + inner
                one_order(slot, block * orders_here + at, at)
            return inner_carry

        lax.fori_loop(0, orders_here // unroll, several, 0)

        @pl.when(block + slot_count < blocks)
        def _():
            for copy in fetch(block + slot_count, slot):
                copy.start()

        return carry

    lax.fori_loop(0, blocks, one_block, 0)

    for chan in range(local):
        rows = slice(chan * pitch, chan * pitch + modes)
        profile = jnp.concatenate(
            [scr[tile, rows, :].astype(BF16) for scr in (north_scr, south_scr) for tile in range(tiles)],
            axis=1,
        )
        field = lax.dot_general(
            profile, inverse_ref[...], (((0,), (0,)), ((), ())), preferred_element_type=F32
        )
        at = chan * q_count
        for band in range(bands):
            for unit in range(sectors // group):
                pieces = []
                for r in range(group):
                    row = place(band, r)
                    pieces.append(field[row : row + q_count, unit * LANES : (unit + 1) * LANES])
                for k in range(group):
                    value = rolled(pieces[0], -k)
                    for r in range(1, group):
                        value = jnp.where(lane_group == r, rolled(pieces[r], r - k), value)
                    back_ref[band, unit * group + k, at : at + q_count, :] = value.astype(BF16)
        give(chan).start()
    for chan in range(local):
        give(chan).wait()


def spectral(received, forward, inverse, tables, weights, quad, group):
    bands, sectors, rows, _ = received.shape
    local = weights.shape[1]
    q_count = rows // local
    orders, degrees, half = tables[0].shape
    lons = forward.shape[1]
    count = len(tables)
    block = max(1, min(orders, 2**19 // (degrees * half)))
    ring = min(orders // block, 4)
    tiles = half // LANES
    anywhere = pl.BlockSpec(memory_space=pl.ANY)
    vmem = pl.BlockSpec(memory_space=pltpu.VMEM)
    lines = pltpu.VMEM((tiles, local * (forward.shape[0] + PAD), LANES), F32)
    return pl.pallas_call(
        functools.partial(
            spectral_kernel, group=group, q_count=q_count, unroll=math.gcd(block, 16), count=count
        ),
        in_specs=[anywhere] + [vmem] * 4 + [anywhere] * count,
        out_specs=anywhere,
        out_shape=jax.ShapeDtypeStruct(received.shape, BF16),
        scratch_shapes=[
            pltpu.VMEM(received.shape, BF16),
            pltpu.VMEM(received.shape, BF16),
            pltpu.VMEM((local, 2 * half, lons), BF16),
            lines,
            lines,
            lines,
            lines,
        ]
        + [pltpu.VMEM((ring, block) + table.shape[1:], BF16) for table in tables]
        + [
            pltpu.SemaphoreType.DMA,
            pltpu.SemaphoreType.DMA((count, ring)),
            pltpu.SemaphoreType.DMA((local,)),
        ],
        compiler_params=params(50 * MIB),
        name="spectral",
    )(received, forward, inverse, weights, quad, *tables)


def disco_kernel(
    tap_ref, grad_ref, low_ref, high_ref, left_ref, right_ref, corner_ref, mix_ref, out_ref, padded, taps_scr
):
    step = pl.program_id(0)
    rows, cols, channels = grad_ref.shape
    rows_here = out_ref.shape[0]
    kernels = mix_ref.shape[0]
    halves = channels // LANES
    origin = 8

    @pl.when(step == 0)
    def _():
        for half in range(halves):
            lanes = slice(half * LANES, (half + 1) * LANES)
            padded[half, REACH : REACH + rows, origin : origin + cols, :] = grad_ref[:, :, lanes].astype(F32)
            corners = corner_ref[:, lanes].astype(F32)
            for edge, (source, base) in enumerate(((low_ref, 0), (high_ref, REACH + rows))):
                values = source[:, lanes].astype(F32)
                for row in range(REACH):
                    padded[half, base + row, origin : origin + cols, :] = values[row * cols : (row + 1) * cols]
                    for side in range(REACH):
                        for end, column in enumerate((origin - REACH, origin + cols)):
                            at = ((edge * 2 + end) * REACH + side) * REACH + row
                            column = column + side
                            padded[half, base + row, column : column + 1, :] = corners[at : at + 1]
            for source, column in ((left_ref, origin - REACH), (right_ref, origin + cols)):
                values = source[:, lanes].astype(F32)
                for side in range(REACH):
                    padded[half, REACH : REACH + rows, column + side, :] = values[side * rows : (side + 1) * rows]

    def one_row(row, carry):
        for half in range(halves):
            sums = [jnp.zeros((cols, LANES), F32) for _ in range(kernels)]
            for lat_tap in range(TAPS):
                source = step * rows_here + row + 2 * REACH - lat_tap
                for lon_tap in range(TAPS):
                    start = origin + REACH - lon_tap
                    slab = padded[half, source, start : start + cols, :]
                    for kernel in range(kernels):
                        tap = tap_ref[source, (kernel * TAPS + lat_tap) * TAPS + lon_tap]
                        sums[kernel] = sums[kernel] + tap * slab
            for kernel in range(kernels):
                taps_scr[kernel, row, :, half * LANES : (half + 1) * LANES] = sums[kernel].astype(BF16)
        return carry

    lax.fori_loop(0, rows_here, one_row, 0)
    total = None
    for kernel in range(kernels):
        flat = taps_scr[kernel].reshape(rows_here * cols, channels)
        term = lax.dot_general(
            flat, mix_ref[kernel], (((1,), (1,)), ((), ())), preferred_element_type=F32
        )
        total = term if total is None else total + term
    out_ref[...] = total.reshape(rows_here, cols, channels)


def disco(taps, grad, low, high, left, right, corners, mix):
    rows, cols, channels = grad.shape
    kernels = mix.shape[0]
    steps = 4

    def whole(shape):
        return pl.BlockSpec(shape, lambda i: (0,) * len(shape))

    return pl.pallas_call(
        disco_kernel,
        grid=(steps,),
        in_specs=[pl.BlockSpec(memory_space=pltpu.SMEM)]
        + [whole(value.shape) for value in (grad, low, high, left, right, corners, mix)],
        out_specs=pl.BlockSpec((rows // steps, cols, channels), lambda i: (i, 0, 0)),
        out_shape=jax.ShapeDtypeStruct(grad.shape, F32),
        scratch_shapes=[
            pltpu.VMEM((channels // LANES, rows + 2 * REACH, cols + 16, LANES), F32),
            pltpu.VMEM((kernels, rows // steps, cols, channels), BF16),
        ],
        compiler_params=params(14 * MIB),
        cost_estimate=pl.CostEstimate(
            flops=1000 * rows * cols * channels, bytes_accessed=8 * rows * cols * channels, transcendentals=0
        ),
        name="disco",
    )(taps, grad, low, high, left, right, corners, mix)


def combine_kernel(
    flip_ref, back_hbm, disco_ref, out_hbm, back_ref, chan_scr, out_ref, in_sems, out_sems, *, group, q_count
):
    rows, cols, channels = disco_ref.shape
    sources, count = back_ref.shape[:2]
    part = rows // CHUNKS
    flip = flip_ref[0]

    def fetch(chunk):
        at = pl.ds(chunk * (sources // CHUNKS), sources // CHUNKS)
        return pltpu.make_async_copy(back_hbm.at[at], back_ref.at[at], in_sems.at[chunk])

    def give(chunk):
        at = pl.ds(chunk * part, part)
        return pltpu.make_async_copy(out_ref.at[at], out_hbm.at[at], out_sems.at[chunk])

    for chunk in range(CHUNKS):
        fetch(chunk).start()
    for chunk in range(CHUNKS):
        fetch(chunk).wait()
        for source in range(chunk * sources // CHUNKS, (chunk + 1) * sources // CHUNKS):
            chan_scr[source * count : (source + 1) * count, :] = back_ref[source].astype(F32)
    for chunk in range(CHUNKS):
        for q_index in range(chunk * part // group, (chunk + 1) * part // group):
            q_from = jnp.where(flip == 1, q_count - 1 - q_index, q_index)
            turned = jnp.concatenate(
                [
                    chan_scr[pl.ds(tile * LANES * q_count + q_from, LANES, stride=q_count), :].T
                    for tile in range(channels // LANES)
                ],
                axis=1,
            )
            for r in range(group):
                row = q_index * group + jnp.where(flip == 1, group - 1 - r, r)
                out_ref[row] = (disco_ref[row] + turned[r * cols : (r + 1) * cols]).astype(BF16)
        give(chunk).start()
    for chunk in range(CHUNKS):
        give(chunk).wait()


def combine(back, local_part, flip, group):
    rows, cols, channels = local_part.shape
    q_count = rows // group
    anywhere = pl.BlockSpec(memory_space=pl.ANY)
    return pl.pallas_call(
        functools.partial(combine_kernel, group=group, q_count=q_count),
        in_specs=[
            pl.BlockSpec(memory_space=pltpu.SMEM),
            anywhere,
            pl.BlockSpec(memory_space=pltpu.VMEM),
        ],
        out_specs=anywhere,
        out_shape=jax.ShapeDtypeStruct(local_part.shape, BF16),
        scratch_shapes=[
            pltpu.VMEM(back.shape, BF16),
            pltpu.VMEM((channels * q_count, LANES), F32),
            pltpu.VMEM(local_part.shape, BF16),
            pltpu.SemaphoreType.DMA((CHUNKS,)),
            pltpu.SemaphoreType.DMA((CHUNKS,)),
        ],
        compiler_params=params(12 * MIB),
        name="combine",
    )(flip, back, local_part)


def shifted(block, lat_step, lon_step):
    lat_count = lax.axis_size("lat")
    lon_count = lax.axis_size("lon")
    pairs = [
        (
            lat * lon_count + lon,
            (lat + lat_step) % lat_count * lon_count + (lon + lon_step) % lon_count,
        )
        for lat in range(lat_count)
        for lon in range(lon_count)
    ]
    return lax.ppermute(block, ("lat", "lon"), pairs)


def halos(first_rows, last_rows, west, east):
    channels = west.shape[-1]

    def corner(side, start):
        block = side.reshape(REACH, -1, channels)[:, start:][:, :REACH]
        return block.reshape(REACH * REACH, channels)

    low = shifted(last_rows, 1, 0)
    high = shifted(first_rows, -1, 0)
    left = shifted(east, 0, 1)
    right = shifted(west, 0, -1)
    corners = [
        shifted(corner(east, -REACH), 1, 1),
        shifted(corner(west, -REACH), 1, -1),
        shifted(corner(east, 0), -1, 1),
        shifted(corner(west, 0), -1, -1),
    ]
    return (low, high, left, right, jnp.concatenate(corners, axis=0))


def fourier_tables(order_count, points):
    order_list = jnp.arange(order_count, dtype=jnp.int32)[:, None]
    grid_pos = jnp.arange(points, dtype=jnp.int32)[None, :]
    angles = 2.0 * math.pi / points * (grid_pos * order_list % points).astype(F32)
    factor = jnp.where(order_list == 0, 1.0, 2.0).astype(F32)
    inverse = jnp.concatenate([jnp.cos(angles), -jnp.sin(angles)], axis=0)
    forward = jnp.concatenate([factor, factor], axis=0) * inverse
    return (forward.astype(BF16), inverse.astype(BF16))


def shards(pre_act, cotangent, spec_weight, disco_weight, disco_filter, support):
    lat_rows, lon_cols, channels = pre_act.shape
    lat_count = lax.axis_size("lat")
    lon_count = lax.axis_size("lon")
    devices = lat_count * lon_count
    band_index = lax.axis_index("lat")
    device_id = band_index * lon_count + lax.axis_index("lon")
    total_lat = lat_rows * lat_count
    total_lon = lon_cols * lon_count
    mode_count = spec_weight.shape[0]
    local = channels // devices
    group = LANES // lon_cols
    q_count = lat_rows // group
    flip = (2 * band_index >= lat_count).astype(jnp.int32).reshape(1)

    grad_pre, to_send, *edges = gradient(pre_act, cotangent, flip, devices, group)
    received = lax.all_to_all(to_send, ("lat", "lon"), 0, 0, tiled=True)

    lane = np.arange(total_lat // 2)
    lats = lane // lat_rows * lat_rows + lane % q_count * group + lane % lat_rows // q_count
    colatitude = math.pi / total_lat * (jnp.asarray(lats, F32) + 0.5)[None, :]
    order_vals = jnp.arange(mode_count, dtype=F32)[:, None]
    start = (
        0.5 * jnp.log((2.0 * order_vals + 1.0) / (4.0 * math.pi))
        + 0.5
        * (
            lax.lgamma(2.0 * order_vals + 1.0)
            - order_vals * math.log(4.0)
            - 2.0 * lax.lgamma(order_vals + 1.0)
        )
        + order_vals * jnp.log(jnp.sin(colatitude))
    )
    degree_norm = jnp.sqrt(jnp.maximum(4.0 * jnp.square(jnp.arange(mode_count, dtype=F32)) - 1.0, 1.0))
    norms = jnp.stack([degree_norm, 1.0 / degree_norm])
    both = mode_count * mode_count * total_lat < 2**25
    tables = legendre(norms, jnp.cos(colatitude), start, both)
    forward, inverse = fourier_tables(mode_count, total_lon)
    quad = 2.0 * math.pi / total_lon * (math.pi / total_lat) * jnp.sin(colatitude)
    weights = jnp.transpose(
        lax.dynamic_slice_in_dim(spec_weight, device_id * local, local, 2), (1, 2, 0)
    )
    offsets = jnp.arange(TAPS, dtype=jnp.int32) - REACH
    allowed = (jnp.abs(offsets)[None, None, :] <= support[:, :, None]).astype(F32)
    tap_coef = jnp.pad(disco_filter * allowed[None], ((0, 0), (REACH, REACH), (0, 0), (0, 0)))
    tap_coef = lax.dynamic_slice_in_dim(tap_coef, band_index * lat_rows, lat_rows + 2 * REACH, 1)
    taps = jnp.transpose(tap_coef, (1, 0, 2, 3)).reshape(lat_rows + 2 * REACH, -1)

    received, rim = lax.optimization_barrier((received, halos(*edges)))
    blocks = received.reshape(lat_count, lon_count, local * q_count, LANES)
    back = spectral(blocks, forward, inverse, tables, weights, quad, group)
    back, taps = lax.optimization_barrier((back, taps))
    returned = lax.all_to_all(
        back.reshape(devices, local * q_count, LANES), ("lat", "lon"), 0, 0, tiled=True
    )
    local_part = disco(taps, grad_pre, *rim, disco_weight)
    return combine(returned, local_part, flip, group)


def solution(mesh):
    return jax.shard_map(
        shards,
        mesh=mesh,
        in_specs=(P("lat", "lon", None), P("lat", "lon", None), P(), P(), P(), P()),
        out_specs=P("lat", "lon", None),
        check_vma=False,
    )
```

```python
import functools
import math

import jax
import jax.numpy as jnp
import numpy as np
from jax import lax
from jax.experimental import pallas as pl
from jax.experimental.pallas import tpu as pltpu
from jax.sharding import PartitionSpec as P

REACH = 2
TAPS = 2 * REACH + 1
LANES = 128
PAD = 8
CHUNKS = 4
F32 = jnp.float32
BF16 = jnp.bfloat16
MIB = 1024 * 1024


def params(limit):
    return pltpu.CompilerParams(vmem_limit_bytes=limit)


def gelu_slope(pre_values):
    normal_cdf = 0.5 * (1.0 + lax.erf(pre_values * (1.0 / math.sqrt(2.0))))
    density = jnp.exp(-0.5 * pre_values * pre_values) * (1.0 / math.sqrt(2.0 * math.pi))
    return normal_cdf + pre_values * density


def grad_kernel(
    flip_ref, pre_hbm, cot_hbm, grad_hbm, send_hbm, first_ref, last_ref, west_ref, east_ref,
    pre_ref, cot_ref, grad_ref, send_ref, rows_scr, chan_scr, in_sems, out_sems, *, group, q_count,
):
    rows, cols, channels = pre_ref.shape
    part = rows // CHUNKS
    flip = flip_ref[0]

    def fetch(chunk):
        at = pl.ds(chunk * part, part)
        return [
            pltpu.make_async_copy(pre_hbm.at[at], pre_ref.at[at], in_sems.at[0, chunk]),
            pltpu.make_async_copy(cot_hbm.at[at], cot_ref.at[at], in_sems.at[1, chunk]),
        ]

    def keep(chunk):
        at = pl.ds(chunk * part, part)
        return pltpu.make_async_copy(grad_ref.at[at], grad_hbm.at[at], out_sems.at[0, chunk])

    def send(chunk):
        count = send_ref.shape[0] // CHUNKS
        at = pl.ds(chunk * count, count)
        return pltpu.make_async_copy(send_ref.at[at], send_hbm.at[at], out_sems.at[1, chunk])

    for chunk in range(CHUNKS):
        for copy in fetch(chunk):
            copy.start()
    def one_block(q_index, carry):
        base = q_index * group
        for row in range(group):
            at = base + row
            grad = (cot_ref[at].astype(F32) * gelu_slope(pre_ref[at].astype(F32))).astype(BF16)
            grad_ref[at] = grad
            rows_scr[at] = grad.astype(F32)
        q_out = jnp.where(flip == 1, q_count - 1 - q_index, q_index)
        slabs = []
        for r in range(group):
            slabs.append(rows_scr[base + jnp.where(flip == 1, group - 1 - r, r)])
        stacked = jnp.concatenate(slabs, axis=0)
        for tile in range(channels // LANES):
            turned = stacked[:, tile * LANES : (tile + 1) * LANES].T
            chan_scr[pl.ds(tile * LANES * q_count + q_out, LANES, stride=q_count), :] = turned
        return carry

    for chunk in range(CHUNKS):
        for copy in fetch(chunk):
            copy.wait()
        lax.fori_loop(chunk * part // group, (chunk + 1) * part // group, one_block, 0)
        keep(chunk).start()
    dests, count = send_ref.shape[:2]

    def one_dest(dest, carry):
        at = pl.ds(pl.multiple_of(dest * count, 16), count)
        send_ref[dest] = chan_scr[at, :].astype(BF16)
        return carry

    for chunk in range(CHUNKS):
        lax.fori_loop(chunk * dests // CHUNKS, (chunk + 1) * dests // CHUNKS, one_dest, 0)
        send(chunk).start()
    for row in range(REACH):
        first_ref[row * cols : (row + 1) * cols, :] = grad_ref[row]
        last_ref[row * cols : (row + 1) * cols, :] = grad_ref[rows - REACH + row]
    for side in range(REACH):
        west_ref[side * rows : (side + 1) * rows, :] = rows_scr[:, side, :].astype(BF16)
        east_ref[side * rows : (side + 1) * rows, :] = rows_scr[:, cols - REACH + side, :].astype(BF16)
    for chunk in range(CHUNKS):
        keep(chunk).wait()
        send(chunk).wait()


def gradient(pre_act, cotangent, flip, devices, group):
    rows, cols, channels = pre_act.shape
    q_count = rows // group
    send = (devices, channels // devices * q_count, LANES)
    edges = [(REACH * cols, channels)] * 2 + [(REACH * rows, channels)] * 2
    anywhere = pl.BlockSpec(memory_space=pl.ANY)
    vmem = pl.BlockSpec(memory_space=pltpu.VMEM)
    return pl.pallas_call(
        functools.partial(grad_kernel, group=group, q_count=q_count),
        in_specs=[pl.BlockSpec(memory_space=pltpu.SMEM), anywhere, anywhere],
        out_specs=[anywhere, anywhere] + [vmem] * 4,
        out_shape=[jax.ShapeDtypeStruct(shape, BF16) for shape in (pre_act.shape, send, *edges)],
        scratch_shapes=[
            pltpu.VMEM(pre_act.shape, BF16),
            pltpu.VMEM(pre_act.shape, BF16),
            pltpu.VMEM(pre_act.shape, BF16),
            pltpu.VMEM(send, BF16),
            pltpu.VMEM(pre_act.shape, F32),
            pltpu.VMEM((channels * q_count, LANES), F32),
            pltpu.SemaphoreType.DMA((2, CHUNKS)),
            pltpu.SemaphoreType.DMA((2, CHUNKS)),
        ],
        compiler_params=params(60 * MIB),
        name="gradient",
    )(flip, pre_act, cotangent)


def legendre_kernel(norm_ref, cos_ref, start_ref, *refs, degrees, span):
    scr = refs[-1]
    pitch = degrees + PAD
    table_ref = refs[0]
    orders = table_ref.shape[0]
    groups = orders // 8
    first = pl.program_id(0) * orders
    cosine = jnp.broadcast_to(cos_ref[...], (8, LANES))
    sub = lax.broadcasted_iota(jnp.int32, (8, LANES), 0)
    order_vals = [(first + 8 * g + sub).astype(F32) for g in range(groups)]
    squares = [order * order for order in order_vals]
    zero = jnp.zeros((8, LANES), F32)

    def chunk(index, state):
        latest, earlier, coef_b, scale = (list(part) for part in state)
        factor = [jnp.exp(value) for value in scale]
        for step in range(span):
            degree = index * span + step
            deg_val = degree.astype(F32)
            norm = norm_ref[0, degree]
            inverse_norm = norm_ref[1, degree]
            for g in range(groups):
                gap = jnp.maximum(deg_val * deg_val - squares[g], 1.0)
                root = lax.rsqrt(gap)
                value = (root * norm) * (cosine * latest[g] - coef_b[g] * earlier[g])
                value = jnp.where(order_vals[g] == deg_val, 1.0, value)
                coef_b[g] = gap * root * inverse_norm
                earlier[g] = latest[g]
                latest[g] = value
                scr[pl.ds(g * 8 * pitch + degree, 8, stride=pitch), :] = value * factor[g]
        for g in range(groups):
            large = jnp.maximum(jnp.abs(latest[g]), jnp.abs(earlier[g])) > 2.0**20
            shrink = jnp.where(large, 2.0**-40, 1.0)
            latest[g] = latest[g] * shrink
            earlier[g] = earlier[g] * shrink
            scale[g] = scale[g] + jnp.where(large, 40.0 * math.log(2.0), 0.0)
        return (tuple(latest), tuple(earlier), tuple(coef_b), tuple(scale))

    starts = tuple(start_ref[8 * g : 8 * g + 8, :] for g in range(groups))
    zeros = (zero,) * groups
    lax.fori_loop(0, degrees // span, chunk, (zeros, zeros, zeros, starts))
    for order in range(orders):
        values = scr[order * pitch : order * pitch + degrees, :]
        table_ref[order] = values.astype(BF16)
        for turned_ref in refs[1:-1]:
            turned_ref[order] = values.T.astype(BF16)


def legendre(norms, cosine, start, both):
    orders, points = start.shape
    degrees = norms.shape[1]
    block = math.gcd(orders, 32)
    return pl.pallas_call(
        functools.partial(legendre_kernel, degrees=degrees, span=8),
        grid=(orders // block, points // LANES),
        in_specs=[
            pl.BlockSpec(memory_space=pltpu.SMEM),
            pl.BlockSpec((1, LANES), lambda i, j: (0, j)),
            pl.BlockSpec((block, LANES), lambda i, j: (i, j)),
        ],
        out_specs=[
            pl.BlockSpec((block, degrees, LANES), lambda i, j: (i, 0, j)),
            pl.BlockSpec((block, LANES, degrees), lambda i, j: (i, j, 0)),
        ][: 1 + both],
        out_shape=[
            jax.ShapeDtypeStruct((orders, degrees, points), BF16),
            jax.ShapeDtypeStruct((orders, points, degrees), BF16),
        ][: 1 + both],
        scratch_shapes=[pltpu.VMEM((block * (degrees + PAD), LANES), F32)],
        compiler_params=params(56 * MIB),
        cost_estimate=pl.CostEstimate(
            flops=4000 * orders * degrees * points,
            bytes_accessed=4 * orders * degrees * points,
            transcendentals=0,
        ),
        name="legendre",
    )(norms, cosine, start)


def spectral_kernel(
    recv_hbm, forward_ref, inverse_ref, weight_ref, quad_ref, *refs, group, q_count, unroll, count
):
    tables = refs[:count]
    back_hbm, recv_ref, back_ref, grid_scr, even_scr, odd_scr, north_scr, south_scr = refs[count : count + 8]
    slots = refs[count + 8 : 2 * count + 8]
    recv_sem, table_sems, back_sems = refs[2 * count + 8 :]
    bands, sectors = recv_ref.shape[:2]
    local, lats, lons = grid_scr.shape
    slot_count, orders_here, degrees, half = slots[0].shape
    tiles = half // LANES
    modes = forward_ref.shape[0]
    orders = modes // 2
    blocks = orders // orders_here
    pitch = modes + PAD
    band_rows = group * q_count
    width = LANES // group
    lane_group = lax.broadcasted_iota(jnp.int32, (q_count, LANES), 1) // width

    def fetch(block, slot):
        at = pl.ds(block * orders_here, orders_here)
        return [
            pltpu.make_async_copy(table.at[at], ring.at[slot], table_sems.at[kind, slot])
            for kind, (table, ring) in enumerate(zip(tables, slots))
        ]

    def give(chan):
        at = pl.ds(pl.multiple_of(chan * q_count, 16), q_count)
        return pltpu.make_async_copy(back_ref.at[:, :, at], back_hbm.at[:, :, at], back_sems.at[chan])

    def place(band, r):
        if band < bands // 2:
            return band * band_rows + r * q_count
        return lats // 2 + (bands - 1 - band) * band_rows + r * q_count

    def rolled(value, places):
        shift = places * width % LANES
        return value if shift == 0 else pltpu.roll(value, shift, 1)

    receive = pltpu.make_async_copy(recv_hbm, recv_ref, recv_sem)
    receive.start()
    for block in range(slot_count):
        for copy in fetch(block, block):
            copy.start()
    receive.wait()

    def analyse(chan, carry):
        at = pl.ds(pl.multiple_of(chan * q_count, 16), q_count)
        for band in range(bands):
            for unit in range(sectors // group):
                pieces = [recv_ref[band, unit * group + k, at, :].astype(F32) for k in range(group)]
                for r in range(group):
                    value = rolled(pieces[0], -r)
                    for k in range(1, group):
                        value = jnp.where(lane_group == k, rolled(pieces[k], k - r), value)
                    row = place(band, r)
                    grid_scr[chan, row : row + q_count, unit * LANES : (unit + 1) * LANES] = value.astype(BF16)
        spectrum = lax.dot_general(
            forward_ref[...], grid_scr[chan], (((1,), (1,)), ((), ())), preferred_element_type=F32
        )
        rows = pl.ds(pl.multiple_of(chan * pitch, 8), modes)
        for tile in range(tiles):
            north = spectrum[:, tile * LANES : (tile + 1) * LANES]
            south = spectrum[:, half + tile * LANES : half + (tile + 1) * LANES]
            even_scr[tile, rows, :] = north + south
            odd_scr[tile, rows, :] = north - south
        return carry

    lax.fori_loop(0, local, analyse, 0)

    def lines(tile, mode):
        if local == 1:
            return (tile, pl.ds(mode, 1), slice(None))
        return (tile, pl.ds(mode, local, stride=pitch), slice(None))

    def load(scr, mode):
        parts = [scr[lines(tile, mode)] for tile in range(tiles)]
        return parts[0] if tiles == 1 else jnp.concatenate(parts, axis=1)

    degree_lane = lax.broadcasted_iota(jnp.int32, (local, degrees), 1)
    real_w = weight_ref[0]
    imag_w = weight_ref[1]
    quad = quad_ref[...]

    def one_order(slot, order, index):
        table = slots[0][slot, index]
        even = (degree_lane + order) % 2 == 0
        stacked = jnp.concatenate(
            [
                load(even_scr, order),
                load(even_scr, orders + order),
                load(odd_scr, order),
                load(odd_scr, orders + order),
            ],
            axis=0,
        ).astype(BF16)
        if count == 2:
            analysed = jnp.dot(stacked, slots[1][slot, index], preferred_element_type=F32)
        else:
            analysed = lax.dot_general(
                stacked, table, (((1,), (1,)), ((), ())), preferred_element_type=F32
            )
        real_a = jnp.where(even, analysed[0:local], analysed[2 * local : 3 * local])
        imag_a = jnp.where(even, analysed[local : 2 * local], analysed[3 * local : 4 * local])
        real_m = real_w * real_a + imag_w * imag_a
        imag_m = real_w * imag_a - imag_w * real_a
        mixed = jnp.concatenate(
            [
                jnp.where(even, real_m, 0.0),
                jnp.where(even, imag_m, 0.0),
                jnp.where(even, 0.0, real_m),
                jnp.where(even, 0.0, imag_m),
            ],
            axis=0,
        ).astype(BF16)
        synth = jnp.dot(mixed, table, preferred_element_type=F32) * quad
        for part in range(2):
            even_part = synth[part * local : (part + 1) * local]
            odd_part = synth[(2 + part) * local : (3 + part) * local]
            for tile in range(tiles):
                lanes = slice(tile * LANES, (tile + 1) * LANES)
                where = lines(tile, part * orders + order)
                north_scr[where] = even_part[:, lanes] + odd_part[:, lanes]
                south_scr[where] = even_part[:, lanes] - odd_part[:, lanes]

    def one_block(block, carry):
        slot = block % slot_count
        for copy in fetch(block, slot):
            copy.wait()

        def several(index, inner_carry):
            for inner in range(unroll):
                at = index * unroll + inner
                one_order(slot, block * orders_here + at, at)
            return inner_carry

        lax.fori_loop(0, orders_here // unroll, several, 0)

        @pl.when(block + slot_count < blocks)
        def _():
            for copy in fetch(block + slot_count, slot):
                copy.start()

        return carry

    lax.fori_loop(0, blocks, one_block, 0)

    def restore(chan, carry):
        rows = pl.ds(pl.multiple_of(chan * pitch, 8), modes)
        profile = jnp.concatenate(
            [scr[tile, rows, :].astype(BF16) for scr in (north_scr, south_scr) for tile in range(tiles)],
            axis=1,
        )
        field = lax.dot_general(
            profile, inverse_ref[...], (((0,), (0,)), ((), ())), preferred_element_type=F32
        )
        at = pl.ds(pl.multiple_of(chan * q_count, 16), q_count)
        for band in range(bands):
            for unit in range(sectors // group):
                pieces = []
                for r in range(group):
                    row = place(band, r)
                    pieces.append(field[row : row + q_count, unit * LANES : (unit + 1) * LANES])
                for k in range(group):
                    value = rolled(pieces[0], -k)
                    for r in range(1, group):
                        value = jnp.where(lane_group == r, rolled(pieces[r], r - k), value)
                    back_ref[band, unit * group + k, at, :] = value.astype(BF16)
        give(chan).start()
        return carry

    lax.fori_loop(0, local, restore, 0)
    for chan in range(local):
        give(chan).wait()


def spectral(received, forward, inverse, tables, weights, quad, group):
    bands, sectors, rows, _ = received.shape
    local = weights.shape[1]
    q_count = rows // local
    orders, degrees, half = tables[0].shape
    lons = forward.shape[1]
    count = len(tables)
    block = max(1, min(orders, 2**19 // (degrees * half)))
    ring = min(orders // block, 4)
    tiles = half // LANES
    anywhere = pl.BlockSpec(memory_space=pl.ANY)
    vmem = pl.BlockSpec(memory_space=pltpu.VMEM)
    lines = pltpu.VMEM((tiles, local * (forward.shape[0] + PAD), LANES), F32)
    return pl.pallas_call(
        functools.partial(
            spectral_kernel, group=group, q_count=q_count, unroll=math.gcd(block, 16), count=count
        ),
        in_specs=[anywhere] + [vmem] * 4 + [anywhere] * count,
        out_specs=anywhere,
        out_shape=jax.ShapeDtypeStruct(received.shape, BF16),
        scratch_shapes=[
            pltpu.VMEM(received.shape, BF16),
            pltpu.VMEM(received.shape, BF16),
            pltpu.VMEM((local, 2 * half, lons), BF16),
            lines,
            lines,
            lines,
            lines,
        ]
        + [pltpu.VMEM((ring, block) + table.shape[1:], BF16) for table in tables]
        + [
            pltpu.SemaphoreType.DMA,
            pltpu.SemaphoreType.DMA((count, ring)),
            pltpu.SemaphoreType.DMA((local,)),
        ],
        compiler_params=params(50 * MIB),
        name="spectral",
    )(received, forward, inverse, weights, quad, *tables)


def disco_kernel(
    tap_ref, grad_ref, low_ref, high_ref, left_ref, right_ref, corner_ref, mix_ref, out_ref, padded, taps_scr
):
    step = pl.program_id(0)
    rows, cols, channels = grad_ref.shape
    rows_here = out_ref.shape[0]
    kernels = mix_ref.shape[0]
    halves = channels // LANES
    origin = 8

    @pl.when(step == 0)
    def _():
        for half in range(halves):
            lanes = slice(half * LANES, (half + 1) * LANES)
            padded[half, REACH : REACH + rows, origin : origin + cols, :] = grad_ref[:, :, lanes].astype(F32)
            corners = corner_ref[:, lanes].astype(F32)
            for edge, (source, base) in enumerate(((low_ref, 0), (high_ref, REACH + rows))):
                values = source[:, lanes].astype(F32)
                for row in range(REACH):
                    padded[half, base + row, origin : origin + cols, :] = values[row * cols : (row + 1) * cols]
                    for side in range(REACH):
                        for end, column in enumerate((origin - REACH, origin + cols)):
                            at = ((end * 2 + edge) * REACH + row) * REACH + side
                            column = column + side
                            padded[half, base + row, column : column + 1, :] = corners[at : at + 1]
            for source, column in ((left_ref, origin - REACH), (right_ref, origin + cols)):
                values = source[:, lanes].astype(F32)
                for side in range(REACH):
                    padded[half, REACH : REACH + rows, column + side, :] = values[side * rows : (side + 1) * rows]

    def one_row(row, carry):
        for half in range(halves):
            sums = [jnp.zeros((cols, LANES), F32) for _ in range(kernels)]
            for lat_tap in range(TAPS):
                source = step * rows_here + row + 2 * REACH - lat_tap
                for lon_tap in range(TAPS):
                    start = origin + REACH - lon_tap
                    slab = padded[half, source, start : start + cols, :]
                    for kernel in range(kernels):
                        tap = tap_ref[source, (kernel * TAPS + lat_tap) * TAPS + lon_tap]
                        sums[kernel] = sums[kernel] + tap * slab
            for kernel in range(kernels):
                taps_scr[kernel, row, :, half * LANES : (half + 1) * LANES] = sums[kernel].astype(BF16)
        return carry

    lax.fori_loop(0, rows_here, one_row, 0)
    total = None
    for kernel in range(kernels):
        flat = taps_scr[kernel].reshape(rows_here * cols, channels)
        term = lax.dot_general(
            flat, mix_ref[kernel], (((1,), (1,)), ((), ())), preferred_element_type=F32
        )
        total = term if total is None else total + term
    out_ref[...] = total.reshape(rows_here, cols, channels)


def disco(taps, grad, low, high, left, right, corners, mix):
    rows, cols, channels = grad.shape
    kernels = mix.shape[0]
    steps = 4

    def whole(shape):
        return pl.BlockSpec(shape, lambda i: (0,) * len(shape))

    return pl.pallas_call(
        disco_kernel,
        grid=(steps,),
        in_specs=[pl.BlockSpec(memory_space=pltpu.SMEM)]
        + [whole(value.shape) for value in (grad, low, high, left, right, corners, mix)],
        out_specs=pl.BlockSpec((rows // steps, cols, channels), lambda i: (i, 0, 0)),
        out_shape=jax.ShapeDtypeStruct(grad.shape, F32),
        scratch_shapes=[
            pltpu.VMEM((channels // LANES, rows + 2 * REACH, cols + 16, LANES), F32),
            pltpu.VMEM((kernels, rows // steps, cols, channels), BF16),
        ],
        compiler_params=params(14 * MIB),
        cost_estimate=pl.CostEstimate(
            flops=1000 * rows * cols * channels, bytes_accessed=8 * rows * cols * channels, transcendentals=0
        ),
        name="disco",
    )(taps, grad, low, high, left, right, corners, mix)


def combine_kernel(
    flip_ref, back_hbm, disco_ref, out_hbm, back_ref, chan_scr, out_ref, in_sems, out_sems, *, group, q_count
):
    rows, cols, channels = disco_ref.shape
    sources, count = back_ref.shape[:2]
    part = rows // CHUNKS
    flip = flip_ref[0]

    def fetch(chunk):
        at = pl.ds(chunk * (sources // CHUNKS), sources // CHUNKS)
        return pltpu.make_async_copy(back_hbm.at[at], back_ref.at[at], in_sems.at[chunk])

    def give(chunk):
        at = pl.ds(chunk * part, part)
        return pltpu.make_async_copy(out_ref.at[at], out_hbm.at[at], out_sems.at[chunk])

    def one_source(source, carry):
        chan_scr[pl.ds(pl.multiple_of(source * count, 16), count), :] = back_ref[source].astype(F32)
        return carry

    def one_block(q_index, carry):
        q_from = jnp.where(flip == 1, q_count - 1 - q_index, q_index)
        turned = jnp.concatenate(
            [
                chan_scr[pl.ds(tile * LANES * q_count + q_from, LANES, stride=q_count), :].T
                for tile in range(channels // LANES)
            ],
            axis=1,
        )
        for r in range(group):
            row = q_index * group + jnp.where(flip == 1, group - 1 - r, r)
            out_ref[row] = (disco_ref[row] + turned[r * cols : (r + 1) * cols]).astype(BF16)
        return carry

    for chunk in range(CHUNKS):
        fetch(chunk).start()
    for chunk in range(CHUNKS):
        fetch(chunk).wait()
        lax.fori_loop(chunk * sources // CHUNKS, (chunk + 1) * sources // CHUNKS, one_source, 0)
    for chunk in range(CHUNKS):
        lax.fori_loop(chunk * part // group, (chunk + 1) * part // group, one_block, 0)
        give(chunk).start()
    for chunk in range(CHUNKS):
        give(chunk).wait()


def combine(back, local_part, flip, group):
    rows, cols, channels = local_part.shape
    q_count = rows // group
    anywhere = pl.BlockSpec(memory_space=pl.ANY)
    return pl.pallas_call(
        functools.partial(combine_kernel, group=group, q_count=q_count),
        in_specs=[
            pl.BlockSpec(memory_space=pltpu.SMEM),
            anywhere,
            pl.BlockSpec(memory_space=pltpu.VMEM),
        ],
        out_specs=anywhere,
        out_shape=jax.ShapeDtypeStruct(local_part.shape, BF16),
        scratch_shapes=[
            pltpu.VMEM(back.shape, BF16),
            pltpu.VMEM((channels * q_count, LANES), F32),
            pltpu.VMEM(local_part.shape, BF16),
            pltpu.SemaphoreType.DMA((CHUNKS,)),
            pltpu.SemaphoreType.DMA((CHUNKS,)),
        ],
        compiler_params=params(12 * MIB),
        name="combine",
    )(flip, back, local_part)


def shifted(block, axis, step):
    count = lax.axis_size(axis)
    return lax.ppermute(block, axis, [(i, (i + step) % count) for i in range(count)])


def corners_of(low, high, channels):
    def ends(start):
        blocks = [side.reshape(REACH, -1, channels)[:, start:][:, :REACH] for side in (low, high)]
        return jnp.concatenate(blocks, axis=0).reshape(2 * REACH * REACH, channels)

    return jnp.concatenate([shifted(ends(-REACH), "lon", 1), shifted(ends(0), "lon", -1)], axis=0)


def fourier_tables(order_count, points):
    order_list = jnp.arange(order_count, dtype=jnp.int32)[:, None]
    grid_pos = jnp.arange(points, dtype=jnp.int32)[None, :]
    angles = 2.0 * math.pi / points * (grid_pos * order_list % points).astype(F32)
    factor = jnp.where(order_list == 0, 1.0, 2.0).astype(F32)
    inverse = jnp.concatenate([jnp.cos(angles), -jnp.sin(angles)], axis=0)
    forward = jnp.concatenate([factor, factor], axis=0) * inverse
    return (forward.astype(BF16), inverse.astype(BF16))


def shards(pre_act, cotangent, spec_weight, disco_weight, disco_filter, support):
    lat_rows, lon_cols, channels = pre_act.shape
    lat_count = lax.axis_size("lat")
    lon_count = lax.axis_size("lon")
    devices = lat_count * lon_count
    band_index = lax.axis_index("lat")
    device_id = band_index * lon_count + lax.axis_index("lon")
    total_lat = lat_rows * lat_count
    total_lon = lon_cols * lon_count
    mode_count = spec_weight.shape[0]
    local = channels // devices
    group = LANES // lon_cols
    q_count = lat_rows // group
    flip = (2 * band_index >= lat_count).astype(jnp.int32).reshape(1)

    grad_pre, to_send, *edges = gradient(pre_act, cotangent, flip, devices, group)
    received = lax.all_to_all(to_send, ("lat", "lon"), 0, 0, tiled=True)

    lane = np.arange(total_lat // 2)
    lats = lane // lat_rows * lat_rows + lane % q_count * group + lane % lat_rows // q_count
    colatitude = math.pi / total_lat * (jnp.asarray(lats, F32) + 0.5)[None, :]
    order_vals = jnp.arange(mode_count, dtype=F32)[:, None]
    start = (
        0.5 * jnp.log((2.0 * order_vals + 1.0) / (4.0 * math.pi))
        + 0.5
        * (
            lax.lgamma(2.0 * order_vals + 1.0)
            - order_vals * math.log(4.0)
            - 2.0 * lax.lgamma(order_vals + 1.0)
        )
        + order_vals * jnp.log(jnp.sin(colatitude))
    )
    degree_norm = jnp.sqrt(jnp.maximum(4.0 * jnp.square(jnp.arange(mode_count, dtype=F32)) - 1.0, 1.0))
    norms = jnp.stack([degree_norm, 1.0 / degree_norm])
    both = mode_count * mode_count * total_lat < 2**25
    tables = legendre(norms, jnp.cos(colatitude), start, both)
    forward, inverse = fourier_tables(mode_count, total_lon)
    quad = 2.0 * math.pi / total_lon * (math.pi / total_lat) * jnp.sin(colatitude)
    weights = jnp.transpose(
        lax.dynamic_slice_in_dim(spec_weight, device_id * local, local, 2), (1, 2, 0)
    )
    offsets = jnp.arange(TAPS, dtype=jnp.int32) - REACH
    allowed = (jnp.abs(offsets)[None, None, :] <= support[:, :, None]).astype(F32)
    tap_coef = jnp.pad(disco_filter * allowed[None], ((0, 0), (REACH, REACH), (0, 0), (0, 0)))
    tap_coef = lax.dynamic_slice_in_dim(tap_coef, band_index * lat_rows, lat_rows + 2 * REACH, 1)
    taps = jnp.transpose(tap_coef, (1, 0, 2, 3)).reshape(lat_rows + 2 * REACH, -1)

    first_rows, last_rows, west, east = edges
    edges, tables = lax.optimization_barrier((edges, tables))
    first_rows, last_rows, west, east = edges
    sides = (
        shifted(last_rows, "lat", 1),
        shifted(first_rows, "lat", -1),
        shifted(east, "lon", 1),
        shifted(west, "lon", -1),
    )
    received, sides = lax.optimization_barrier((received, sides))
    blocks = received.reshape(lat_count, lon_count, local * q_count, LANES)
    back = spectral(blocks, forward, inverse, tables, weights, quad, group)
    back, taps, sides = lax.optimization_barrier((back, taps, sides))
    corners = corners_of(sides[0], sides[1], channels)
    returned = lax.all_to_all(
        back.reshape(devices, local * q_count, LANES), ("lat", "lon"), 0, 0, tiled=True
    )
    local_part = disco(taps, grad_pre, *sides, corners, disco_weight)
    return combine(returned, local_part, flip, group)


def solution(mesh):
    return jax.shard_map(
        shards,
        mesh=mesh,
        in_specs=(P("lat", "lon", None), P("lat", "lon", None), P(), P(), P(), P()),
        out_specs=P("lat", "lon", None),
        check_vma=False,
    )
```

```python
import functools
import math

import jax
import jax.numpy as jnp
import numpy as np
from jax import lax
from jax.experimental import pallas as pl
from jax.experimental.pallas import tpu as pltpu
from jax.sharding import PartitionSpec as P

REACH = 2
TAPS = 2 * REACH + 1
LANES = 128
PAD = 8
CHUNKS = 4
F32 = jnp.float32
BF16 = jnp.bfloat16
MIB = 1024 * 1024


def params(limit):
    return pltpu.CompilerParams(vmem_limit_bytes=limit)


def gelu_slope(pre_values):
    normal_cdf = 0.5 * (1.0 + lax.erf(pre_values * (1.0 / math.sqrt(2.0))))
    density = jnp.exp(-0.5 * pre_values * pre_values) * (1.0 / math.sqrt(2.0 * math.pi))
    return normal_cdf + pre_values * density


def grad_kernel(
    flip_ref, pre_hbm, cot_hbm, grad_hbm, send_hbm, first_ref, last_ref, west_ref, east_ref, corner_ref,
    pre_ref, cot_ref, grad_ref, send_ref, rows_scr, chan_scr, in_sems, out_sems, *, group, q_count,
):
    rows, cols, channels = pre_ref.shape
    part = rows // CHUNKS
    flip = flip_ref[0]

    def fetch(chunk):
        at = pl.ds(chunk * part, part)
        return [
            pltpu.make_async_copy(pre_hbm.at[at], pre_ref.at[at], in_sems.at[0, chunk]),
            pltpu.make_async_copy(cot_hbm.at[at], cot_ref.at[at], in_sems.at[1, chunk]),
        ]

    def keep(chunk):
        at = pl.ds(chunk * part, part)
        return pltpu.make_async_copy(grad_ref.at[at], grad_hbm.at[at], out_sems.at[0, chunk])

    def send(chunk):
        count = send_ref.shape[0] // CHUNKS
        at = pl.ds(chunk * count, count)
        return pltpu.make_async_copy(send_ref.at[at], send_hbm.at[at], out_sems.at[1, chunk])

    for chunk in range(CHUNKS):
        for copy in fetch(chunk):
            copy.start()
    for chunk in range(CHUNKS):
        for copy in fetch(chunk):
            copy.wait()
        for row in range(chunk * part, (chunk + 1) * part):
            grad = (cot_ref[row].astype(F32) * gelu_slope(pre_ref[row].astype(F32))).astype(BF16)
            grad_ref[row] = grad
            rows_scr[row] = grad.astype(F32)
        keep(chunk).start()
        for q_index in range(chunk * part // group, (chunk + 1) * part // group):
            q_out = jnp.where(flip == 1, q_count - 1 - q_index, q_index)
            slabs = []
            for r in range(group):
                slabs.append(rows_scr[q_index * group + jnp.where(flip == 1, group - 1 - r, r)])
            stacked = jnp.concatenate(slabs, axis=0)
            for tile in range(channels // LANES):
                turned = stacked[:, tile * LANES : (tile + 1) * LANES].T
                chan_scr[pl.ds(tile * LANES * q_count + q_out, LANES, stride=q_count), :] = turned
    dests, count = send_ref.shape[:2]
    for chunk in range(CHUNKS):
        for dest in range(chunk * dests // CHUNKS, (chunk + 1) * dests // CHUNKS):
            send_ref[dest] = chan_scr[dest * count : (dest + 1) * count, :].astype(BF16)
        send(chunk).start()
    for row in range(REACH):
        first_ref[row * cols : (row + 1) * cols, :] = grad_ref[row]
        last_ref[row * cols : (row + 1) * cols, :] = grad_ref[rows - REACH + row]
    corners = [
        rows_scr[start + row, column : column + REACH, :]
        for start in (0, rows - REACH)
        for column in (0, cols - REACH)
        for row in range(REACH)
    ]
    corner_ref[...] = jnp.concatenate(corners, axis=0).astype(BF16)
    for side in range(REACH):
        west_ref[side * rows : (side + 1) * rows, :] = rows_scr[:, side, :].astype(BF16)
        east_ref[side * rows : (side + 1) * rows, :] = rows_scr[:, cols - REACH + side, :].astype(BF16)
    for chunk in range(CHUNKS):
        keep(chunk).wait()
        send(chunk).wait()


def gradient(pre_act, cotangent, flip, devices, group):
    rows, cols, channels = pre_act.shape
    q_count = rows // group
    send = (devices, channels // devices * q_count, LANES)
    edges = [(REACH * cols, channels)] * 2 + [(REACH * rows, channels)] * 2
    edges += [(4 * REACH * REACH, channels)]
    anywhere = pl.BlockSpec(memory_space=pl.ANY)
    vmem = pl.BlockSpec(memory_space=pltpu.VMEM)
    return pl.pallas_call(
        functools.partial(grad_kernel, group=group, q_count=q_count),
        in_specs=[pl.BlockSpec(memory_space=pltpu.SMEM), anywhere, anywhere],
        out_specs=[anywhere, anywhere] + [vmem] * len(edges),
        out_shape=[jax.ShapeDtypeStruct(shape, BF16) for shape in (pre_act.shape, send, *edges)],
        scratch_shapes=[
            pltpu.VMEM(pre_act.shape, BF16),
            pltpu.VMEM(pre_act.shape, BF16),
            pltpu.VMEM(pre_act.shape, BF16),
            pltpu.VMEM(send, BF16),
            pltpu.VMEM(pre_act.shape, F32),
            pltpu.VMEM((channels * q_count, LANES), F32),
            pltpu.SemaphoreType.DMA((2, CHUNKS)),
            pltpu.SemaphoreType.DMA((2, CHUNKS)),
        ],
        compiler_params=params(60 * MIB),
        name="gradient",
    )(flip, pre_act, cotangent)


def legendre_kernel(norm_ref, cos_ref, start_ref, *refs, degrees, span):
    scr = refs[-1]
    pitch = degrees + PAD
    table_ref = refs[0]
    orders = table_ref.shape[0]
    groups = orders // 8
    first = pl.program_id(0) * orders
    cosine = jnp.broadcast_to(cos_ref[...], (8, LANES))
    sub = lax.broadcasted_iota(jnp.int32, (8, LANES), 0)
    order_vals = [(first + 8 * g + sub).astype(F32) for g in range(groups)]
    squares = [order * order for order in order_vals]
    zero = jnp.zeros((8, LANES), F32)

    def chunk(index, state):
        latest, earlier, coef_b, scale = (list(part) for part in state)
        factor = [jnp.exp(value) for value in scale]
        for step in range(span):
            degree = index * span + step
            deg_val = degree.astype(F32)
            norm = norm_ref[0, degree]
            inverse_norm = norm_ref[1, degree]
            for g in range(groups):
                gap = jnp.maximum(deg_val * deg_val - squares[g], 1.0)
                root = lax.rsqrt(gap)
                value = (root * norm) * (cosine * latest[g] - coef_b[g] * earlier[g])
                value = jnp.where(order_vals[g] == deg_val, 1.0, value)
                coef_b[g] = gap * root * inverse_norm
                earlier[g] = latest[g]
                latest[g] = value
                scr[pl.ds(g * 8 * pitch + degree, 8, stride=pitch), :] = value * factor[g]
        for g in range(groups):
            large = jnp.maximum(jnp.abs(latest[g]), jnp.abs(earlier[g])) > 2.0**20
            shrink = jnp.where(large, 2.0**-40, 1.0)
            latest[g] = latest[g] * shrink
            earlier[g] = earlier[g] * shrink
            scale[g] = scale[g] + jnp.where(large, 40.0 * math.log(2.0), 0.0)
        return (tuple(latest), tuple(earlier), tuple(coef_b), tuple(scale))

    starts = tuple(start_ref[8 * g : 8 * g + 8, :] for g in range(groups))
    zeros = (zero,) * groups
    lax.fori_loop(0, degrees // span, chunk, (zeros, zeros, zeros, starts))
    for order in range(orders):
        values = scr[order * pitch : order * pitch + degrees, :]
        table_ref[order] = values.astype(BF16)
        for turned_ref in refs[1:-1]:
            turned_ref[order] = values.T.astype(BF16)


def legendre(norms, cosine, start, both):
    orders, points = start.shape
    degrees = norms.shape[1]
    block = math.gcd(orders, 32)
    return pl.pallas_call(
        functools.partial(legendre_kernel, degrees=degrees, span=8),
        grid=(orders // block, points // LANES),
        in_specs=[
            pl.BlockSpec(memory_space=pltpu.SMEM),
            pl.BlockSpec((1, LANES), lambda i, j: (0, j)),
            pl.BlockSpec((block, LANES), lambda i, j: (i, j)),
        ],
        out_specs=[
            pl.BlockSpec((block, degrees, LANES), lambda i, j: (i, 0, j)),
            pl.BlockSpec((block, LANES, degrees), lambda i, j: (i, j, 0)),
        ][: 1 + both],
        out_shape=[
            jax.ShapeDtypeStruct((orders, degrees, points), BF16),
            jax.ShapeDtypeStruct((orders, points, degrees), BF16),
        ][: 1 + both],
        scratch_shapes=[pltpu.VMEM((block * (degrees + PAD), LANES), F32)],
        compiler_params=params(56 * MIB),
        cost_estimate=pl.CostEstimate(
            flops=4000 * orders * degrees * points,
            bytes_accessed=4 * orders * degrees * points,
            transcendentals=0,
        ),
        name="legendre",
    )(norms, cosine, start)


def spectral_kernel(
    recv_hbm, forward_ref, inverse_ref, weight_ref, quad_ref, *refs, group, q_count, unroll, count
):
    tables = refs[:count]
    back_hbm, recv_ref, back_ref, grid_scr, even_scr, odd_scr, north_scr, south_scr = refs[count : count + 8]
    slots = refs[count + 8 : 2 * count + 8]
    recv_sem, table_sems, back_sems = refs[2 * count + 8 :]
    bands, sectors = recv_ref.shape[:2]
    local, lats, lons = grid_scr.shape
    slot_count, orders_here, degrees, half = slots[0].shape
    tiles = half // LANES
    modes = forward_ref.shape[0]
    orders = modes // 2
    blocks = orders // orders_here
    pitch = modes + PAD
    band_rows = group * q_count
    width = LANES // group
    lane_group = lax.broadcasted_iota(jnp.int32, (q_count, LANES), 1) // width

    def fetch(block, slot):
        at = pl.ds(block * orders_here, orders_here)
        return [
            pltpu.make_async_copy(table.at[at], ring.at[slot], table_sems.at[kind, slot])
            for kind, (table, ring) in enumerate(zip(tables, slots))
        ]

    def give(chan):
        at = pl.ds(chan * q_count, q_count)
        return pltpu.make_async_copy(back_ref.at[:, :, at], back_hbm.at[:, :, at], back_sems.at[chan])

    def place(band, r):
        if band < bands // 2:
            return band * band_rows + r * q_count
        return lats // 2 + (bands - 1 - band) * band_rows + r * q_count

    def rolled(value, places):
        shift = places * width % LANES
        return value if shift == 0 else pltpu.roll(value, shift, 1)

    receive = pltpu.make_async_copy(recv_hbm, recv_ref, recv_sem)
    receive.start()
    for block in range(slot_count):
        for copy in fetch(block, block):
            copy.start()
    receive.wait()

    for chan in range(local):
        at = chan * q_count
        for band in range(bands):
            for unit in range(sectors // group):
                pieces = [
                    recv_ref[band, unit * group + k, at : at + q_count, :].astype(F32) for k in range(group)
                ]
                for r in range(group):
                    value = rolled(pieces[0], -r)
                    for k in range(1, group):
                        value = jnp.where(lane_group == k, rolled(pieces[k], k - r), value)
                    row = place(band, r)
                    grid_scr[chan, row : row + q_count, unit * LANES : (unit + 1) * LANES] = value.astype(BF16)
        spectrum = lax.dot_general(
            forward_ref[...], grid_scr[chan], (((1,), (1,)), ((), ())), preferred_element_type=F32
        )
        for tile in range(tiles):
            north = spectrum[:, tile * LANES : (tile + 1) * LANES]
            south = spectrum[:, half + tile * LANES : half + (tile + 1) * LANES]
            even_scr[tile, chan * pitch : chan * pitch + modes, :] = north + south
            odd_scr[tile, chan * pitch : chan * pitch + modes, :] = north - south

    def lines(tile, mode):
        if local == 1:
            return (tile, pl.ds(mode, 1), slice(None))
        return (tile, pl.ds(mode, local, stride=pitch), slice(None))

    def load(scr, mode):
        parts = [scr[lines(tile, mode)] for tile in range(tiles)]
        return parts[0] if tiles == 1 else jnp.concatenate(parts, axis=1)

    degree_lane = lax.broadcasted_iota(jnp.int32, (local, degrees), 1)
    real_w = weight_ref[0]
    imag_w = weight_ref[1]
    quad = quad_ref[...]

    def one_order(slot, order, index):
        table = slots[0][slot, index]
        even = (degree_lane + order) % 2 == 0
        stacked = jnp.concatenate(
            [
                load(even_scr, order),
                load(even_scr, orders + order),
                load(odd_scr, order),
                load(odd_scr, orders + order),
            ],
            axis=0,
        ).astype(BF16)
        if count == 2:
            analysed = jnp.dot(stacked, slots[1][slot, index], preferred_element_type=F32)
        else:
            analysed = lax.dot_general(
                stacked, table, (((1,), (1,)), ((), ())), preferred_element_type=F32
            )
        real_a = jnp.where(even, analysed[0:local], analysed[2 * local : 3 * local])
        imag_a = jnp.where(even, analysed[local : 2 * local], analysed[3 * local : 4 * local])
        real_m = real_w * real_a + imag_w * imag_a
        imag_m = real_w * imag_a - imag_w * real_a
        mixed = jnp.concatenate(
            [
                jnp.where(even, real_m, 0.0),
                jnp.where(even, imag_m, 0.0),
                jnp.where(even, 0.0, real_m),
                jnp.where(even, 0.0, imag_m),
            ],
            axis=0,
        ).astype(BF16)
        synth = jnp.dot(mixed, table, preferred_element_type=F32) * quad
        for part in range(2):
            even_part = synth[part * local : (part + 1) * local]
            odd_part = synth[(2 + part) * local : (3 + part) * local]
            for tile in range(tiles):
                lanes = slice(tile * LANES, (tile + 1) * LANES)
                where = lines(tile, part * orders + order)
                north_scr[where] = even_part[:, lanes] + odd_part[:, lanes]
                south_scr[where] = even_part[:, lanes] - odd_part[:, lanes]

    def one_block(block, carry):
        slot = block % slot_count
        for copy in fetch(block, slot):
            copy.wait()

        def several(index, inner_carry):
            for inner in range(unroll):
                at = index * unroll + inner
                one_order(slot, block * orders_here + at, at)
            return inner_carry

        lax.fori_loop(0, orders_here // unroll, several, 0)

        @pl.when(block + slot_count < blocks)
        def _():
            for copy in fetch(block + slot_count, slot):
                copy.start()

        return carry

    lax.fori_loop(0, blocks, one_block, 0)

    for chan in range(local):
        rows = slice(chan * pitch, chan * pitch + modes)
        profile = jnp.concatenate(
            [scr[tile, rows, :].astype(BF16) for scr in (north_scr, south_scr) for tile in range(tiles)],
            axis=1,
        )
        field = lax.dot_general(
            profile, inverse_ref[...], (((0,), (0,)), ((), ())), preferred_element_type=F32
        )
        at = chan * q_count
        for band in range(bands):
            for unit in range(sectors // group):
                pieces = []
                for r in range(group):
                    row = place(band, r)
                    pieces.append(field[row : row + q_count, unit * LANES : (unit + 1) * LANES])
                for k in range(group):
                    value = rolled(pieces[0], -k)
                    for r in range(1, group):
                        value = jnp.where(lane_group == r, rolled(pieces[r], r - k), value)
                    back_ref[band, unit * group + k, at : at + q_count, :] = value.astype(BF16)
        give(chan).start()
    for chan in range(local):
        give(chan).wait()


def spectral(received, forward, inverse, tables, weights, quad, group):
    bands, sectors, rows, _ = received.shape
    local = weights.shape[1]
    q_count = rows // local
    orders, degrees, half = tables[0].shape
    lons = forward.shape[1]
    count = len(tables)
    block = max(1, min(orders, 2**19 // (degrees * half)))
    ring = min(orders // block, 4)
    tiles = half // LANES
    anywhere = pl.BlockSpec(memory_space=pl.ANY)
    vmem = pl.BlockSpec(memory_space=pltpu.VMEM)
    lines = pltpu.VMEM((tiles, local * (forward.shape[0] + PAD), LANES), F32)
    return pl.pallas_call(
        functools.partial(
            spectral_kernel, group=group, q_count=q_count, unroll=math.gcd(block, 16), count=count
        ),
        in_specs=[anywhere] + [vmem] * 4 + [anywhere] * count,
        out_specs=anywhere,
        out_shape=jax.ShapeDtypeStruct(received.shape, BF16),
        scratch_shapes=[
            pltpu.VMEM(received.shape, BF16),
            pltpu.VMEM(received.shape, BF16),
            pltpu.VMEM((local, 2 * half, lons), BF16),
            lines,
            lines,
            lines,
            lines,
        ]
        + [pltpu.VMEM((ring, block) + table.shape[1:], BF16) for table in tables]
        + [
            pltpu.SemaphoreType.DMA,
            pltpu.SemaphoreType.DMA((count, ring)),
            pltpu.SemaphoreType.DMA((local,)),
        ],
        compiler_params=params(50 * MIB),
        name="spectral",
    )(received, forward, inverse, weights, quad, *tables)


def disco_kernel(
    tap_ref, diagonal_ref, grad_ref, low_ref, high_ref, left_ref, right_ref, corner_ref, mix_ref, out_ref, padded, taps_scr
):
    step = pl.program_id(0)
    rows, cols, channels = grad_ref.shape
    rows_here = out_ref.shape[0]
    kernels = mix_ref.shape[0]
    halves = channels // LANES
    origin = 8

    @pl.when(step == 0)
    def _():
        for half in range(halves):
            lanes = slice(half * LANES, (half + 1) * LANES)
            padded[half, REACH : REACH + rows, origin : origin + cols, :] = grad_ref[:, :, lanes].astype(F32)
            for edge, (source, base) in enumerate(((low_ref, 0), (high_ref, REACH + rows))):
                values = source[:, lanes].astype(F32)
                for row in range(REACH):
                    padded[half, base + row, origin : origin + cols, :] = values[row * cols : (row + 1) * cols]
            for which in range(4):
                block = corner_ref[diagonal_ref[which]][:, lanes].astype(F32)
                base = (0, REACH + rows)[which // 2]
                column = (origin - REACH, origin + cols)[which % 2]
                for row in range(REACH):
                    at = ((3 - which) * REACH + row) * REACH
                    padded[half, base + row, column : column + REACH, :] = block[at : at + REACH]
            for source, column in ((left_ref, origin - REACH), (right_ref, origin + cols)):
                values = source[:, lanes].astype(F32)
                for side in range(REACH):
                    padded[half, REACH : REACH + rows, column + side, :] = values[side * rows : (side + 1) * rows]

    def one_row(row, carry):
        for half in range(halves):
            sums = [jnp.zeros((cols, LANES), F32) for _ in range(kernels)]
            for lat_tap in range(TAPS):
                source = step * rows_here + row + 2 * REACH - lat_tap
                for lon_tap in range(TAPS):
                    start = origin + REACH - lon_tap
                    slab = padded[half, source, start : start + cols, :]
                    for kernel in range(kernels):
                        tap = tap_ref[source, (kernel * TAPS + lat_tap) * TAPS + lon_tap]
                        sums[kernel] = sums[kernel] + tap * slab
            for kernel in range(kernels):
                taps_scr[kernel, row, :, half * LANES : (half + 1) * LANES] = sums[kernel].astype(BF16)
        return carry

    lax.fori_loop(0, rows_here, one_row, 0)
    total = None
    for kernel in range(kernels):
        flat = taps_scr[kernel].reshape(rows_here * cols, channels)
        term = lax.dot_general(
            flat, mix_ref[kernel], (((1,), (1,)), ((), ())), preferred_element_type=F32
        )
        total = term if total is None else total + term
    out_ref[...] = total.reshape(rows_here, cols, channels)


def disco(taps, diagonal, grad, low, high, left, right, corners, mix):
    rows, cols, channels = grad.shape
    kernels = mix.shape[0]
    steps = 4

    def whole(shape):
        return pl.BlockSpec(shape, lambda i: (0,) * len(shape))

    return pl.pallas_call(
        disco_kernel,
        grid=(steps,),
        in_specs=[pl.BlockSpec(memory_space=pltpu.SMEM)] * 2
        + [whole(value.shape) for value in (grad, low, high, left, right, corners, mix)],
        out_specs=pl.BlockSpec((rows // steps, cols, channels), lambda i: (i, 0, 0)),
        out_shape=jax.ShapeDtypeStruct(grad.shape, F32),
        scratch_shapes=[
            pltpu.VMEM((channels // LANES, rows + 2 * REACH, cols + 16, LANES), F32),
            pltpu.VMEM((kernels, rows // steps, cols, channels), BF16),
        ],
        compiler_params=params(14 * MIB),
        cost_estimate=pl.CostEstimate(
            flops=1000 * rows * cols * channels, bytes_accessed=8 * rows * cols * channels, transcendentals=0
        ),
        name="disco",
    )(taps, diagonal, grad, low, high, left, right, corners, mix)


def combine_kernel(
    flip_ref, back_hbm, disco_ref, out_hbm, back_ref, chan_scr, out_ref, in_sems, out_sems, *, group, q_count
):
    rows, cols, channels = disco_ref.shape
    sources, count = back_ref.shape[:2]
    part = rows // CHUNKS
    flip = flip_ref[0]

    def fetch(chunk):
        at = pl.ds(chunk * (sources // CHUNKS), sources // CHUNKS)
        return pltpu.make_async_copy(back_hbm.at[at], back_ref.at[at], in_sems.at[chunk])

    def give(chunk):
        at = pl.ds(chunk * part, part)
        return pltpu.make_async_copy(out_ref.at[at], out_hbm.at[at], out_sems.at[chunk])

    for chunk in range(CHUNKS):
        fetch(chunk).start()
    for chunk in range(CHUNKS):
        fetch(chunk).wait()
        for source in range(chunk * sources // CHUNKS, (chunk + 1) * sources // CHUNKS):
            chan_scr[source * count : (source + 1) * count, :] = back_ref[source].astype(F32)
    for chunk in range(CHUNKS):
        for q_index in range(chunk * part // group, (chunk + 1) * part // group):
            q_from = jnp.where(flip == 1, q_count - 1 - q_index, q_index)
            turned = jnp.concatenate(
                [
                    chan_scr[pl.ds(tile * LANES * q_count + q_from, LANES, stride=q_count), :].T
                    for tile in range(channels // LANES)
                ],
                axis=1,
            )
            for r in range(group):
                row = q_index * group + jnp.where(flip == 1, group - 1 - r, r)
                out_ref[row] = (disco_ref[row] + turned[r * cols : (r + 1) * cols]).astype(BF16)
        give(chunk).start()
    for chunk in range(CHUNKS):
        give(chunk).wait()


def combine(back, local_part, flip, group):
    rows, cols, channels = local_part.shape
    q_count = rows // group
    anywhere = pl.BlockSpec(memory_space=pl.ANY)
    return pl.pallas_call(
        functools.partial(combine_kernel, group=group, q_count=q_count),
        in_specs=[
            pl.BlockSpec(memory_space=pltpu.SMEM),
            anywhere,
            pl.BlockSpec(memory_space=pltpu.VMEM),
        ],
        out_specs=anywhere,
        out_shape=jax.ShapeDtypeStruct(local_part.shape, BF16),
        scratch_shapes=[
            pltpu.VMEM(back.shape, BF16),
            pltpu.VMEM((channels * q_count, LANES), F32),
            pltpu.VMEM(local_part.shape, BF16),
            pltpu.SemaphoreType.DMA((CHUNKS,)),
            pltpu.SemaphoreType.DMA((CHUNKS,)),
        ],
        compiler_params=params(12 * MIB),
        name="combine",
    )(flip, back, local_part)


def shifted(block, axis, step):
    count = lax.axis_size(axis)
    return lax.ppermute(block, axis, [(i, (i + step) % count) for i in range(count)])


def fourier_tables(order_count, points):
    order_list = jnp.arange(order_count, dtype=jnp.int32)[:, None]
    grid_pos = jnp.arange(points, dtype=jnp.int32)[None, :]
    angles = 2.0 * math.pi / points * (grid_pos * order_list % points).astype(F32)
    factor = jnp.where(order_list == 0, 1.0, 2.0).astype(F32)
    inverse = jnp.concatenate([jnp.cos(angles), -jnp.sin(angles)], axis=0)
    forward = jnp.concatenate([factor, factor], axis=0) * inverse
    return (forward.astype(BF16), inverse.astype(BF16))


def shards(pre_act, cotangent, spec_weight, disco_weight, disco_filter, support):
    lat_rows, lon_cols, channels = pre_act.shape
    lat_count = lax.axis_size("lat")
    lon_count = lax.axis_size("lon")
    devices = lat_count * lon_count
    band_index = lax.axis_index("lat")
    device_id = band_index * lon_count + lax.axis_index("lon")
    total_lat = lat_rows * lat_count
    total_lon = lon_cols * lon_count
    mode_count = spec_weight.shape[0]
    local = channels // devices
    group = LANES // lon_cols
    q_count = lat_rows // group
    flip = (2 * band_index >= lat_count).astype(jnp.int32).reshape(1)

    grad_pre, to_send, *edges = gradient(pre_act, cotangent, flip, devices, group)
    received = lax.all_to_all(to_send, ("lat", "lon"), 0, 0, tiled=True)

    lane = np.arange(total_lat // 2)
    lats = lane // lat_rows * lat_rows + lane % q_count * group + lane % lat_rows // q_count
    colatitude = math.pi / total_lat * (jnp.asarray(lats, F32) + 0.5)[None, :]
    order_vals = jnp.arange(mode_count, dtype=F32)[:, None]
    start = (
        0.5 * jnp.log((2.0 * order_vals + 1.0) / (4.0 * math.pi))
        + 0.5
        * (
            lax.lgamma(2.0 * order_vals + 1.0)
            - order_vals * math.log(4.0)
            - 2.0 * lax.lgamma(order_vals + 1.0)
        )
        + order_vals * jnp.log(jnp.sin(colatitude))
    )
    degree_norm = jnp.sqrt(jnp.maximum(4.0 * jnp.square(jnp.arange(mode_count, dtype=F32)) - 1.0, 1.0))
    norms = jnp.stack([degree_norm, 1.0 / degree_norm])
    both = mode_count * mode_count * total_lat < 2**25
    tables = legendre(norms, jnp.cos(colatitude), start, both)
    forward, inverse = fourier_tables(mode_count, total_lon)
    quad = 2.0 * math.pi / total_lon * (math.pi / total_lat) * jnp.sin(colatitude)
    weights = jnp.transpose(
        lax.dynamic_slice_in_dim(spec_weight, device_id * local, local, 2), (1, 2, 0)
    )
    offsets = jnp.arange(TAPS, dtype=jnp.int32) - REACH
    allowed = (jnp.abs(offsets)[None, None, :] <= support[:, :, None]).astype(F32)
    tap_coef = jnp.pad(disco_filter * allowed[None], ((0, 0), (REACH, REACH), (0, 0), (0, 0)))
    tap_coef = lax.dynamic_slice_in_dim(tap_coef, band_index * lat_rows, lat_rows + 2 * REACH, 1)
    taps = jnp.transpose(tap_coef, (1, 0, 2, 3)).reshape(lat_rows + 2 * REACH, -1)

    everyone = lax.all_gather(edges.pop(), ("lat", "lon"))
    edges, tables = lax.optimization_barrier((edges, tables))
    first_rows, last_rows, west, east = edges
    sides = (
        shifted(last_rows, "lat", 1),
        shifted(first_rows, "lat", -1),
        shifted(east, "lon", 1),
        shifted(west, "lon", -1),
    )
    received, sides, everyone = lax.optimization_barrier((received, sides, everyone))
    lat_steps = np.array([-1, -1, 1, 1])
    lon_steps = np.array([-1, 1, -1, 1])
    diagonal = (band_index + lat_steps) % lat_count * lon_count
    diagonal = diagonal + (lax.axis_index("lon") + lon_steps) % lon_count
    blocks = received.reshape(lat_count, lon_count, local * q_count, LANES)
    back = spectral(blocks, forward, inverse, tables, weights, quad, group)
    back, taps = lax.optimization_barrier((back, taps))
    returned = lax.all_to_all(
        back.reshape(devices, local * q_count, LANES), ("lat", "lon"), 0, 0, tiled=True
    )
    local_part = disco(taps, diagonal, grad_pre, *sides, everyone, disco_weight)
    return combine(returned, local_part, flip, group)


def solution(mesh):
    return jax.shard_map(
        shards,
        mesh=mesh,
        in_specs=(P("lat", "lon", None), P("lat", "lon", None), P(), P(), P(), P()),
        out_specs=P("lat", "lon", None),
        check_vma=False,
    )
```

```python
import functools
import math

import jax
import jax.numpy as jnp
import numpy as np
from jax import lax
from jax.experimental import pallas as pl
from jax.experimental.pallas import tpu as pltpu
from jax.sharding import PartitionSpec as P

REACH = 2
TAPS = 2 * REACH + 1
LANES = 128
PAD = 8
CHUNKS = 4
F32 = jnp.float32
BF16 = jnp.bfloat16
MIB = 1024 * 1024


def params(limit):
    return pltpu.CompilerParams(vmem_limit_bytes=limit)


def gelu_slope(pre_values):
    normal_cdf = 0.5 * (1.0 + lax.erf(pre_values * (1.0 / math.sqrt(2.0))))
    density = jnp.exp(-0.5 * pre_values * pre_values) * (1.0 / math.sqrt(2.0 * math.pi))
    return normal_cdf + pre_values * density


def grad_kernel(
    flip_ref, pre_hbm, cot_hbm, grad_hbm, send_hbm, first_ref, last_ref, west_ref, east_ref,
    pre_ref, cot_ref, grad_ref, send_ref, rows_scr, chan_scr, in_sems, out_sems, *, group, q_count,
):
    rows, cols, channels = pre_ref.shape
    part = rows // CHUNKS
    flip = flip_ref[0]

    def fetch(chunk):
        at = pl.ds(chunk * part, part)
        return [
            pltpu.make_async_copy(pre_hbm.at[at], pre_ref.at[at], in_sems.at[0, chunk]),
            pltpu.make_async_copy(cot_hbm.at[at], cot_ref.at[at], in_sems.at[1, chunk]),
        ]

    def keep(chunk):
        at = pl.ds(chunk * part, part)
        return pltpu.make_async_copy(grad_ref.at[at], grad_hbm.at[at], out_sems.at[0, chunk])

    def send(chunk):
        count = send_ref.shape[0] // CHUNKS
        at = pl.ds(chunk * count, count)
        return pltpu.make_async_copy(send_ref.at[at], send_hbm.at[at], out_sems.at[1, chunk])

    for chunk in range(CHUNKS):
        for copy in fetch(chunk):
            copy.start()
    for chunk in range(CHUNKS):
        for copy in fetch(chunk):
            copy.wait()
        for row in range(chunk * part, (chunk + 1) * part):
            grad = (cot_ref[row].astype(F32) * gelu_slope(pre_ref[row].astype(F32))).astype(BF16)
            grad_ref[row] = grad
            rows_scr[row] = grad.astype(F32)
        keep(chunk).start()
        for q_index in range(chunk * part // group, (chunk + 1) * part // group):
            q_out = jnp.where(flip == 1, q_count - 1 - q_index, q_index)
            slabs = []
            for r in range(group):
                slabs.append(rows_scr[q_index * group + jnp.where(flip == 1, group - 1 - r, r)])
            stacked = jnp.concatenate(slabs, axis=0)
            for tile in range(channels // LANES):
                turned = stacked[:, tile * LANES : (tile + 1) * LANES].T
                chan_scr[pl.ds(tile * LANES * q_count + q_out, LANES, stride=q_count), :] = turned
    dests, count = send_ref.shape[:2]
    for chunk in range(CHUNKS):
        for dest in range(chunk * dests // CHUNKS, (chunk + 1) * dests // CHUNKS):
            send_ref[dest] = chan_scr[dest * count : (dest + 1) * count, :].astype(BF16)
        send(chunk).start()
    for row in range(REACH):
        first_ref[row * cols : (row + 1) * cols, :] = grad_ref[row]
        last_ref[row * cols : (row + 1) * cols, :] = grad_ref[rows - REACH + row]
    for side in range(REACH):
        west_ref[side * rows : (side + 1) * rows, :] = rows_scr[:, side, :].astype(BF16)
        east_ref[side * rows : (side + 1) * rows, :] = rows_scr[:, cols - REACH + side, :].astype(BF16)
    for chunk in range(CHUNKS):
        keep(chunk).wait()
        send(chunk).wait()


def gradient(pre_act, cotangent, flip, devices, group):
    rows, cols, channels = pre_act.shape
    q_count = rows // group
    send = (devices, channels // devices * q_count, LANES)
    edges = [(REACH * cols, channels)] * 2 + [(REACH * rows, channels)] * 2
    anywhere = pl.BlockSpec(memory_space=pl.ANY)
    vmem = pl.BlockSpec(memory_space=pltpu.VMEM)
    return pl.pallas_call(
        functools.partial(grad_kernel, group=group, q_count=q_count),
        in_specs=[pl.BlockSpec(memory_space=pltpu.SMEM), anywhere, anywhere],
        out_specs=[anywhere, anywhere] + [vmem] * len(edges),
        out_shape=[jax.ShapeDtypeStruct(shape, BF16) for shape in (pre_act.shape, send, *edges)],
        scratch_shapes=[
            pltpu.VMEM(pre_act.shape, BF16),
            pltpu.VMEM(pre_act.shape, BF16),
            pltpu.VMEM(pre_act.shape, BF16),
            pltpu.VMEM(send, BF16),
            pltpu.VMEM(pre_act.shape, F32),
            pltpu.VMEM((channels * q_count, LANES), F32),
            pltpu.SemaphoreType.DMA((2, CHUNKS)),
            pltpu.SemaphoreType.DMA((2, CHUNKS)),
        ],
        compiler_params=params(60 * MIB),
        name="gradient",
    )(flip, pre_act, cotangent)


def legendre_kernel(norm_ref, cos_ref, start_ref, *refs, degrees, span):
    scr = refs[-1]
    pitch = degrees + PAD
    table_ref = refs[0]
    orders = table_ref.shape[0]
    groups = orders // 8
    first = pl.program_id(0) * orders
    cosine = jnp.broadcast_to(cos_ref[...], (8, LANES))
    sub = lax.broadcasted_iota(jnp.int32, (8, LANES), 0)
    order_vals = [(first + 8 * g + sub).astype(F32) for g in range(groups)]
    squares = [order * order for order in order_vals]
    zero = jnp.zeros((8, LANES), F32)

    def chunk(index, state):
        latest, earlier, coef_b, scale = (list(part) for part in state)
        factor = [jnp.exp(value) for value in scale]
        for step in range(span):
            degree = index * span + step
            deg_val = degree.astype(F32)
            norm = norm_ref[0, degree]
            inverse_norm = norm_ref[1, degree]
            for g in range(groups):
                gap = jnp.maximum(deg_val * deg_val - squares[g], 1.0)
                root = lax.rsqrt(gap)
                value = (root * norm) * (cosine * latest[g] - coef_b[g] * earlier[g])
                value = jnp.where(order_vals[g] == deg_val, 1.0, value)
                coef_b[g] = gap * root * inverse_norm
                earlier[g] = latest[g]
                latest[g] = value
                scr[pl.ds(g * 8 * pitch + degree, 8, stride=pitch), :] = value * factor[g]
        for g in range(groups):
            large = jnp.maximum(jnp.abs(latest[g]), jnp.abs(earlier[g])) > 2.0**20
            shrink = jnp.where(large, 2.0**-40, 1.0)
            latest[g] = latest[g] * shrink
            earlier[g] = earlier[g] * shrink
            scale[g] = scale[g] + jnp.where(large, 40.0 * math.log(2.0), 0.0)
        return (tuple(latest), tuple(earlier), tuple(coef_b), tuple(scale))

    starts = tuple(start_ref[8 * g : 8 * g + 8, :] for g in range(groups))
    zeros = (zero,) * groups
    lax.fori_loop(0, degrees // span, chunk, (zeros, zeros, zeros, starts))
    for order in range(orders):
        values = scr[order * pitch : order * pitch + degrees, :]
        table_ref[order] = values.astype(BF16)
        for turned_ref in refs[1:-1]:
            turned_ref[order] = values.T.astype(BF16)


def legendre(norms, cosine, start, both):
    orders, points = start.shape
    degrees = norms.shape[1]
    block = math.gcd(orders, 32)
    return pl.pallas_call(
        functools.partial(legendre_kernel, degrees=degrees, span=8),
        grid=(orders // block, points // LANES),
        in_specs=[
            pl.BlockSpec(memory_space=pltpu.SMEM),
            pl.BlockSpec((1, LANES), lambda i, j: (0, j)),
            pl.BlockSpec((block, LANES), lambda i, j: (i, j)),
        ],
        out_specs=[
            pl.BlockSpec((block, degrees, LANES), lambda i, j: (i, 0, j)),
            pl.BlockSpec((block, LANES, degrees), lambda i, j: (i, j, 0)),
        ][: 1 + both],
        out_shape=[
            jax.ShapeDtypeStruct((orders, degrees, points), BF16),
            jax.ShapeDtypeStruct((orders, points, degrees), BF16),
        ][: 1 + both],
        scratch_shapes=[pltpu.VMEM((block * (degrees + PAD), LANES), F32)],
        compiler_params=params(56 * MIB),
        cost_estimate=pl.CostEstimate(
            flops=4000 * orders * degrees * points,
            bytes_accessed=4 * orders * degrees * points,
            transcendentals=0,
        ),
        name="legendre",
    )(norms, cosine, start)


def spectral_kernel(
    recv_hbm, forward_ref, inverse_ref, weight_ref, quad_ref, *refs, group, q_count, unroll, count
):
    tables = refs[:count]
    back_hbm, recv_ref, back_ref, grid_scr, even_scr, odd_scr, north_scr, south_scr = refs[count : count + 8]
    slots = refs[count + 8 : 2 * count + 8]
    recv_sem, table_sems, back_sems = refs[2 * count + 8 :]
    bands, sectors = recv_ref.shape[:2]
    local, lats, lons = grid_scr.shape
    slot_count, orders_here, degrees, half = slots[0].shape
    tiles = half // LANES
    modes = forward_ref.shape[0]
    orders = modes // 2
    blocks = orders // orders_here
    pitch = modes + PAD
    band_rows = group * q_count
    width = LANES // group
    lane_group = lax.broadcasted_iota(jnp.int32, (q_count, LANES), 1) // width

    def fetch(block, slot):
        at = pl.ds(block * orders_here, orders_here)
        return [
            pltpu.make_async_copy(table.at[at], ring.at[slot], table_sems.at[kind, slot])
            for kind, (table, ring) in enumerate(zip(tables, slots))
        ]

    def give(chan):
        at = pl.ds(chan * q_count, q_count)
        return pltpu.make_async_copy(back_ref.at[:, :, at], back_hbm.at[:, :, at], back_sems.at[chan])

    def place(band, r):
        if band < bands // 2:
            return band * band_rows + r * q_count
        return lats // 2 + (bands - 1 - band) * band_rows + r * q_count

    def rolled(value, places):
        shift = places * width % LANES
        return value if shift == 0 else pltpu.roll(value, shift, 1)

    receive = pltpu.make_async_copy(recv_hbm, recv_ref, recv_sem)
    receive.start()
    for block in range(slot_count):
        for copy in fetch(block, block):
            copy.start()
    receive.wait()

    for chan in range(local):
        at = chan * q_count
        for band in range(bands):
            for unit in range(sectors // group):
                pieces = [
                    recv_ref[band, unit * group + k, at : at + q_count, :].astype(F32) for k in range(group)
                ]
                for r in range(group):
                    value = rolled(pieces[0], -r)
                    for k in range(1, group):
                        value = jnp.where(lane_group == k, rolled(pieces[k], k - r), value)
                    row = place(band, r)
                    grid_scr[chan, row : row + q_count, unit * LANES : (unit + 1) * LANES] = value.astype(BF16)
        spectrum = lax.dot_general(
            forward_ref[...], grid_scr[chan], (((1,), (1,)), ((), ())), preferred_element_type=F32
        )
        for tile in range(tiles):
            north = spectrum[:, tile * LANES : (tile + 1) * LANES]
            south = spectrum[:, half + tile * LANES : half + (tile + 1) * LANES]
            even_scr[tile, chan * pitch : chan * pitch + modes, :] = north + south
            odd_scr[tile, chan * pitch : chan * pitch + modes, :] = north - south

    def lines(tile, mode):
        if local == 1:
            return (tile, pl.ds(mode, 1), slice(None))
        return (tile, pl.ds(mode, local, stride=pitch), slice(None))

    def load(scr, mode):
        parts = [scr[lines(tile, mode)] for tile in range(tiles)]
        return parts[0] if tiles == 1 else jnp.concatenate(parts, axis=1)

    degree_lane = lax.broadcasted_iota(jnp.int32, (local, degrees), 1)
    real_w = weight_ref[0]
    imag_w = weight_ref[1]
    quad = quad_ref[...]

    def one_order(slot, order, index):
        table = slots[0][slot, index]
        even = (degree_lane + order) % 2 == 0
        stacked = jnp.concatenate(
            [
                load(even_scr, order),
                load(even_scr, orders + order),
                load(odd_scr, order),
                load(odd_scr, orders + order),
            ],
            axis=0,
        ).astype(BF16)
        if count == 2:
            analysed = jnp.dot(stacked, slots[1][slot, index], preferred_element_type=F32)
        else:
            analysed = lax.dot_general(
                stacked, table, (((1,), (1,)), ((), ())), preferred_element_type=F32
            )
        real_a = jnp.where(even, analysed[0:local], analysed[2 * local : 3 * local])
        imag_a = jnp.where(even, analysed[local : 2 * local], analysed[3 * local : 4 * local])
        real_m = real_w * real_a + imag_w * imag_a
        imag_m = real_w * imag_a - imag_w * real_a
        mixed = jnp.concatenate(
            [
                jnp.where(even, real_m, 0.0),
                jnp.where(even, imag_m, 0.0),
                jnp.where(even, 0.0, real_m),
                jnp.where(even, 0.0, imag_m),
            ],
            axis=0,
        ).astype(BF16)
        synth = jnp.dot(mixed, table, preferred_element_type=F32) * quad
        for part in range(2):
            even_part = synth[part * local : (part + 1) * local]
            odd_part = synth[(2 + part) * local : (3 + part) * local]
            for tile in range(tiles):
                lanes = slice(tile * LANES, (tile + 1) * LANES)
                where = lines(tile, part * orders + order)
                north_scr[where] = even_part[:, lanes] + odd_part[:, lanes]
                south_scr[where] = even_part[:, lanes] - odd_part[:, lanes]

    def one_block(block, carry):
        slot = block % slot_count
        for copy in fetch(block, slot):
            copy.wait()

        def several(index, inner_carry):
            for inner in range(unroll):
                at = index * unroll + inner
                one_order(slot, block * orders_here + at, at)
            return inner_carry

        lax.fori_loop(0, orders_here // unroll, several, 0)

        @pl.when(block + slot_count < blocks)
        def _():
            for copy in fetch(block + slot_count, slot):
                copy.start()

        return carry

    lax.fori_loop(0, blocks, one_block, 0)

    for chan in range(local):
        rows = slice(chan * pitch, chan * pitch + modes)
        profile = jnp.concatenate(
            [scr[tile, rows, :].astype(BF16) for scr in (north_scr, south_scr) for tile in range(tiles)],
            axis=1,
        )
        field = lax.dot_general(
            profile, inverse_ref[...], (((0,), (0,)), ((), ())), preferred_element_type=F32
        )
        at = chan * q_count
        for band in range(bands):
            for unit in range(sectors // group):
                pieces = []
                for r in range(group):
                    row = place(band, r)
                    pieces.append(field[row : row + q_count, unit * LANES : (unit + 1) * LANES])
                for k in range(group):
                    value = rolled(pieces[0], -k)
                    for r in range(1, group):
                        value = jnp.where(lane_group == r, rolled(pieces[r], r - k), value)
                    back_ref[band, unit * group + k, at : at + q_count, :] = value.astype(BF16)
        give(chan).start()
    for chan in range(local):
        give(chan).wait()


def spectral(received, forward, inverse, tables, weights, quad, group):
    bands, sectors, rows, _ = received.shape
    local = weights.shape[1]
    q_count = rows // local
    orders, degrees, half = tables[0].shape
    lons = forward.shape[1]
    count = len(tables)
    block = max(1, min(orders, 2**19 // (degrees * half)))
    ring = min(orders // block, 4)
    tiles = half // LANES
    anywhere = pl.BlockSpec(memory_space=pl.ANY)
    vmem = pl.BlockSpec(memory_space=pltpu.VMEM)
    lines = pltpu.VMEM((tiles, local * (forward.shape[0] + PAD), LANES), F32)
    return pl.pallas_call(
        functools.partial(
            spectral_kernel, group=group, q_count=q_count, unroll=math.gcd(block, 16), count=count
        ),
        in_specs=[anywhere] + [vmem] * 4 + [anywhere] * count,
        out_specs=anywhere,
        out_shape=jax.ShapeDtypeStruct(received.shape, BF16),
        scratch_shapes=[
            pltpu.VMEM(received.shape, BF16),
            pltpu.VMEM(received.shape, BF16),
            pltpu.VMEM((local, 2 * half, lons), BF16),
            lines,
            lines,
            lines,
            lines,
        ]
        + [pltpu.VMEM((ring, block) + table.shape[1:], BF16) for table in tables]
        + [
            pltpu.SemaphoreType.DMA,
            pltpu.SemaphoreType.DMA((count, ring)),
            pltpu.SemaphoreType.DMA((local,)),
        ],
        compiler_params=params(50 * MIB),
        cost_estimate=pl.CostEstimate(
            flops=2**33 * orders // 128, bytes_accessed=4 * orders * degrees * half, transcendentals=0
        ),
        name="spectral",
    )(received, forward, inverse, weights, quad, *tables)


def disco_kernel(
    tap_ref, grad_ref, low_ref, high_ref, left_ref, right_ref, corner_ref, mix_ref, out_ref, padded, taps_scr
):
    step = pl.program_id(0)
    rows, cols, channels = grad_ref.shape
    rows_here = out_ref.shape[0]
    kernels = mix_ref.shape[0]
    halves = channels // LANES
    origin = 8

    @pl.when(step == 0)
    def _():
        for half in range(halves):
            lanes = slice(half * LANES, (half + 1) * LANES)
            padded[half, REACH : REACH + rows, origin : origin + cols, :] = grad_ref[:, :, lanes].astype(F32)
            for edge, (source, base) in enumerate(((low_ref, 0), (high_ref, REACH + rows))):
                values = source[:, lanes].astype(F32)
                for row in range(REACH):
                    padded[half, base + row, origin : origin + cols, :] = values[row * cols : (row + 1) * cols]
            for which in range(4):
                values = corner_ref[:, lanes].astype(F32)
                base = (0, REACH + rows)[which % 2]
                column = (origin - REACH, origin + cols)[which // 2]
                for row in range(REACH):
                    at = (which * REACH + row) * REACH
                    padded[half, base + row, column : column + REACH, :] = values[at : at + REACH]
            for source, column in ((left_ref, origin - REACH), (right_ref, origin + cols)):
                values = source[:, lanes].astype(F32)
                for side in range(REACH):
                    padded[half, REACH : REACH + rows, column + side, :] = values[side * rows : (side + 1) * rows]

    def one_row(row, carry):
        for half in range(halves):
            sums = [jnp.zeros((cols, LANES), F32) for _ in range(kernels)]
            for lat_tap in range(TAPS):
                source = step * rows_here + row + 2 * REACH - lat_tap
                for lon_tap in range(TAPS):
                    start = origin + REACH - lon_tap
                    slab = padded[half, source, start : start + cols, :]
                    for kernel in range(kernels):
                        tap = tap_ref[source, (kernel * TAPS + lat_tap) * TAPS + lon_tap]
                        sums[kernel] = sums[kernel] + tap * slab
            for kernel in range(kernels):
                taps_scr[kernel, row, :, half * LANES : (half + 1) * LANES] = sums[kernel].astype(BF16)
        return carry

    lax.fori_loop(0, rows_here, one_row, 0)
    total = None
    for kernel in range(kernels):
        flat = taps_scr[kernel].reshape(rows_here * cols, channels)
        term = lax.dot_general(
            flat, mix_ref[kernel], (((1,), (1,)), ((), ())), preferred_element_type=F32
        )
        total = term if total is None else total + term
    out_ref[...] = total.reshape(rows_here, cols, channels)


def disco(taps, grad, low, high, left, right, corners, mix):
    rows, cols, channels = grad.shape
    kernels = mix.shape[0]
    steps = 4

    def whole(shape):
        return pl.BlockSpec(shape, lambda i: (0,) * len(shape))

    return pl.pallas_call(
        disco_kernel,
        grid=(steps,),
        in_specs=[pl.BlockSpec(memory_space=pltpu.SMEM)]
        + [whole(value.shape) for value in (grad, low, high, left, right, corners, mix)],
        out_specs=pl.BlockSpec((rows // steps, cols, channels), lambda i: (i, 0, 0)),
        out_shape=jax.ShapeDtypeStruct(grad.shape, F32),
        scratch_shapes=[
            pltpu.VMEM((channels // LANES, rows + 2 * REACH, cols + 16, LANES), F32),
            pltpu.VMEM((kernels, rows // steps, cols, channels), BF16),
        ],
        compiler_params=params(14 * MIB),
        cost_estimate=pl.CostEstimate(
            flops=1000 * rows * cols * channels, bytes_accessed=8 * rows * cols * channels, transcendentals=0
        ),
        name="disco",
    )(taps, grad, low, high, left, right, corners, mix)


def combine_kernel(
    flip_ref, back_hbm, disco_ref, out_hbm, back_ref, chan_scr, out_ref, in_sems, out_sems, *, group, q_count
):
    rows, cols, channels = disco_ref.shape
    sources, count = back_ref.shape[:2]
    part = rows // CHUNKS
    flip = flip_ref[0]

    def fetch(chunk):
        at = pl.ds(chunk * (sources // CHUNKS), sources // CHUNKS)
        return pltpu.make_async_copy(back_hbm.at[at], back_ref.at[at], in_sems.at[chunk])

    def give(chunk):
        at = pl.ds(chunk * part, part)
        return pltpu.make_async_copy(out_ref.at[at], out_hbm.at[at], out_sems.at[chunk])

    for chunk in range(CHUNKS):
        fetch(chunk).start()
    for chunk in range(CHUNKS):
        fetch(chunk).wait()
        for source in range(chunk * sources // CHUNKS, (chunk + 1) * sources // CHUNKS):
            chan_scr[source * count : (source + 1) * count, :] = back_ref[source].astype(F32)
    for chunk in range(CHUNKS):
        for q_index in range(chunk * part // group, (chunk + 1) * part // group):
            q_from = jnp.where(flip == 1, q_count - 1 - q_index, q_index)
            turned = jnp.concatenate(
                [
                    chan_scr[pl.ds(tile * LANES * q_count + q_from, LANES, stride=q_count), :].T
                    for tile in range(channels // LANES)
                ],
                axis=1,
            )
            for r in range(group):
                row = q_index * group + jnp.where(flip == 1, group - 1 - r, r)
                out_ref[row] = (disco_ref[row] + turned[r * cols : (r + 1) * cols]).astype(BF16)
        give(chunk).start()
    for chunk in range(CHUNKS):
        give(chunk).wait()


def combine(back, local_part, flip, group):
    rows, cols, channels = local_part.shape
    q_count = rows // group
    anywhere = pl.BlockSpec(memory_space=pl.ANY)
    return pl.pallas_call(
        functools.partial(combine_kernel, group=group, q_count=q_count),
        in_specs=[
            pl.BlockSpec(memory_space=pltpu.SMEM),
            anywhere,
            pl.BlockSpec(memory_space=pltpu.VMEM),
        ],
        out_specs=anywhere,
        out_shape=jax.ShapeDtypeStruct(local_part.shape, BF16),
        scratch_shapes=[
            pltpu.VMEM(back.shape, BF16),
            pltpu.VMEM((channels * q_count, LANES), F32),
            pltpu.VMEM(local_part.shape, BF16),
            pltpu.SemaphoreType.DMA((CHUNKS,)),
            pltpu.SemaphoreType.DMA((CHUNKS,)),
        ],
        compiler_params=params(12 * MIB),
        name="combine",
    )(flip, back, local_part)


def shifted(block, axis, step):
    count = lax.axis_size(axis)
    return lax.ppermute(block, axis, [(i, (i + step) % count) for i in range(count)])


def corners_of(low, high, channels):
    def ends(start):
        blocks = [side.reshape(REACH, -1, channels)[:, start:][:, :REACH] for side in (low, high)]
        return jnp.concatenate(blocks, axis=0).reshape(2 * REACH * REACH, channels)

    return jnp.concatenate([shifted(ends(-REACH), "lon", 1), shifted(ends(0), "lon", -1)], axis=0)


def fourier_tables(order_count, points):
    order_list = jnp.arange(order_count, dtype=jnp.int32)[:, None]
    grid_pos = jnp.arange(points, dtype=jnp.int32)[None, :]
    angles = 2.0 * math.pi / points * (grid_pos * order_list % points).astype(F32)
    factor = jnp.where(order_list == 0, 1.0, 2.0).astype(F32)
    inverse = jnp.concatenate([jnp.cos(angles), -jnp.sin(angles)], axis=0)
    forward = jnp.concatenate([factor, factor], axis=0) * inverse
    return (forward.astype(BF16), inverse.astype(BF16))


def shards(pre_act, cotangent, spec_weight, disco_weight, disco_filter, support):
    lat_rows, lon_cols, channels = pre_act.shape
    lat_count = lax.axis_size("lat")
    lon_count = lax.axis_size("lon")
    devices = lat_count * lon_count
    band_index = lax.axis_index("lat")
    device_id = band_index * lon_count + lax.axis_index("lon")
    total_lat = lat_rows * lat_count
    total_lon = lon_cols * lon_count
    mode_count = spec_weight.shape[0]
    local = channels // devices
    group = LANES // lon_cols
    q_count = lat_rows // group
    flip = (2 * band_index >= lat_count).astype(jnp.int32).reshape(1)

    grad_pre, to_send, *edges = gradient(pre_act, cotangent, flip, devices, group)
    received = lax.all_to_all(to_send, ("lat", "lon"), 0, 0, tiled=True)

    lane = np.arange(total_lat // 2)
    lats = lane // lat_rows * lat_rows + lane % q_count * group + lane % lat_rows // q_count
    colatitude = math.pi / total_lat * (jnp.asarray(lats, F32) + 0.5)[None, :]
    order_vals = jnp.arange(mode_count, dtype=F32)[:, None]
    start = (
        0.5 * jnp.log((2.0 * order_vals + 1.0) / (4.0 * math.pi))
        + 0.5
        * (
            lax.lgamma(2.0 * order_vals + 1.0)
            - order_vals * math.log(4.0)
            - 2.0 * lax.lgamma(order_vals + 1.0)
        )
        + order_vals * jnp.log(jnp.sin(colatitude))
    )
    degree_norm = jnp.sqrt(jnp.maximum(4.0 * jnp.square(jnp.arange(mode_count, dtype=F32)) - 1.0, 1.0))
    norms = jnp.stack([degree_norm, 1.0 / degree_norm])
    both = mode_count * mode_count * total_lat < 2**25
    tables = legendre(norms, jnp.cos(colatitude), start, both)
    forward, inverse = fourier_tables(mode_count, total_lon)
    quad = 2.0 * math.pi / total_lon * (math.pi / total_lat) * jnp.sin(colatitude)
    weights = jnp.transpose(
        lax.dynamic_slice_in_dim(spec_weight, device_id * local, local, 2), (1, 2, 0)
    )
    offsets = jnp.arange(TAPS, dtype=jnp.int32) - REACH
    allowed = (jnp.abs(offsets)[None, None, :] <= support[:, :, None]).astype(F32)
    tap_coef = jnp.pad(disco_filter * allowed[None], ((0, 0), (REACH, REACH), (0, 0), (0, 0)))
    tap_coef = lax.dynamic_slice_in_dim(tap_coef, band_index * lat_rows, lat_rows + 2 * REACH, 1)
    taps = jnp.transpose(tap_coef, (1, 0, 2, 3)).reshape(lat_rows + 2 * REACH, -1)

    edges, tables = lax.optimization_barrier((edges, tables))
    first_rows, last_rows, west, east = edges
    sides = (
        shifted(last_rows, "lat", 1),
        shifted(first_rows, "lat", -1),
        shifted(east, "lon", 1),
        shifted(west, "lon", -1),
    )
    corners = corners_of(sides[0], sides[1], channels)
    received, sides = lax.optimization_barrier((received, sides))
    blocks = received.reshape(lat_count, lon_count, local * q_count, LANES)
    back = spectral(blocks, forward, inverse, tables, weights, quad, group)
    back, taps, corners = lax.optimization_barrier((back, taps, corners))
    returned = lax.all_to_all(
        back.reshape(devices, local * q_count, LANES), ("lat", "lon"), 0, 0, tiled=True
    )
    local_part = disco(taps, grad_pre, *sides, corners, disco_weight)
    return combine(returned, local_part, flip, group)


def solution(mesh):
    return jax.shard_map(
        shards,
        mesh=mesh,
        in_specs=(P("lat", "lon", None), P("lat", "lon", None), P(), P(), P(), P()),
        out_specs=P("lat", "lon", None),
        check_vma=False,
    )
```

```python
import functools
import math

import jax
import jax.numpy as jnp
import numpy as np
from jax import lax
from jax.experimental import pallas as pl
from jax.experimental.pallas import tpu as pltpu
from jax.sharding import PartitionSpec as P

REACH = 2
TAPS = 2 * REACH + 1
LANES = 128
PAD = 8
CHUNKS = 4
F32 = jnp.float32
BF16 = jnp.bfloat16
MIB = 1024 * 1024


def params(limit):
    return pltpu.CompilerParams(vmem_limit_bytes=limit)


def gelu_slope(pre_values):
    normal_cdf = 0.5 * (1.0 + lax.erf(pre_values * (1.0 / math.sqrt(2.0))))
    density = jnp.exp(-0.5 * pre_values * pre_values) * (1.0 / math.sqrt(2.0 * math.pi))
    return normal_cdf + pre_values * density


def grad_kernel(
    flip_ref, pre_hbm, cot_hbm, grad_hbm, send_hbm, first_ref, last_ref, west_ref, east_ref,
    pre_ref, cot_ref, grad_ref, send_ref, rows_scr, chan_scr, in_sems, out_sems, *, group, q_count,
):
    rows, cols, channels = pre_ref.shape
    part = rows // CHUNKS
    flip = flip_ref[0]

    def fetch(chunk):
        at = pl.ds(chunk * part, part)
        return [
            pltpu.make_async_copy(pre_hbm.at[at], pre_ref.at[at], in_sems.at[0, chunk]),
            pltpu.make_async_copy(cot_hbm.at[at], cot_ref.at[at], in_sems.at[1, chunk]),
        ]

    def keep(chunk):
        at = pl.ds(chunk * part, part)
        return pltpu.make_async_copy(grad_ref.at[at], grad_hbm.at[at], out_sems.at[0, chunk])

    def send(chunk):
        count = send_ref.shape[0] // CHUNKS
        at = pl.ds(chunk * count, count)
        return pltpu.make_async_copy(send_ref.at[at], send_hbm.at[at], out_sems.at[1, chunk])

    for chunk in range(CHUNKS):
        for copy in fetch(chunk):
            copy.start()
    for chunk in range(CHUNKS):
        for copy in fetch(chunk):
            copy.wait()
        for row in range(chunk * part, (chunk + 1) * part):
            grad = (cot_ref[row].astype(F32) * gelu_slope(pre_ref[row].astype(F32))).astype(BF16)
            grad_ref[row] = grad
            rows_scr[row] = grad.astype(F32)
        keep(chunk).start()
        for q_index in range(chunk * part // group, (chunk + 1) * part // group):
            q_out = jnp.where(flip == 1, q_count - 1 - q_index, q_index)
            slabs = []
            for r in range(group):
                slabs.append(rows_scr[q_index * group + jnp.where(flip == 1, group - 1 - r, r)])
            stacked = jnp.concatenate(slabs, axis=0)
            for tile in range(channels // LANES):
                turned = stacked[:, tile * LANES : (tile + 1) * LANES].T
                chan_scr[pl.ds(tile * LANES * q_count + q_out, LANES, stride=q_count), :] = turned
    dests, count = send_ref.shape[:2]
    for chunk in range(CHUNKS):
        for dest in range(chunk * dests // CHUNKS, (chunk + 1) * dests // CHUNKS):
            send_ref[dest] = chan_scr[dest * count : (dest + 1) * count, :].astype(BF16)
        send(chunk).start()
    for row in range(REACH):
        first_ref[row * cols : (row + 1) * cols, :] = grad_ref[row]
        last_ref[row * cols : (row + 1) * cols, :] = grad_ref[rows - REACH + row]
    for side in range(REACH):
        west_ref[side * rows : (side + 1) * rows, :] = rows_scr[:, side, :].astype(BF16)
        east_ref[side * rows : (side + 1) * rows, :] = rows_scr[:, cols - REACH + side, :].astype(BF16)
    for chunk in range(CHUNKS):
        keep(chunk).wait()
        send(chunk).wait()


def gradient(pre_act, cotangent, flip, devices, group):
    rows, cols, channels = pre_act.shape
    q_count = rows // group
    send = (devices, channels // devices * q_count, LANES)
    edges = [(REACH * cols, channels)] * 2 + [(REACH * rows, channels)] * 2
    anywhere = pl.BlockSpec(memory_space=pl.ANY)
    vmem = pl.BlockSpec(memory_space=pltpu.VMEM)
    return pl.pallas_call(
        functools.partial(grad_kernel, group=group, q_count=q_count),
        in_specs=[pl.BlockSpec(memory_space=pltpu.SMEM), anywhere, anywhere],
        out_specs=[anywhere, anywhere] + [vmem] * len(edges),
        out_shape=[jax.ShapeDtypeStruct(shape, BF16) for shape in (pre_act.shape, send, *edges)],
        scratch_shapes=[
            pltpu.VMEM(pre_act.shape, BF16),
            pltpu.VMEM(pre_act.shape, BF16),
            pltpu.VMEM(pre_act.shape, BF16),
            pltpu.VMEM(send, BF16),
            pltpu.VMEM(pre_act.shape, F32),
            pltpu.VMEM((channels * q_count, LANES), F32),
            pltpu.SemaphoreType.DMA((2, CHUNKS)),
            pltpu.SemaphoreType.DMA((2, CHUNKS)),
        ],
        compiler_params=params(60 * MIB),
        name="gradient",
    )(flip, pre_act, cotangent)


def legendre_kernel(norm_ref, cos_ref, start_ref, *refs, degrees, span):
    scr = refs[-1]
    pitch = degrees + PAD
    table_ref = refs[0]
    orders = table_ref.shape[0]
    groups = orders // 8
    first = pl.program_id(0) * orders
    cosine = jnp.broadcast_to(cos_ref[...], (8, LANES))
    sub = lax.broadcasted_iota(jnp.int32, (8, LANES), 0)
    order_vals = [(first + 8 * g + sub).astype(F32) for g in range(groups)]
    squares = [order * order for order in order_vals]
    zero = jnp.zeros((8, LANES), F32)

    def chunk(index, state):
        latest, earlier, coef_b, scale = (list(part) for part in state)
        factor = [jnp.exp(value) for value in scale]
        for step in range(span):
            degree = index * span + step
            deg_val = degree.astype(F32)
            norm = norm_ref[0, degree]
            inverse_norm = norm_ref[1, degree]
            for g in range(groups):
                gap = jnp.maximum(deg_val * deg_val - squares[g], 1.0)
                root = lax.rsqrt(gap)
                value = (root * norm) * (cosine * latest[g] - coef_b[g] * earlier[g])
                value = jnp.where(order_vals[g] == deg_val, 1.0, value)
                coef_b[g] = gap * root * inverse_norm
                earlier[g] = latest[g]
                latest[g] = value
                scr[pl.ds(g * 8 * pitch + degree, 8, stride=pitch), :] = value * factor[g]
        for g in range(groups):
            large = jnp.maximum(jnp.abs(latest[g]), jnp.abs(earlier[g])) > 2.0**20
            shrink = jnp.where(large, 2.0**-40, 1.0)
            latest[g] = latest[g] * shrink
            earlier[g] = earlier[g] * shrink
            scale[g] = scale[g] + jnp.where(large, 40.0 * math.log(2.0), 0.0)
        return (tuple(latest), tuple(earlier), tuple(coef_b), tuple(scale))

    starts = tuple(start_ref[8 * g : 8 * g + 8, :] for g in range(groups))
    zeros = (zero,) * groups
    lax.fori_loop(0, degrees // span, chunk, (zeros, zeros, zeros, starts))
    for order in range(orders):
        values = scr[order * pitch : order * pitch + degrees, :]
        table_ref[order] = values.astype(BF16)
        for turned_ref in refs[1:-1]:
            turned_ref[order] = values.T.astype(BF16)


def legendre(norms, cosine, start, both):
    orders, points = start.shape
    degrees = norms.shape[1]
    block = math.gcd(orders, 32)
    return pl.pallas_call(
        functools.partial(legendre_kernel, degrees=degrees, span=8),
        grid=(orders // block, points // LANES),
        in_specs=[
            pl.BlockSpec(memory_space=pltpu.SMEM),
            pl.BlockSpec((1, LANES), lambda i, j: (0, j)),
            pl.BlockSpec((block, LANES), lambda i, j: (i, j)),
        ],
        out_specs=[
            pl.BlockSpec((block, degrees, LANES), lambda i, j: (i, 0, j)),
            pl.BlockSpec((block, LANES, degrees), lambda i, j: (i, j, 0)),
        ][: 1 + both],
        out_shape=[
            jax.ShapeDtypeStruct((orders, degrees, points), BF16),
            jax.ShapeDtypeStruct((orders, points, degrees), BF16),
        ][: 1 + both],
        scratch_shapes=[pltpu.VMEM((block * (degrees + PAD), LANES), F32)],
        compiler_params=params(56 * MIB),
        cost_estimate=pl.CostEstimate(
            flops=4000 * orders * degrees * points,
            bytes_accessed=4 * orders * degrees * points,
            transcendentals=0,
        ),
        name="legendre",
    )(norms, cosine, start)


def spectral_kernel(
    recv_hbm, forward_ref, inverse_ref, weight_ref, quad_ref, *refs, group, q_count, unroll, count
):
    tables = refs[:count]
    back_hbm, recv_ref, back_ref, grid_scr, even_scr, odd_scr, north_scr, south_scr = refs[count : count + 8]
    slots = refs[count + 8 : 2 * count + 8]
    recv_sem, table_sems, back_sems = refs[2 * count + 8 :]
    bands, sectors = recv_ref.shape[:2]
    local, lats, lons = grid_scr.shape
    slot_count, orders_here, degrees, half = slots[0].shape
    tiles = half // LANES
    modes = forward_ref.shape[0]
    orders = modes // 2
    blocks = orders // orders_here
    pitch = modes + PAD
    band_rows = group * q_count
    width = LANES // group
    lane_group = lax.broadcasted_iota(jnp.int32, (q_count, LANES), 1) // width

    def fetch(block, slot):
        at = pl.ds(block * orders_here, orders_here)
        return [
            pltpu.make_async_copy(table.at[at], ring.at[slot], table_sems.at[kind, slot])
            for kind, (table, ring) in enumerate(zip(tables, slots))
        ]

    def give(chan):
        at = pl.ds(chan * q_count, q_count)
        return pltpu.make_async_copy(back_ref.at[:, :, at], back_hbm.at[:, :, at], back_sems.at[chan])

    def place(band, r):
        if band < bands // 2:
            return band * band_rows + r * q_count
        return lats // 2 + (bands - 1 - band) * band_rows + r * q_count

    def rolled(value, places):
        shift = places * width % LANES
        return value if shift == 0 else pltpu.roll(value, shift, 1)

    receive = pltpu.make_async_copy(recv_hbm, recv_ref, recv_sem)
    receive.start()
    for block in range(slot_count):
        for copy in fetch(block, block):
            copy.start()
    receive.wait()

    for chan in range(local):
        at = chan * q_count
        for band in range(bands):
            for unit in range(sectors // group):
                pieces = [
                    recv_ref[band, unit * group + k, at : at + q_count, :].astype(F32) for k in range(group)
                ]
                for r in range(group):
                    value = rolled(pieces[0], -r)
                    for k in range(1, group):
                        value = jnp.where(lane_group == k, rolled(pieces[k], k - r), value)
                    row = place(band, r)
                    grid_scr[chan, row : row + q_count, unit * LANES : (unit + 1) * LANES] = value.astype(BF16)
        spectrum = lax.dot_general(
            forward_ref[...], grid_scr[chan], (((1,), (1,)), ((), ())), preferred_element_type=F32
        )
        for tile in range(tiles):
            north = spectrum[:, tile * LANES : (tile + 1) * LANES]
            south = spectrum[:, half + tile * LANES : half + (tile + 1) * LANES]
            even_scr[tile, chan * pitch : chan * pitch + modes, :] = north + south
            odd_scr[tile, chan * pitch : chan * pitch + modes, :] = north - south

    def lines(tile, mode):
        if local == 1:
            return (tile, pl.ds(mode, 1), slice(None))
        return (tile, pl.ds(mode, local, stride=pitch), slice(None))

    def load(scr, mode):
        parts = [scr[lines(tile, mode)] for tile in range(tiles)]
        return parts[0] if tiles == 1 else jnp.concatenate(parts, axis=1)

    degree_lane = lax.broadcasted_iota(jnp.int32, (local, degrees), 1)
    real_w = weight_ref[0]
    imag_w = weight_ref[1]
    quad = quad_ref[...]

    def one_order(slot, order, index):
        table = slots[0][slot, index]
        even = (degree_lane + order) % 2 == 0
        stacked = jnp.concatenate(
            [
                load(even_scr, order),
                load(even_scr, orders + order),
                load(odd_scr, order),
                load(odd_scr, orders + order),
            ],
            axis=0,
        ).astype(BF16)
        if count == 2:
            analysed = jnp.dot(stacked, slots[1][slot, index], preferred_element_type=F32)
        else:
            analysed = lax.dot_general(
                stacked, table, (((1,), (1,)), ((), ())), preferred_element_type=F32
            )
        real_a = jnp.where(even, analysed[0:local], analysed[2 * local : 3 * local])
        imag_a = jnp.where(even, analysed[local : 2 * local], analysed[3 * local : 4 * local])
        real_m = real_w * real_a + imag_w * imag_a
        imag_m = real_w * imag_a - imag_w * real_a
        mixed = jnp.concatenate(
            [
                jnp.where(even, real_m, 0.0),
                jnp.where(even, imag_m, 0.0),
                jnp.where(even, 0.0, real_m),
                jnp.where(even, 0.0, imag_m),
            ],
            axis=0,
        ).astype(BF16)
        synth = jnp.dot(mixed, table, preferred_element_type=F32) * quad
        for part in range(2):
            even_part = synth[part * local : (part + 1) * local]
            odd_part = synth[(2 + part) * local : (3 + part) * local]
            for tile in range(tiles):
                lanes = slice(tile * LANES, (tile + 1) * LANES)
                where = lines(tile, part * orders + order)
                north_scr[where] = even_part[:, lanes] + odd_part[:, lanes]
                south_scr[where] = even_part[:, lanes] - odd_part[:, lanes]

    def one_block(block, carry):
        slot = block % slot_count
        for copy in fetch(block, slot):
            copy.wait()

        def several(index, inner_carry):
            for inner in range(unroll):
                at = index * unroll + inner
                one_order(slot, block * orders_here + at, at)
            return inner_carry

        lax.fori_loop(0, orders_here // unroll, several, 0)

        @pl.when(block + slot_count < blocks)
        def _():
            for copy in fetch(block + slot_count, slot):
                copy.start()

        return carry

    lax.fori_loop(0, blocks, one_block, 0)

    for chan in range(local):
        rows = slice(chan * pitch, chan * pitch + modes)
        profile = jnp.concatenate(
            [scr[tile, rows, :].astype(BF16) for scr in (north_scr, south_scr) for tile in range(tiles)],
            axis=1,
        )
        field = lax.dot_general(
            profile, inverse_ref[...], (((0,), (0,)), ((), ())), preferred_element_type=F32
        )
        at = chan * q_count
        for band in range(bands):
            for unit in range(sectors // group):
                pieces = []
                for r in range(group):
                    row = place(band, r)
                    pieces.append(field[row : row + q_count, unit * LANES : (unit + 1) * LANES])
                for k in range(group):
                    value = rolled(pieces[0], -k)
                    for r in range(1, group):
                        value = jnp.where(lane_group == r, rolled(pieces[r], r - k), value)
                    back_ref[band, unit * group + k, at : at + q_count, :] = value.astype(BF16)
        give(chan).start()
    for chan in range(local):
        give(chan).wait()


def spectral(received, forward, inverse, tables, weights, quad, group):
    bands, sectors, rows, _ = received.shape
    local = weights.shape[1]
    q_count = rows // local
    orders, degrees, half = tables[0].shape
    lons = forward.shape[1]
    count = len(tables)
    block = max(1, min(orders, 2**19 // (degrees * half)))
    ring = min(orders // block, 4)
    tiles = half // LANES
    anywhere = pl.BlockSpec(memory_space=pl.ANY)
    vmem = pl.BlockSpec(memory_space=pltpu.VMEM)
    lines = pltpu.VMEM((tiles, local * (forward.shape[0] + PAD), LANES), F32)
    return pl.pallas_call(
        functools.partial(
            spectral_kernel, group=group, q_count=q_count, unroll=math.gcd(block, 32), count=count
        ),
        in_specs=[anywhere] + [vmem] * 4 + [anywhere] * count,
        out_specs=anywhere,
        out_shape=jax.ShapeDtypeStruct(received.shape, BF16),
        scratch_shapes=[
            pltpu.VMEM(received.shape, BF16),
            pltpu.VMEM(received.shape, BF16),
            pltpu.VMEM((local, 2 * half, lons), BF16),
            lines,
            lines,
            lines,
            lines,
        ]
        + [pltpu.VMEM((ring, block) + table.shape[1:], BF16) for table in tables]
        + [
            pltpu.SemaphoreType.DMA,
            pltpu.SemaphoreType.DMA((count, ring)),
            pltpu.SemaphoreType.DMA((local,)),
        ],
        compiler_params=params(50 * MIB),
        cost_estimate=pl.CostEstimate(
            flops=2**33 * orders // 128, bytes_accessed=4 * orders * degrees * half, transcendentals=0
        ),
        name="spectral",
    )(received, forward, inverse, weights, quad, *tables)


def disco_kernel(
    tap_ref, grad_ref, low_ref, high_ref, left_ref, right_ref, corner_ref, mix_ref, out_ref, padded, taps_scr
):
    step = pl.program_id(0)
    rows, cols, channels = grad_ref.shape
    rows_here = out_ref.shape[0]
    kernels = mix_ref.shape[0]
    halves = channels // LANES
    origin = 8

    @pl.when(step == 0)
    def _():
        for half in range(halves):
            lanes = slice(half * LANES, (half + 1) * LANES)
            padded[half, REACH : REACH + rows, origin : origin + cols, :] = grad_ref[:, :, lanes].astype(F32)
            for edge, (source, base) in enumerate(((low_ref, 0), (high_ref, REACH + rows))):
                values = source[:, lanes].astype(F32)
                for row in range(REACH):
                    padded[half, base + row, origin : origin + cols, :] = values[row * cols : (row + 1) * cols]
            for which in range(4):
                values = corner_ref[:, lanes].astype(F32)
                base = (0, REACH + rows)[which % 2]
                column = (origin - REACH, origin + cols)[which // 2]
                for row in range(REACH):
                    at = (which * REACH + row) * REACH
                    padded[half, base + row, column : column + REACH, :] = values[at : at + REACH]
            for source, column in ((left_ref, origin - REACH), (right_ref, origin + cols)):
                values = source[:, lanes].astype(F32)
                for side in range(REACH):
                    padded[half, REACH : REACH + rows, column + side, :] = values[side * rows : (side + 1) * rows]

    def one_row(row, carry):
        for half in range(halves):
            sums = [jnp.zeros((cols, LANES), F32) for _ in range(kernels)]
            for lat_tap in range(TAPS):
                source = step * rows_here + row + 2 * REACH - lat_tap
                for lon_tap in range(TAPS):
                    start = origin + REACH - lon_tap
                    slab = padded[half, source, start : start + cols, :]
                    for kernel in range(kernels):
                        tap = tap_ref[source, (kernel * TAPS + lat_tap) * TAPS + lon_tap]
                        sums[kernel] = sums[kernel] + tap * slab
            for kernel in range(kernels):
                taps_scr[kernel, row, :, half * LANES : (half + 1) * LANES] = sums[kernel].astype(BF16)
        return carry

    lax.fori_loop(0, rows_here, one_row, 0)
    total = None
    for kernel in range(kernels):
        flat = taps_scr[kernel].reshape(rows_here * cols, channels)
        term = lax.dot_general(
            flat, mix_ref[kernel], (((1,), (1,)), ((), ())), preferred_element_type=F32
        )
        total = term if total is None else total + term
    out_ref[...] = total.reshape(rows_here, cols, channels)


def disco(taps, grad, low, high, left, right, corners, mix):
    rows, cols, channels = grad.shape
    kernels = mix.shape[0]
    steps = 4

    def whole(shape):
        return pl.BlockSpec(shape, lambda i: (0,) * len(shape))

    return pl.pallas_call(
        disco_kernel,
        grid=(steps,),
        in_specs=[pl.BlockSpec(memory_space=pltpu.SMEM)]
        + [whole(value.shape) for value in (grad, low, high, left, right, corners, mix)],
        out_specs=pl.BlockSpec((rows // steps, cols, channels), lambda i: (i, 0, 0)),
        out_shape=jax.ShapeDtypeStruct(grad.shape, F32),
        scratch_shapes=[
            pltpu.VMEM((channels // LANES, rows + 2 * REACH, cols + 16, LANES), F32),
            pltpu.VMEM((kernels, rows // steps, cols, channels), BF16),
        ],
        compiler_params=params(14 * MIB),
        cost_estimate=pl.CostEstimate(
            flops=1000 * rows * cols * channels, bytes_accessed=8 * rows * cols * channels, transcendentals=0
        ),
        name="disco",
    )(taps, grad, low, high, left, right, corners, mix)


def combine_kernel(
    flip_ref, back_hbm, disco_ref, out_hbm, back_ref, chan_scr, out_ref, in_sems, out_sems, *, group, q_count
):
    rows, cols, channels = disco_ref.shape
    sources, count = back_ref.shape[:2]
    part = rows // CHUNKS
    flip = flip_ref[0]

    def fetch(chunk):
        at = pl.ds(chunk * (sources // CHUNKS), sources // CHUNKS)
        return pltpu.make_async_copy(back_hbm.at[at], back_ref.at[at], in_sems.at[chunk])

    def give(chunk):
        at = pl.ds(chunk * part, part)
        return pltpu.make_async_copy(out_ref.at[at], out_hbm.at[at], out_sems.at[chunk])

    for chunk in range(CHUNKS):
        fetch(chunk).start()
    for chunk in range(CHUNKS):
        fetch(chunk).wait()
        for source in range(chunk * sources // CHUNKS, (chunk + 1) * sources // CHUNKS):
            chan_scr[source * count : (source + 1) * count, :] = back_ref[source].astype(F32)
    for chunk in range(CHUNKS):
        for q_index in range(chunk * part // group, (chunk + 1) * part // group):
            q_from = jnp.where(flip == 1, q_count - 1 - q_index, q_index)
            turned = jnp.concatenate(
                [
                    chan_scr[pl.ds(tile * LANES * q_count + q_from, LANES, stride=q_count), :].T
                    for tile in range(channels // LANES)
                ],
                axis=1,
            )
            for r in range(group):
                row = q_index * group + jnp.where(flip == 1, group - 1 - r, r)
                out_ref[row] = (disco_ref[row] + turned[r * cols : (r + 1) * cols]).astype(BF16)
        give(chunk).start()
    for chunk in range(CHUNKS):
        give(chunk).wait()


def combine(back, local_part, flip, group):
    rows, cols, channels = local_part.shape
    q_count = rows // group
    anywhere = pl.BlockSpec(memory_space=pl.ANY)
    return pl.pallas_call(
        functools.partial(combine_kernel, group=group, q_count=q_count),
        in_specs=[
            pl.BlockSpec(memory_space=pltpu.SMEM),
            anywhere,
            pl.BlockSpec(memory_space=pltpu.VMEM),
        ],
        out_specs=anywhere,
        out_shape=jax.ShapeDtypeStruct(local_part.shape, BF16),
        scratch_shapes=[
            pltpu.VMEM(back.shape, BF16),
            pltpu.VMEM((channels * q_count, LANES), F32),
            pltpu.VMEM(local_part.shape, BF16),
            pltpu.SemaphoreType.DMA((CHUNKS,)),
            pltpu.SemaphoreType.DMA((CHUNKS,)),
        ],
        compiler_params=params(12 * MIB),
        name="combine",
    )(flip, back, local_part)


def shifted(block, axis, step):
    count = lax.axis_size(axis)
    return lax.ppermute(block, axis, [(i, (i + step) % count) for i in range(count)])


def corners_of(low, high, channels):
    def ends(start):
        blocks = [side.reshape(REACH, -1, channels)[:, start:][:, :REACH] for side in (low, high)]
        return jnp.concatenate(blocks, axis=0).reshape(2 * REACH * REACH, channels)

    return jnp.concatenate([shifted(ends(-REACH), "lon", 1), shifted(ends(0), "lon", -1)], axis=0)


def fourier_tables(order_count, points):
    order_list = jnp.arange(order_count, dtype=jnp.int32)[:, None]
    grid_pos = jnp.arange(points, dtype=jnp.int32)[None, :]
    angles = 2.0 * math.pi / points * (grid_pos * order_list % points).astype(F32)
    factor = jnp.where(order_list == 0, 1.0, 2.0).astype(F32)
    inverse = jnp.concatenate([jnp.cos(angles), -jnp.sin(angles)], axis=0)
    forward = jnp.concatenate([factor, factor], axis=0) * inverse
    return (forward.astype(BF16), inverse.astype(BF16))


def shards(pre_act, cotangent, spec_weight, disco_weight, disco_filter, support):
    lat_rows, lon_cols, channels = pre_act.shape
    lat_count = lax.axis_size("lat")
    lon_count = lax.axis_size("lon")
    devices = lat_count * lon_count
    band_index = lax.axis_index("lat")
    device_id = band_index * lon_count + lax.axis_index("lon")
    total_lat = lat_rows * lat_count
    total_lon = lon_cols * lon_count
    mode_count = spec_weight.shape[0]
    local = channels // devices
    group = LANES // lon_cols
    q_count = lat_rows // group
    flip = (2 * band_index >= lat_count).astype(jnp.int32).reshape(1)

    grad_pre, to_send, *edges = gradient(pre_act, cotangent, flip, devices, group)
    received = lax.all_to_all(to_send, ("lat", "lon"), 0, 0, tiled=True)

    lane = np.arange(total_lat // 2)
    lats = lane // lat_rows * lat_rows + lane % q_count * group + lane % lat_rows // q_count
    colatitude = math.pi / total_lat * (jnp.asarray(lats, F32) + 0.5)[None, :]
    order_vals = jnp.arange(mode_count, dtype=F32)[:, None]
    start = (
        0.5 * jnp.log((2.0 * order_vals + 1.0) / (4.0 * math.pi))
        + 0.5
        * (
            lax.lgamma(2.0 * order_vals + 1.0)
            - order_vals * math.log(4.0)
            - 2.0 * lax.lgamma(order_vals + 1.0)
        )
        + order_vals * jnp.log(jnp.sin(colatitude))
    )
    degree_norm = jnp.sqrt(jnp.maximum(4.0 * jnp.square(jnp.arange(mode_count, dtype=F32)) - 1.0, 1.0))
    norms = jnp.stack([degree_norm, 1.0 / degree_norm])
    both = mode_count * mode_count * total_lat < 2**25
    tables = legendre(norms, jnp.cos(colatitude), start, both)
    forward, inverse = fourier_tables(mode_count, total_lon)
    quad = 2.0 * math.pi / total_lon * (math.pi / total_lat) * jnp.sin(colatitude)
    weights = jnp.transpose(
        lax.dynamic_slice_in_dim(spec_weight, device_id * local, local, 2), (1, 2, 0)
    )
    offsets = jnp.arange(TAPS, dtype=jnp.int32) - REACH
    allowed = (jnp.abs(offsets)[None, None, :] <= support[:, :, None]).astype(F32)
    tap_coef = jnp.pad(disco_filter * allowed[None], ((0, 0), (REACH, REACH), (0, 0), (0, 0)))
    tap_coef = lax.dynamic_slice_in_dim(tap_coef, band_index * lat_rows, lat_rows + 2 * REACH, 1)
    taps = jnp.transpose(tap_coef, (1, 0, 2, 3)).reshape(lat_rows + 2 * REACH, -1)

    edges, tables = lax.optimization_barrier((edges, tables))
    first_rows, last_rows, west, east = edges
    sides = (
        shifted(last_rows, "lat", 1),
        shifted(first_rows, "lat", -1),
        shifted(east, "lon", 1),
        shifted(west, "lon", -1),
    )
    corners = corners_of(sides[0], sides[1], channels)
    received, sides = lax.optimization_barrier((received, sides))
    blocks = received.reshape(lat_count, lon_count, local * q_count, LANES)
    back = spectral(blocks, forward, inverse, tables, weights, quad, group)
    back, taps, corners = lax.optimization_barrier((back, taps, corners))
    returned = lax.all_to_all(
        back.reshape(devices, local * q_count, LANES), ("lat", "lon"), 0, 0, tiled=True
    )
    local_part = disco(taps, grad_pre, *sides, corners, disco_weight)
    return combine(returned, local_part, flip, group)


def solution(mesh):
    return jax.shard_map(
        shards,
        mesh=mesh,
        in_specs=(P("lat", "lon", None), P("lat", "lon", None), P(), P(), P(), P()),
        out_specs=P("lat", "lon", None),
        check_vma=False,
    )
```

```python
import functools
import math

import jax
import jax.numpy as jnp
import numpy as np
from jax import lax
from jax.experimental import pallas as pl
from jax.experimental.pallas import tpu as pltpu
from jax.sharding import PartitionSpec as P

REACH = 2
TAPS = 2 * REACH + 1
LANES = 128
PAD = 8
CHUNKS = 4
F32 = jnp.float32
BF16 = jnp.bfloat16
MIB = 1024 * 1024


def params(limit):
    return pltpu.CompilerParams(vmem_limit_bytes=limit)


def gelu_slope(pre_values):
    normal_cdf = 0.5 * (1.0 + lax.erf(pre_values * (1.0 / math.sqrt(2.0))))
    density = jnp.exp(-0.5 * pre_values * pre_values) * (1.0 / math.sqrt(2.0 * math.pi))
    return normal_cdf + pre_values * density


def grad_kernel(
    flip_ref, pre_hbm, cot_hbm, grad_hbm, send_hbm, first_ref, last_ref, west_ref, east_ref,
    pre_ref, cot_ref, grad_ref, send_ref, rows_scr, chan_scr, in_sems, out_sems, *, group, q_count,
):
    rows, cols, channels = pre_ref.shape
    part = rows // CHUNKS
    flip = flip_ref[0]

    def fetch(chunk):
        at = pl.ds(chunk * part, part)
        return [
            pltpu.make_async_copy(pre_hbm.at[at], pre_ref.at[at], in_sems.at[0, chunk]),
            pltpu.make_async_copy(cot_hbm.at[at], cot_ref.at[at], in_sems.at[1, chunk]),
        ]

    def keep(chunk):
        at = pl.ds(chunk * part, part)
        return pltpu.make_async_copy(grad_ref.at[at], grad_hbm.at[at], out_sems.at[0, chunk])

    def send(chunk):
        count = send_ref.shape[0] // CHUNKS
        at = pl.ds(chunk * count, count)
        return pltpu.make_async_copy(send_ref.at[at], send_hbm.at[at], out_sems.at[1, chunk])

    for chunk in range(CHUNKS):
        for copy in fetch(chunk):
            copy.start()
    for chunk in range(CHUNKS):
        for copy in fetch(chunk):
            copy.wait()
        for row in range(chunk * part, (chunk + 1) * part):
            grad = (cot_ref[row].astype(F32) * gelu_slope(pre_ref[row].astype(F32))).astype(BF16)
            grad_ref[row] = grad
            rows_scr[row] = grad.astype(F32)
        keep(chunk).start()
        for q_index in range(chunk * part // group, (chunk + 1) * part // group):
            q_out = jnp.where(flip == 1, q_count - 1 - q_index, q_index)
            slabs = []
            for r in range(group):
                slabs.append(rows_scr[q_index * group + jnp.where(flip == 1, group - 1 - r, r)])
            stacked = jnp.concatenate(slabs, axis=0)
            for tile in range(channels // LANES):
                turned = stacked[:, tile * LANES : (tile + 1) * LANES].T
                chan_scr[pl.ds(tile * LANES * q_count + q_out, LANES, stride=q_count), :] = turned
    dests, count = send_ref.shape[:2]
    for chunk in range(CHUNKS):
        for dest in range(chunk * dests // CHUNKS, (chunk + 1) * dests // CHUNKS):
            send_ref[dest] = chan_scr[dest * count : (dest + 1) * count, :].astype(BF16)
        send(chunk).start()
    for row in range(REACH):
        first_ref[row * cols : (row + 1) * cols, :] = grad_ref[row]
        last_ref[row * cols : (row + 1) * cols, :] = grad_ref[rows - REACH + row]
    for side in range(REACH):
        west_ref[side * rows : (side + 1) * rows, :] = rows_scr[:, side, :].astype(BF16)
        east_ref[side * rows : (side + 1) * rows, :] = rows_scr[:, cols - REACH + side, :].astype(BF16)
    for chunk in range(CHUNKS):
        keep(chunk).wait()
        send(chunk).wait()


def gradient(pre_act, cotangent, flip, devices, group):
    rows, cols, channels = pre_act.shape
    q_count = rows // group
    send = (devices, channels // devices * q_count, LANES)
    edges = [(REACH * cols, channels)] * 2 + [(REACH * rows, channels)] * 2
    anywhere = pl.BlockSpec(memory_space=pl.ANY)
    vmem = pl.BlockSpec(memory_space=pltpu.VMEM)
    return pl.pallas_call(
        functools.partial(grad_kernel, group=group, q_count=q_count),
        in_specs=[pl.BlockSpec(memory_space=pltpu.SMEM), anywhere, anywhere],
        out_specs=[anywhere, anywhere] + [vmem] * len(edges),
        out_shape=[jax.ShapeDtypeStruct(shape, BF16) for shape in (pre_act.shape, send, *edges)],
        scratch_shapes=[
            pltpu.VMEM(pre_act.shape, BF16),
            pltpu.VMEM(pre_act.shape, BF16),
            pltpu.VMEM(pre_act.shape, BF16),
            pltpu.VMEM(send, BF16),
            pltpu.VMEM(pre_act.shape, F32),
            pltpu.VMEM((channels * q_count, LANES), F32),
            pltpu.SemaphoreType.DMA((2, CHUNKS)),
            pltpu.SemaphoreType.DMA((2, CHUNKS)),
        ],
        compiler_params=params(60 * MIB),
        name="gradient",
    )(flip, pre_act, cotangent)


def legendre_kernel(norm_ref, cos_ref, start_ref, *refs, degrees, span):
    scr = refs[-1]
    pitch = degrees + PAD
    table_ref = refs[0]
    orders = table_ref.shape[0]
    groups = orders // 8
    first = pl.program_id(0) * orders
    cosine = jnp.broadcast_to(cos_ref[...], (8, LANES))
    sub = lax.broadcasted_iota(jnp.int32, (8, LANES), 0)
    order_vals = [(first + 8 * g + sub).astype(F32) for g in range(groups)]
    squares = [order * order for order in order_vals]
    zero = jnp.zeros((8, LANES), F32)

    def chunk(index, state):
        latest, earlier, coef_b, scale = (list(part) for part in state)
        factor = [jnp.exp(value) for value in scale]
        for step in range(span):
            degree = index * span + step
            deg_val = degree.astype(F32)
            norm = norm_ref[0, degree]
            inverse_norm = norm_ref[1, degree]
            for g in range(groups):
                gap = jnp.maximum(deg_val * deg_val - squares[g], 1.0)
                root = lax.rsqrt(gap)
                value = (root * norm) * (cosine * latest[g] - coef_b[g] * earlier[g])
                value = jnp.where(order_vals[g] == deg_val, 1.0, value)
                coef_b[g] = gap * root * inverse_norm
                earlier[g] = latest[g]
                latest[g] = value
                scr[pl.ds(g * 8 * pitch + degree, 8, stride=pitch), :] = value * factor[g]
        for g in range(groups):
            large = jnp.maximum(jnp.abs(latest[g]), jnp.abs(earlier[g])) > 2.0**20
            shrink = jnp.where(large, 2.0**-40, 1.0)
            latest[g] = latest[g] * shrink
            earlier[g] = earlier[g] * shrink
            scale[g] = scale[g] + jnp.where(large, 40.0 * math.log(2.0), 0.0)
        return (tuple(latest), tuple(earlier), tuple(coef_b), tuple(scale))

    starts = tuple(start_ref[8 * g : 8 * g + 8, :] for g in range(groups))
    zeros = (zero,) * groups
    lax.fori_loop(0, degrees // span, chunk, (zeros, zeros, zeros, starts))
    for order in range(orders):
        values = scr[order * pitch : order * pitch + degrees, :]
        table_ref[order] = values.astype(BF16)
        for turned_ref in refs[1:-1]:
            turned_ref[order] = values.T.astype(BF16)


def legendre(norms, cosine, start, both):
    orders, points = start.shape
    degrees = norms.shape[1]
    block = math.gcd(orders, 32)
    return pl.pallas_call(
        functools.partial(legendre_kernel, degrees=degrees, span=8),
        grid=(orders // block, points // LANES),
        in_specs=[
            pl.BlockSpec(memory_space=pltpu.SMEM),
            pl.BlockSpec((1, LANES), lambda i, j: (0, j)),
            pl.BlockSpec((block, LANES), lambda i, j: (i, j)),
        ],
        out_specs=[
            pl.BlockSpec((block, degrees, LANES), lambda i, j: (i, 0, j)),
            pl.BlockSpec((block, LANES, degrees), lambda i, j: (i, j, 0)),
        ][: 1 + both],
        out_shape=[
            jax.ShapeDtypeStruct((orders, degrees, points), BF16),
            jax.ShapeDtypeStruct((orders, points, degrees), BF16),
        ][: 1 + both],
        scratch_shapes=[pltpu.VMEM((block * (degrees + PAD), LANES), F32)],
        compiler_params=params(56 * MIB),
        cost_estimate=pl.CostEstimate(
            flops=4000 * orders * degrees * points,
            bytes_accessed=4 * orders * degrees * points,
            transcendentals=0,
        ),
        name="legendre",
    )(norms, cosine, start)


def spectral_kernel(
    recv_hbm, forward_ref, inverse_ref, weight_ref, quad_ref, *refs, group, q_count, unroll, count
):
    tables = refs[:count]
    back_hbm, recv_ref, back_ref, grid_scr, even_scr, odd_scr, north_scr, south_scr = refs[count : count + 8]
    slots = refs[count + 8 : 2 * count + 8]
    recv_sem, table_sems, back_sems = refs[2 * count + 8 :]
    sectors, bands = recv_ref.shape[:2]
    local, lats, lons = grid_scr.shape
    slot_count, orders_here, degrees, half = slots[0].shape
    tiles = half // LANES
    modes = forward_ref.shape[0]
    orders = modes // 2
    blocks = orders // orders_here
    pitch = modes + PAD
    band_rows = group * q_count
    width = LANES // group
    lane_group = lax.broadcasted_iota(jnp.int32, (q_count, LANES), 1) // width

    def fetch(block, slot):
        at = pl.ds(block * orders_here, orders_here)
        return [
            pltpu.make_async_copy(table.at[at], ring.at[slot], table_sems.at[kind, slot])
            for kind, (table, ring) in enumerate(zip(tables, slots))
        ]

    def give(chan):
        at = pl.ds(chan * q_count, q_count)
        return pltpu.make_async_copy(back_ref.at[:, :, at], back_hbm.at[:, :, at], back_sems.at[chan])

    def place(band, r):
        if band < bands // 2:
            return band * band_rows + r * q_count
        return lats // 2 + (bands - 1 - band) * band_rows + r * q_count

    def rolled(value, places):
        shift = places * width % LANES
        return value if shift == 0 else pltpu.roll(value, shift, 1)

    receive = pltpu.make_async_copy(recv_hbm, recv_ref, recv_sem)
    receive.start()
    for block in range(slot_count):
        for copy in fetch(block, block):
            copy.start()
    receive.wait()

    for chan in range(local):
        at = chan * q_count
        for band in range(bands):
            for unit in range(sectors // group):
                pieces = [
                    recv_ref[unit * group + k, band, at : at + q_count, :].astype(F32) for k in range(group)
                ]
                for r in range(group):
                    value = rolled(pieces[0], -r)
                    for k in range(1, group):
                        value = jnp.where(lane_group == k, rolled(pieces[k], k - r), value)
                    row = place(band, r)
                    grid_scr[chan, row : row + q_count, unit * LANES : (unit + 1) * LANES] = value.astype(BF16)
        spectrum = lax.dot_general(
            forward_ref[...], grid_scr[chan], (((1,), (1,)), ((), ())), preferred_element_type=F32
        )
        for tile in range(tiles):
            north = spectrum[:, tile * LANES : (tile + 1) * LANES]
            south = spectrum[:, half + tile * LANES : half + (tile + 1) * LANES]
            even_scr[tile, chan * pitch : chan * pitch + modes, :] = north + south
            odd_scr[tile, chan * pitch : chan * pitch + modes, :] = north - south

    def lines(tile, mode):
        if local == 1:
            return (tile, pl.ds(mode, 1), slice(None))
        return (tile, pl.ds(mode, local, stride=pitch), slice(None))

    def load(scr, mode):
        parts = [scr[lines(tile, mode)] for tile in range(tiles)]
        return parts[0] if tiles == 1 else jnp.concatenate(parts, axis=1)

    degree_lane = lax.broadcasted_iota(jnp.int32, (local, degrees), 1)
    real_w = weight_ref[0]
    imag_w = weight_ref[1]
    quad = quad_ref[...]

    def one_order(slot, order, index):
        table = slots[0][slot, index]
        even = (degree_lane + order) % 2 == 0
        stacked = jnp.concatenate(
            [
                load(even_scr, order),
                load(even_scr, orders + order),
                load(odd_scr, order),
                load(odd_scr, orders + order),
            ],
            axis=0,
        ).astype(BF16)
        if count == 2:
            analysed = jnp.dot(stacked, slots[1][slot, index], preferred_element_type=F32)
        else:
            analysed = lax.dot_general(
                stacked, table, (((1,), (1,)), ((), ())), preferred_element_type=F32
            )
        real_a = jnp.where(even, analysed[0:local], analysed[2 * local : 3 * local])
        imag_a = jnp.where(even, analysed[local : 2 * local], analysed[3 * local : 4 * local])
        real_m = real_w * real_a + imag_w * imag_a
        imag_m = real_w * imag_a - imag_w * real_a
        mixed = jnp.concatenate(
            [
                jnp.where(even, real_m, 0.0),
                jnp.where(even, imag_m, 0.0),
                jnp.where(even, 0.0, real_m),
                jnp.where(even, 0.0, imag_m),
            ],
            axis=0,
        ).astype(BF16)
        synth = jnp.dot(mixed, table, preferred_element_type=F32) * quad
        for part in range(2):
            even_part = synth[part * local : (part + 1) * local]
            odd_part = synth[(2 + part) * local : (3 + part) * local]
            for tile in range(tiles):
                lanes = slice(tile * LANES, (tile + 1) * LANES)
                where = lines(tile, part * orders + order)
                north_scr[where] = even_part[:, lanes] + odd_part[:, lanes]
                south_scr[where] = even_part[:, lanes] - odd_part[:, lanes]

    def one_block(block, carry):
        slot = block % slot_count
        for copy in fetch(block, slot):
            copy.wait()

        def several(index, inner_carry):
            for inner in range(unroll):
                at = index * unroll + inner
                one_order(slot, block * orders_here + at, at)
            return inner_carry

        lax.fori_loop(0, orders_here // unroll, several, 0)

        @pl.when(block + slot_count < blocks)
        def _():
            for copy in fetch(block + slot_count, slot):
                copy.start()

        return carry

    lax.fori_loop(0, blocks, one_block, 0)

    for chan in range(local):
        rows = slice(chan * pitch, chan * pitch + modes)
        profile = jnp.concatenate(
            [scr[tile, rows, :].astype(BF16) for scr in (north_scr, south_scr) for tile in range(tiles)],
            axis=1,
        )
        field = lax.dot_general(
            profile, inverse_ref[...], (((0,), (0,)), ((), ())), preferred_element_type=F32
        )
        at = chan * q_count
        for band in range(bands):
            for unit in range(sectors // group):
                pieces = []
                for r in range(group):
                    row = place(band, r)
                    pieces.append(field[row : row + q_count, unit * LANES : (unit + 1) * LANES])
                for k in range(group):
                    value = rolled(pieces[0], -k)
                    for r in range(1, group):
                        value = jnp.where(lane_group == r, rolled(pieces[r], r - k), value)
                    back_ref[unit * group + k, band, at : at + q_count, :] = value.astype(BF16)
        give(chan).start()
    for chan in range(local):
        give(chan).wait()


def spectral(received, forward, inverse, tables, weights, quad, group):
    rows = received.shape[2]
    local = weights.shape[1]
    q_count = rows // local
    orders, degrees, half = tables[0].shape
    lons = forward.shape[1]
    count = len(tables)
    block = max(1, min(orders, 2**19 // (degrees * half)))
    ring = min(orders // block, 4)
    tiles = half // LANES
    anywhere = pl.BlockSpec(memory_space=pl.ANY)
    vmem = pl.BlockSpec(memory_space=pltpu.VMEM)
    lines = pltpu.VMEM((tiles, local * (forward.shape[0] + PAD), LANES), F32)
    return pl.pallas_call(
        functools.partial(
            spectral_kernel, group=group, q_count=q_count, unroll=math.gcd(block, 32), count=count
        ),
        in_specs=[anywhere] + [vmem] * 4 + [anywhere] * count,
        out_specs=anywhere,
        out_shape=jax.ShapeDtypeStruct(received.shape, BF16),
        scratch_shapes=[
            pltpu.VMEM(received.shape, BF16),
            pltpu.VMEM(received.shape, BF16),
            pltpu.VMEM((local, 2 * half, lons), BF16),
            lines,
            lines,
            lines,
            lines,
        ]
        + [pltpu.VMEM((ring, block) + table.shape[1:], BF16) for table in tables]
        + [
            pltpu.SemaphoreType.DMA,
            pltpu.SemaphoreType.DMA((count, ring)),
            pltpu.SemaphoreType.DMA((local,)),
        ],
        compiler_params=params(50 * MIB),
        cost_estimate=pl.CostEstimate(
            flops=2**33 * orders // 128, bytes_accessed=4 * orders * degrees * half, transcendentals=0
        ),
        name="spectral",
    )(received, forward, inverse, weights, quad, *tables)


def disco_kernel(
    tap_ref, grad_ref, low_ref, high_ref, left_ref, right_ref, corner_ref, mix_ref, out_ref, padded, taps_scr
):
    step = pl.program_id(0)
    rows, cols, channels = grad_ref.shape
    rows_here = out_ref.shape[0]
    kernels = mix_ref.shape[0]
    halves = channels // LANES
    origin = 8

    @pl.when(step == 0)
    def _():
        for half in range(halves):
            lanes = slice(half * LANES, (half + 1) * LANES)
            padded[half, REACH : REACH + rows, origin : origin + cols, :] = grad_ref[:, :, lanes].astype(F32)
            for edge, (source, base) in enumerate(((low_ref, 0), (high_ref, REACH + rows))):
                values = source[:, lanes].astype(F32)
                for row in range(REACH):
                    padded[half, base + row, origin : origin + cols, :] = values[row * cols : (row + 1) * cols]
            for which in range(4):
                values = corner_ref[:, lanes].astype(F32)
                base = (0, REACH + rows)[which % 2]
                column = (origin - REACH, origin + cols)[which // 2]
                for row in range(REACH):
                    at = (which * REACH + row) * REACH
                    padded[half, base + row, column : column + REACH, :] = values[at : at + REACH]
            for source, column in ((left_ref, origin - REACH), (right_ref, origin + cols)):
                values = source[:, lanes].astype(F32)
                for side in range(REACH):
                    padded[half, REACH : REACH + rows, column + side, :] = values[side * rows : (side + 1) * rows]

    def one_row(row, carry):
        for half in range(halves):
            sums = [jnp.zeros((cols, LANES), F32) for _ in range(kernels)]
            for lat_tap in range(TAPS):
                source = step * rows_here + row + 2 * REACH - lat_tap
                for lon_tap in range(TAPS):
                    start = origin + REACH - lon_tap
                    slab = padded[half, source, start : start + cols, :]
                    for kernel in range(kernels):
                        tap = tap_ref[source, (kernel * TAPS + lat_tap) * TAPS + lon_tap]
                        sums[kernel] = sums[kernel] + tap * slab
            for kernel in range(kernels):
                taps_scr[kernel, row, :, half * LANES : (half + 1) * LANES] = sums[kernel].astype(BF16)
        return carry

    lax.fori_loop(0, rows_here, one_row, 0)
    total = None
    for kernel in range(kernels):
        flat = taps_scr[kernel].reshape(rows_here * cols, channels)
        term = lax.dot_general(
            flat, mix_ref[kernel], (((1,), (1,)), ((), ())), preferred_element_type=F32
        )
        total = term if total is None else total + term
    out_ref[...] = total.reshape(rows_here, cols, channels)


def disco(taps, grad, low, high, left, right, corners, mix):
    rows, cols, channels = grad.shape
    kernels = mix.shape[0]
    steps = 4

    def whole(shape):
        return pl.BlockSpec(shape, lambda i: (0,) * len(shape))

    return pl.pallas_call(
        disco_kernel,
        grid=(steps,),
        in_specs=[pl.BlockSpec(memory_space=pltpu.SMEM)]
        + [whole(value.shape) for value in (grad, low, high, left, right, corners, mix)],
        out_specs=pl.BlockSpec((rows // steps, cols, channels), lambda i: (i, 0, 0)),
        out_shape=jax.ShapeDtypeStruct(grad.shape, F32),
        scratch_shapes=[
            pltpu.VMEM((channels // LANES, rows + 2 * REACH, cols + 16, LANES), F32),
            pltpu.VMEM((kernels, rows // steps, cols, channels), BF16),
        ],
        compiler_params=params(14 * MIB),
        cost_estimate=pl.CostEstimate(
            flops=1000 * rows * cols * channels, bytes_accessed=8 * rows * cols * channels, transcendentals=0
        ),
        name="disco",
    )(taps, grad, low, high, left, right, corners, mix)


def combine_kernel(
    flip_ref, back_hbm, disco_ref, out_hbm, back_ref, chan_scr, out_ref, in_sems, out_sems, *, group, q_count
):
    rows, cols, channels = disco_ref.shape
    sources, count = back_ref.shape[:2]
    part = rows // CHUNKS
    flip = flip_ref[0]

    def fetch(chunk):
        at = pl.ds(chunk * (sources // CHUNKS), sources // CHUNKS)
        return pltpu.make_async_copy(back_hbm.at[at], back_ref.at[at], in_sems.at[chunk])

    def give(chunk):
        at = pl.ds(chunk * part, part)
        return pltpu.make_async_copy(out_ref.at[at], out_hbm.at[at], out_sems.at[chunk])

    for chunk in range(CHUNKS):
        fetch(chunk).start()
    for chunk in range(CHUNKS):
        fetch(chunk).wait()
        for source in range(chunk * sources // CHUNKS, (chunk + 1) * sources // CHUNKS):
            chan_scr[source * count : (source + 1) * count, :] = back_ref[source].astype(F32)
    for chunk in range(CHUNKS):
        for q_index in range(chunk * part // group, (chunk + 1) * part // group):
            q_from = jnp.where(flip == 1, q_count - 1 - q_index, q_index)
            turned = jnp.concatenate(
                [
                    chan_scr[pl.ds(tile * LANES * q_count + q_from, LANES, stride=q_count), :].T
                    for tile in range(channels // LANES)
                ],
                axis=1,
            )
            for r in range(group):
                row = q_index * group + jnp.where(flip == 1, group - 1 - r, r)
                out_ref[row] = (disco_ref[row] + turned[r * cols : (r + 1) * cols]).astype(BF16)
        give(chunk).start()
    for chunk in range(CHUNKS):
        give(chunk).wait()


def combine(back, local_part, flip, group):
    rows, cols, channels = local_part.shape
    q_count = rows // group
    anywhere = pl.BlockSpec(memory_space=pl.ANY)
    return pl.pallas_call(
        functools.partial(combine_kernel, group=group, q_count=q_count),
        in_specs=[
            pl.BlockSpec(memory_space=pltpu.SMEM),
            anywhere,
            pl.BlockSpec(memory_space=pltpu.VMEM),
        ],
        out_specs=anywhere,
        out_shape=jax.ShapeDtypeStruct(local_part.shape, BF16),
        scratch_shapes=[
            pltpu.VMEM(back.shape, BF16),
            pltpu.VMEM((channels * q_count, LANES), F32),
            pltpu.VMEM(local_part.shape, BF16),
            pltpu.SemaphoreType.DMA((CHUNKS,)),
            pltpu.SemaphoreType.DMA((CHUNKS,)),
        ],
        compiler_params=params(12 * MIB),
        name="combine",
    )(flip, back, local_part)


def shifted(block, axis, step):
    count = lax.axis_size(axis)
    return lax.ppermute(block, axis, [(i, (i + step) % count) for i in range(count)])


def corners_of(low, high, channels):
    def ends(start):
        blocks = [side.reshape(REACH, -1, channels)[:, start:][:, :REACH] for side in (low, high)]
        return jnp.concatenate(blocks, axis=0).reshape(2 * REACH * REACH, channels)

    return jnp.concatenate([shifted(ends(-REACH), "lon", 1), shifted(ends(0), "lon", -1)], axis=0)


def fourier_tables(order_count, points):
    order_list = jnp.arange(order_count, dtype=jnp.int32)[:, None]
    grid_pos = jnp.arange(points, dtype=jnp.int32)[None, :]
    angles = 2.0 * math.pi / points * (grid_pos * order_list % points).astype(F32)
    factor = jnp.where(order_list == 0, 1.0, 2.0).astype(F32)
    inverse = jnp.concatenate([jnp.cos(angles), -jnp.sin(angles)], axis=0)
    forward = jnp.concatenate([factor, factor], axis=0) * inverse
    return (forward.astype(BF16), inverse.astype(BF16))


def shards(pre_act, cotangent, spec_weight, disco_weight, disco_filter, support):
    lat_rows, lon_cols, channels = pre_act.shape
    lat_count = lax.axis_size("lat")
    lon_count = lax.axis_size("lon")
    devices = lat_count * lon_count
    band_index = lax.axis_index("lat")
    device_id = lax.axis_index("lon") * lat_count + band_index
    total_lat = lat_rows * lat_count
    total_lon = lon_cols * lon_count
    mode_count = spec_weight.shape[0]
    local = channels // devices
    group = LANES // lon_cols
    q_count = lat_rows // group
    flip = (2 * band_index >= lat_count).astype(jnp.int32).reshape(1)

    grad_pre, to_send, *edges = gradient(pre_act, cotangent, flip, devices, group)
    received = lax.all_to_all(to_send, ("lon", "lat"), 0, 0, tiled=True)

    lane = np.arange(total_lat // 2)
    lats = lane // lat_rows * lat_rows + lane % q_count * group + lane % lat_rows // q_count
    colatitude = math.pi / total_lat * (jnp.asarray(lats, F32) + 0.5)[None, :]
    order_vals = jnp.arange(mode_count, dtype=F32)[:, None]
    start = (
        0.5 * jnp.log((2.0 * order_vals + 1.0) / (4.0 * math.pi))
        + 0.5
        * (
            lax.lgamma(2.0 * order_vals + 1.0)
            - order_vals * math.log(4.0)
            - 2.0 * lax.lgamma(order_vals + 1.0)
        )
        + order_vals * jnp.log(jnp.sin(colatitude))
    )
    degree_norm = jnp.sqrt(jnp.maximum(4.0 * jnp.square(jnp.arange(mode_count, dtype=F32)) - 1.0, 1.0))
    norms = jnp.stack([degree_norm, 1.0 / degree_norm])
    both = mode_count * mode_count * total_lat < 2**25
    tables = legendre(norms, jnp.cos(colatitude), start, both)
    forward, inverse = fourier_tables(mode_count, total_lon)
    quad = 2.0 * math.pi / total_lon * (math.pi / total_lat) * jnp.sin(colatitude)
    weights = jnp.transpose(
        lax.dynamic_slice_in_dim(spec_weight, device_id * local, local, 2), (1, 2, 0)
    )
    offsets = jnp.arange(TAPS, dtype=jnp.int32) - REACH
    allowed = (jnp.abs(offsets)[None, None, :] <= support[:, :, None]).astype(F32)
    tap_coef = jnp.pad(disco_filter * allowed[None], ((0, 0), (REACH, REACH), (0, 0), (0, 0)))
    tap_coef = lax.dynamic_slice_in_dim(tap_coef, band_index * lat_rows, lat_rows + 2 * REACH, 1)
    taps = jnp.transpose(tap_coef, (1, 0, 2, 3)).reshape(lat_rows + 2 * REACH, -1)

    edges, tables = lax.optimization_barrier((edges, tables))
    first_rows, last_rows, west, east = edges
    sides = (
        shifted(last_rows, "lat", 1),
        shifted(first_rows, "lat", -1),
        shifted(east, "lon", 1),
        shifted(west, "lon", -1),
    )
    corners = corners_of(sides[0], sides[1], channels)
    received, sides = lax.optimization_barrier((received, sides))
    blocks = received.reshape(lon_count, lat_count, local * q_count, LANES)
    back = spectral(blocks, forward, inverse, tables, weights, quad, group)
    back, taps, corners = lax.optimization_barrier((back, taps, corners))
    returned = lax.all_to_all(
        back.reshape(devices, local * q_count, LANES), ("lon", "lat"), 0, 0, tiled=True
    )
    local_part = disco(taps, grad_pre, *sides, corners, disco_weight)
    return combine(returned, local_part, flip, group)


def solution(mesh):
    return jax.shard_map(
        shards,
        mesh=mesh,
        in_specs=(P("lat", "lon", None), P("lat", "lon", None), P(), P(), P(), P()),
        out_specs=P("lat", "lon", None),
        check_vma=False,
    )
```

```python
import functools
import math

import jax
import jax.numpy as jnp
import numpy as np
from jax import lax
from jax.experimental import pallas as pl
from jax.experimental.pallas import tpu as pltpu
from jax.sharding import PartitionSpec as P

REACH = 2
TAPS = 2 * REACH + 1
LANES = 128
PAD = 8
CHUNKS = 4
F32 = jnp.float32
BF16 = jnp.bfloat16
MIB = 1024 * 1024


def params(limit):
    return pltpu.CompilerParams(vmem_limit_bytes=limit)


def gelu_slope(pre_values):
    normal_cdf = 0.5 * (1.0 + lax.erf(pre_values * (1.0 / math.sqrt(2.0))))
    density = jnp.exp(-0.5 * pre_values * pre_values) * (1.0 / math.sqrt(2.0 * math.pi))
    return normal_cdf + pre_values * density


def grad_kernel(
    flip_ref, pre_hbm, cot_hbm, grad_hbm, send_hbm, first_hbm, last_hbm, west_hbm, east_hbm,
    pre_ref, cot_ref, grad_ref, send_ref, first_ref, last_ref, west_ref, east_ref, rows_scr, chan_scr,
    in_sems, out_sems, edge_sems, *, group, q_count,
):
    rows, cols, channels = pre_ref.shape
    part = rows // CHUNKS
    flip = flip_ref[0]

    def fetch(chunk):
        at = pl.ds(chunk * part, part)
        return [
            pltpu.make_async_copy(pre_hbm.at[at], pre_ref.at[at], in_sems.at[0, chunk]),
            pltpu.make_async_copy(cot_hbm.at[at], cot_ref.at[at], in_sems.at[1, chunk]),
        ]

    def keep(chunk):
        at = pl.ds(chunk * part, part)
        return pltpu.make_async_copy(grad_ref.at[at], grad_hbm.at[at], out_sems.at[0, chunk])

    def send(chunk):
        count = send_ref.shape[0] // CHUNKS
        at = pl.ds(chunk * count, count)
        return pltpu.make_async_copy(send_ref.at[at], send_hbm.at[at], out_sems.at[1, chunk])

    for chunk in range(CHUNKS):
        for copy in fetch(chunk):
            copy.start()
    for chunk in range(CHUNKS):
        for copy in fetch(chunk):
            copy.wait()
        for row in range(chunk * part, (chunk + 1) * part):
            grad = (cot_ref[row].astype(F32) * gelu_slope(pre_ref[row].astype(F32))).astype(BF16)
            grad_ref[row] = grad
            rows_scr[row] = grad.astype(F32)
        keep(chunk).start()
        for q_index in range(chunk * part // group, (chunk + 1) * part // group):
            q_out = jnp.where(flip == 1, q_count - 1 - q_index, q_index)
            slabs = []
            for r in range(group):
                slabs.append(rows_scr[q_index * group + jnp.where(flip == 1, group - 1 - r, r)])
            stacked = jnp.concatenate(slabs, axis=0)
            for tile in range(channels // LANES):
                turned = stacked[:, tile * LANES : (tile + 1) * LANES].T
                chan_scr[pl.ds(tile * LANES * q_count + q_out, LANES, stride=q_count), :] = turned
    for row in range(REACH):
        first_ref[row * cols : (row + 1) * cols, :] = grad_ref[row]
        last_ref[row * cols : (row + 1) * cols, :] = grad_ref[rows - REACH + row]
    for side in range(REACH):
        west_ref[side * rows : (side + 1) * rows, :] = rows_scr[:, side, :].astype(BF16)
        east_ref[side * rows : (side + 1) * rows, :] = rows_scr[:, cols - REACH + side, :].astype(BF16)
    pairs = ((first_ref, first_hbm), (last_ref, last_hbm), (west_ref, west_hbm), (east_ref, east_hbm))
    edges = [pltpu.make_async_copy(ref, hbm, edge_sems.at[at]) for at, (ref, hbm) in enumerate(pairs)]
    for edge in edges:
        edge.start()
    dests, count = send_ref.shape[:2]
    for chunk in range(CHUNKS):
        for dest in range(chunk * dests // CHUNKS, (chunk + 1) * dests // CHUNKS):
            send_ref[dest] = chan_scr[dest * count : (dest + 1) * count, :].astype(BF16)
        send(chunk).start()
    for chunk in range(CHUNKS):
        keep(chunk).wait()
        send(chunk).wait()
    for edge in edges:
        edge.wait()


def gradient(pre_act, cotangent, flip, devices, group):
    rows, cols, channels = pre_act.shape
    q_count = rows // group
    send = (devices, channels // devices * q_count, LANES)
    edges = [(REACH * cols, channels)] * 2 + [(REACH * rows, channels)] * 2
    anywhere = pl.BlockSpec(memory_space=pl.ANY)
    return pl.pallas_call(
        functools.partial(grad_kernel, group=group, q_count=q_count),
        in_specs=[pl.BlockSpec(memory_space=pltpu.SMEM), anywhere, anywhere],
        out_specs=[anywhere] * (2 + len(edges)),
        out_shape=[jax.ShapeDtypeStruct(shape, BF16) for shape in (pre_act.shape, send, *edges)],
        scratch_shapes=[
            pltpu.VMEM(pre_act.shape, BF16),
            pltpu.VMEM(pre_act.shape, BF16),
            pltpu.VMEM(pre_act.shape, BF16),
            pltpu.VMEM(send, BF16),
            *[pltpu.VMEM(edge, BF16) for edge in edges],
            pltpu.VMEM(pre_act.shape, F32),
            pltpu.VMEM((channels * q_count, LANES), F32),
            pltpu.SemaphoreType.DMA((2, CHUNKS)),
            pltpu.SemaphoreType.DMA((2, CHUNKS)),
            pltpu.SemaphoreType.DMA((4,)),
        ],
        compiler_params=params(60 * MIB),
        name="gradient",
    )(flip, pre_act, cotangent)


def legendre_kernel(norm_ref, cos_ref, start_ref, *refs, degrees, span):
    scr = refs[-1]
    pitch = degrees + PAD
    table_ref = refs[0]
    orders = table_ref.shape[0]
    groups = orders // 8
    first = pl.program_id(0) * orders
    cosine = jnp.broadcast_to(cos_ref[...], (8, LANES))
    sub = lax.broadcasted_iota(jnp.int32, (8, LANES), 0)
    order_vals = [(first + 8 * g + sub).astype(F32) for g in range(groups)]
    squares = [order * order for order in order_vals]
    zero = jnp.zeros((8, LANES), F32)

    def chunk(index, state):
        latest, earlier, coef_b, scale = (list(part) for part in state)
        factor = [jnp.exp(value) for value in scale]
        for step in range(span):
            degree = index * span + step
            deg_val = degree.astype(F32)
            norm = norm_ref[0, degree]
            inverse_norm = norm_ref[1, degree]
            for g in range(groups):
                gap = jnp.maximum(deg_val * deg_val - squares[g], 1.0)
                root = lax.rsqrt(gap)
                value = (root * norm) * (cosine * latest[g] - coef_b[g] * earlier[g])
                value = jnp.where(order_vals[g] == deg_val, 1.0, value)
                coef_b[g] = gap * root * inverse_norm
                earlier[g] = latest[g]
                latest[g] = value
                scr[pl.ds(g * 8 * pitch + degree, 8, stride=pitch), :] = value * factor[g]
        for g in range(groups):
            large = jnp.maximum(jnp.abs(latest[g]), jnp.abs(earlier[g])) > 2.0**20
            shrink = jnp.where(large, 2.0**-40, 1.0)
            latest[g] = latest[g] * shrink
            earlier[g] = earlier[g] * shrink
            scale[g] = scale[g] + jnp.where(large, 40.0 * math.log(2.0), 0.0)
        return (tuple(latest), tuple(earlier), tuple(coef_b), tuple(scale))

    starts = tuple(start_ref[8 * g : 8 * g + 8, :] for g in range(groups))
    zeros = (zero,) * groups
    lax.fori_loop(0, degrees // span, chunk, (zeros, zeros, zeros, starts))
    for order in range(orders):
        values = scr[order * pitch : order * pitch + degrees, :]
        table_ref[order] = values.astype(BF16)
        for turned_ref in refs[1:-1]:
            turned_ref[order] = values.T.astype(BF16)


def legendre(norms, cosine, start, both):
    orders, points = start.shape
    degrees = norms.shape[1]
    block = math.gcd(orders, 32)
    return pl.pallas_call(
        functools.partial(legendre_kernel, degrees=degrees, span=8),
        grid=(orders // block, points // LANES),
        in_specs=[
            pl.BlockSpec(memory_space=pltpu.SMEM),
            pl.BlockSpec((1, LANES), lambda i, j: (0, j)),
            pl.BlockSpec((block, LANES), lambda i, j: (i, j)),
        ],
        out_specs=[
            pl.BlockSpec((block, degrees, LANES), lambda i, j: (i, 0, j)),
            pl.BlockSpec((block, LANES, degrees), lambda i, j: (i, j, 0)),
        ][: 1 + both],
        out_shape=[
            jax.ShapeDtypeStruct((orders, degrees, points), BF16),
            jax.ShapeDtypeStruct((orders, points, degrees), BF16),
        ][: 1 + both],
        scratch_shapes=[pltpu.VMEM((block * (degrees + PAD), LANES), F32)],
        compiler_params=params(56 * MIB),
        cost_estimate=pl.CostEstimate(
            flops=4000 * orders * degrees * points,
            bytes_accessed=4 * orders * degrees * points,
            transcendentals=0,
        ),
        name="legendre",
    )(norms, cosine, start)


def spectral_kernel(
    recv_hbm, forward_ref, inverse_ref, weight_ref, quad_ref, *refs, group, q_count, unroll, count
):
    tables = refs[:count]
    back_hbm, recv_ref, back_ref, grid_scr, even_scr, odd_scr, north_scr, south_scr = refs[count : count + 8]
    slots = refs[count + 8 : 2 * count + 8]
    recv_sem, table_sems, back_sems = refs[2 * count + 8 :]
    sectors, bands = recv_ref.shape[:2]
    local, lats, lons = grid_scr.shape
    slot_count, orders_here, degrees, half = slots[0].shape
    tiles = half // LANES
    modes = forward_ref.shape[0]
    orders = modes // 2
    blocks = orders // orders_here
    pitch = modes + PAD
    band_rows = group * q_count
    width = LANES // group
    lane_group = lax.broadcasted_iota(jnp.int32, (q_count, LANES), 1) // width

    def fetch(block, slot):
        at = pl.ds(block * orders_here, orders_here)
        return [
            pltpu.make_async_copy(table.at[at], ring.at[slot], table_sems.at[kind, slot])
            for kind, (table, ring) in enumerate(zip(tables, slots))
        ]

    def give(chan):
        at = pl.ds(chan * q_count, q_count)
        return pltpu.make_async_copy(back_ref.at[:, :, at], back_hbm.at[:, :, at], back_sems.at[chan])

    def place(band, r):
        if band < bands // 2:
            return band * band_rows + r * q_count
        return lats // 2 + (bands - 1 - band) * band_rows + r * q_count

    def rolled(value, places):
        shift = places * width % LANES
        return value if shift == 0 else pltpu.roll(value, shift, 1)

    receive = pltpu.make_async_copy(recv_hbm, recv_ref, recv_sem)
    receive.start()
    for block in range(slot_count):
        for copy in fetch(block, block):
            copy.start()
    receive.wait()

    for chan in range(local):
        at = chan * q_count
        for band in range(bands):
            for unit in range(sectors // group):
                pieces = [
                    recv_ref[unit * group + k, band, at : at + q_count, :].astype(F32) for k in range(group)
                ]
                for r in range(group):
                    value = rolled(pieces[0], -r)
                    for k in range(1, group):
                        value = jnp.where(lane_group == k, rolled(pieces[k], k - r), value)
                    row = place(band, r)
                    grid_scr[chan, row : row + q_count, unit * LANES : (unit + 1) * LANES] = value.astype(BF16)
        spectrum = lax.dot_general(
            forward_ref[...], grid_scr[chan], (((1,), (1,)), ((), ())), preferred_element_type=F32
        )
        for tile in range(tiles):
            north = spectrum[:, tile * LANES : (tile + 1) * LANES]
            south = spectrum[:, half + tile * LANES : half + (tile + 1) * LANES]
            even_scr[tile, chan * pitch : chan * pitch + modes, :] = north + south
            odd_scr[tile, chan * pitch : chan * pitch + modes, :] = north - south

    def lines(tile, mode):
        if local == 1:
            return (tile, pl.ds(mode, 1), slice(None))
        return (tile, pl.ds(mode, local, stride=pitch), slice(None))

    def load(scr, mode):
        parts = [scr[lines(tile, mode)] for tile in range(tiles)]
        return parts[0] if tiles == 1 else jnp.concatenate(parts, axis=1)

    degree_lane = lax.broadcasted_iota(jnp.int32, (local, degrees), 1)
    real_w = weight_ref[0]
    imag_w = weight_ref[1]
    quad = quad_ref[...]

    def one_order(slot, order, index):
        table = slots[0][slot, index]
        even = (degree_lane + order) % 2 == 0
        stacked = jnp.concatenate(
            [
                load(even_scr, order),
                load(even_scr, orders + order),
                load(odd_scr, order),
                load(odd_scr, orders + order),
            ],
            axis=0,
        ).astype(BF16)
        if count == 2:
            analysed = jnp.dot(stacked, slots[1][slot, index], preferred_element_type=F32)
        else:
            analysed = lax.dot_general(
                stacked, table, (((1,), (1,)), ((), ())), preferred_element_type=F32
            )
        real_a = jnp.where(even, analysed[0:local], analysed[2 * local : 3 * local])
        imag_a = jnp.where(even, analysed[local : 2 * local], analysed[3 * local : 4 * local])
        real_m = real_w * real_a + imag_w * imag_a
        imag_m = real_w * imag_a - imag_w * real_a
        mixed = jnp.concatenate(
            [
                jnp.where(even, real_m, 0.0),
                jnp.where(even, imag_m, 0.0),
                jnp.where(even, 0.0, real_m),
                jnp.where(even, 0.0, imag_m),
            ],
            axis=0,
        ).astype(BF16)
        synth = jnp.dot(mixed, table, preferred_element_type=F32) * quad
        for part in range(2):
            even_part = synth[part * local : (part + 1) * local]
            odd_part = synth[(2 + part) * local : (3 + part) * local]
            for tile in range(tiles):
                lanes = slice(tile * LANES, (tile + 1) * LANES)
                where = lines(tile, part * orders + order)
                north_scr[where] = even_part[:, lanes] + odd_part[:, lanes]
                south_scr[where] = even_part[:, lanes] - odd_part[:, lanes]

    def one_block(block, carry):
        slot = block % slot_count
        for copy in fetch(block, slot):
            copy.wait()

        def several(index, inner_carry):
            for inner in range(unroll):
                at = index * unroll + inner
                one_order(slot, block * orders_here + at, at)
            return inner_carry

        lax.fori_loop(0, orders_here // unroll, several, 0)

        @pl.when(block + slot_count < blocks)
        def _():
            for copy in fetch(block + slot_count, slot):
                copy.start()

        return carry

    lax.fori_loop(0, blocks, one_block, 0)

    for chan in range(local):
        rows = slice(chan * pitch, chan * pitch + modes)
        profile = jnp.concatenate(
            [scr[tile, rows, :].astype(BF16) for scr in (north_scr, south_scr) for tile in range(tiles)],
            axis=1,
        )
        field = lax.dot_general(
            profile, inverse_ref[...], (((0,), (0,)), ((), ())), preferred_element_type=F32
        )
        at = chan * q_count
        for band in range(bands):
            for unit in range(sectors // group):
                pieces = []
                for r in range(group):
                    row = place(band, r)
                    pieces.append(field[row : row + q_count, unit * LANES : (unit + 1) * LANES])
                for k in range(group):
                    value = rolled(pieces[0], -k)
                    for r in range(1, group):
                        value = jnp.where(lane_group == r, rolled(pieces[r], r - k), value)
                    back_ref[unit * group + k, band, at : at + q_count, :] = value.astype(BF16)
        give(chan).start()
    for chan in range(local):
        give(chan).wait()


def spectral(received, forward, inverse, tables, weights, quad, group):
    rows = received.shape[2]
    local = weights.shape[1]
    q_count = rows // local
    orders, degrees, half = tables[0].shape
    lons = forward.shape[1]
    count = len(tables)
    block = max(1, min(orders, 2**19 // (degrees * half)))
    ring = min(orders // block, 4)
    tiles = half // LANES
    anywhere = pl.BlockSpec(memory_space=pl.ANY)
    vmem = pl.BlockSpec(memory_space=pltpu.VMEM)
    lines = pltpu.VMEM((tiles, local * (forward.shape[0] + PAD), LANES), F32)
    return pl.pallas_call(
        functools.partial(
            spectral_kernel, group=group, q_count=q_count, unroll=math.gcd(block, 32), count=count
        ),
        in_specs=[anywhere] + [vmem] * 4 + [anywhere] * count,
        out_specs=anywhere,
        out_shape=jax.ShapeDtypeStruct(received.shape, BF16),
        scratch_shapes=[
            pltpu.VMEM(received.shape, BF16),
            pltpu.VMEM(received.shape, BF16),
            pltpu.VMEM((local, 2 * half, lons), BF16),
            lines,
            lines,
            lines,
            lines,
        ]
        + [pltpu.VMEM((ring, block) + table.shape[1:], BF16) for table in tables]
        + [
            pltpu.SemaphoreType.DMA,
            pltpu.SemaphoreType.DMA((count, ring)),
            pltpu.SemaphoreType.DMA((local,)),
        ],
        compiler_params=params(50 * MIB),
        cost_estimate=pl.CostEstimate(
            flops=2**33 * orders // 128, bytes_accessed=4 * orders * degrees * half, transcendentals=0
        ),
        name="spectral",
    )(received, forward, inverse, weights, quad, *tables)


def disco_kernel(
    tap_ref, grad_ref, low_ref, high_ref, left_ref, right_ref, corner_ref, mix_ref, out_ref, padded, taps_scr
):
    step = pl.program_id(0)
    rows, cols, channels = grad_ref.shape
    rows_here = out_ref.shape[0]
    kernels = mix_ref.shape[0]
    halves = channels // LANES
    origin = 8

    @pl.when(step == 0)
    def _():
        for half in range(halves):
            lanes = slice(half * LANES, (half + 1) * LANES)
            padded[half, REACH : REACH + rows, origin : origin + cols, :] = grad_ref[:, :, lanes].astype(F32)
            for edge, (source, base) in enumerate(((low_ref, 0), (high_ref, REACH + rows))):
                values = source[:, lanes].astype(F32)
                for row in range(REACH):
                    padded[half, base + row, origin : origin + cols, :] = values[row * cols : (row + 1) * cols]
            for which in range(4):
                values = corner_ref[:, lanes].astype(F32)
                base = (0, REACH + rows)[which % 2]
                column = (origin - REACH, origin + cols)[which // 2]
                for row in range(REACH):
                    at = (which * REACH + row) * REACH
                    padded[half, base + row, column : column + REACH, :] = values[at : at + REACH]
            for source, column in ((left_ref, origin - REACH), (right_ref, origin + cols)):
                values = source[:, lanes].astype(F32)
                for side in range(REACH):
                    padded[half, REACH : REACH + rows, column + side, :] = values[side * rows : (side + 1) * rows]

    def one_row(row, carry):
        for half in range(halves):
            sums = [jnp.zeros((cols, LANES), F32) for _ in range(kernels)]
            for lat_tap in range(TAPS):
                source = step * rows_here + row + 2 * REACH - lat_tap
                for lon_tap in range(TAPS):
                    start = origin + REACH - lon_tap
                    slab = padded[half, source, start : start + cols, :]
                    for kernel in range(kernels):
                        tap = tap_ref[source, (kernel * TAPS + lat_tap) * TAPS + lon_tap]
                        sums[kernel] = sums[kernel] + tap * slab
            for kernel in range(kernels):
                taps_scr[kernel, row, :, half * LANES : (half + 1) * LANES] = sums[kernel].astype(BF16)
        return carry

    lax.fori_loop(0, rows_here, one_row, 0)
    total = None
    for kernel in range(kernels):
        flat = taps_scr[kernel].reshape(rows_here * cols, channels)
        term = lax.dot_general(
            flat, mix_ref[kernel], (((1,), (1,)), ((), ())), preferred_element_type=F32
        )
        total = term if total is None else total + term
    out_ref[...] = total.reshape(rows_here, cols, channels)


def disco(taps, grad, low, high, left, right, corners, mix):
    rows, cols, channels = grad.shape
    kernels = mix.shape[0]
    steps = 4

    def whole(shape):
        return pl.BlockSpec(shape, lambda i: (0,) * len(shape))

    return pl.pallas_call(
        disco_kernel,
        grid=(steps,),
        in_specs=[pl.BlockSpec(memory_space=pltpu.SMEM)]
        + [whole(value.shape) for value in (grad, low, high, left, right, corners, mix)],
        out_specs=pl.BlockSpec((rows // steps, cols, channels), lambda i: (i, 0, 0)),
        out_shape=jax.ShapeDtypeStruct(grad.shape, F32),
        scratch_shapes=[
            pltpu.VMEM((channels // LANES, rows + 2 * REACH, cols + 16, LANES), F32),
            pltpu.VMEM((kernels, rows // steps, cols, channels), BF16),
        ],
        compiler_params=params(14 * MIB),
        cost_estimate=pl.CostEstimate(
            flops=1000 * rows * cols * channels, bytes_accessed=8 * rows * cols * channels, transcendentals=0
        ),
        name="disco",
    )(taps, grad, low, high, left, right, corners, mix)


def combine_kernel(
    flip_ref, back_hbm, disco_ref, out_hbm, back_ref, chan_scr, out_ref, in_sems, out_sems, *, group, q_count
):
    rows, cols, channels = disco_ref.shape
    sources, count = back_ref.shape[:2]
    part = rows // CHUNKS
    flip = flip_ref[0]

    def fetch(chunk):
        at = pl.ds(chunk * (sources // CHUNKS), sources // CHUNKS)
        return pltpu.make_async_copy(back_hbm.at[at], back_ref.at[at], in_sems.at[chunk])

    def give(chunk):
        at = pl.ds(chunk * part, part)
        return pltpu.make_async_copy(out_ref.at[at], out_hbm.at[at], out_sems.at[chunk])

    for chunk in range(CHUNKS):
        fetch(chunk).start()
    for chunk in range(CHUNKS):
        fetch(chunk).wait()
        for source in range(chunk * sources // CHUNKS, (chunk + 1) * sources // CHUNKS):
            chan_scr[source * count : (source + 1) * count, :] = back_ref[source].astype(F32)
    for chunk in range(CHUNKS):
        for q_index in range(chunk * part // group, (chunk + 1) * part // group):
            q_from = jnp.where(flip == 1, q_count - 1 - q_index, q_index)
            turned = jnp.concatenate(
                [
                    chan_scr[pl.ds(tile * LANES * q_count + q_from, LANES, stride=q_count), :].T
                    for tile in range(channels // LANES)
                ],
                axis=1,
            )
            for r in range(group):
                row = q_index * group + jnp.where(flip == 1, group - 1 - r, r)
                out_ref[row] = (disco_ref[row] + turned[r * cols : (r + 1) * cols]).astype(BF16)
        give(chunk).start()
    for chunk in range(CHUNKS):
        give(chunk).wait()


def combine(back, local_part, flip, group):
    rows, cols, channels = local_part.shape
    q_count = rows // group
    anywhere = pl.BlockSpec(memory_space=pl.ANY)
    return pl.pallas_call(
        functools.partial(combine_kernel, group=group, q_count=q_count),
        in_specs=[
            pl.BlockSpec(memory_space=pltpu.SMEM),
            anywhere,
            pl.BlockSpec(memory_space=pltpu.VMEM),
        ],
        out_specs=anywhere,
        out_shape=jax.ShapeDtypeStruct(local_part.shape, BF16),
        scratch_shapes=[
            pltpu.VMEM(back.shape, BF16),
            pltpu.VMEM((channels * q_count, LANES), F32),
            pltpu.VMEM(local_part.shape, BF16),
            pltpu.SemaphoreType.DMA((CHUNKS,)),
            pltpu.SemaphoreType.DMA((CHUNKS,)),
        ],
        compiler_params=params(12 * MIB),
        name="combine",
    )(flip, back, local_part)


def shifted(block, axis, step):
    count = lax.axis_size(axis)
    return lax.ppermute(block, axis, [(i, (i + step) % count) for i in range(count)])


def corners_of(low, high, channels):
    def ends(start):
        blocks = [side.reshape(REACH, -1, channels)[:, start:][:, :REACH] for side in (low, high)]
        return jnp.concatenate(blocks, axis=0).reshape(2 * REACH * REACH, channels)

    return jnp.concatenate([shifted(ends(-REACH), "lon", 1), shifted(ends(0), "lon", -1)], axis=0)


def fourier_tables(order_count, points):
    order_list = jnp.arange(order_count, dtype=jnp.int32)[:, None]
    grid_pos = jnp.arange(points, dtype=jnp.int32)[None, :]
    angles = 2.0 * math.pi / points * (grid_pos * order_list % points).astype(F32)
    factor = jnp.where(order_list == 0, 1.0, 2.0).astype(F32)
    inverse = jnp.concatenate([jnp.cos(angles), -jnp.sin(angles)], axis=0)
    forward = jnp.concatenate([factor, factor], axis=0) * inverse
    return (forward.astype(BF16), inverse.astype(BF16))


def shards(pre_act, cotangent, spec_weight, disco_weight, disco_filter, support):
    lat_rows, lon_cols, channels = pre_act.shape
    lat_count = lax.axis_size("lat")
    lon_count = lax.axis_size("lon")
    devices = lat_count * lon_count
    band_index = lax.axis_index("lat")
    device_id = lax.axis_index("lon") * lat_count + band_index
    total_lat = lat_rows * lat_count
    total_lon = lon_cols * lon_count
    mode_count = spec_weight.shape[0]
    local = channels // devices
    group = LANES // lon_cols
    q_count = lat_rows // group
    flip = (2 * band_index >= lat_count).astype(jnp.int32).reshape(1)

    grad_pre, to_send, *edges = gradient(pre_act, cotangent, flip, devices, group)
    received = lax.all_to_all(to_send, ("lon", "lat"), 0, 0, tiled=True)

    lane = np.arange(total_lat // 2)
    lats = lane // lat_rows * lat_rows + lane % q_count * group + lane % lat_rows // q_count
    colatitude = math.pi / total_lat * (jnp.asarray(lats, F32) + 0.5)[None, :]
    order_vals = jnp.arange(mode_count, dtype=F32)[:, None]
    start = (
        0.5 * jnp.log((2.0 * order_vals + 1.0) / (4.0 * math.pi))
        + 0.5
        * (
            lax.lgamma(2.0 * order_vals + 1.0)
            - order_vals * math.log(4.0)
            - 2.0 * lax.lgamma(order_vals + 1.0)
        )
        + order_vals * jnp.log(jnp.sin(colatitude))
    )
    degree_norm = jnp.sqrt(jnp.maximum(4.0 * jnp.square(jnp.arange(mode_count, dtype=F32)) - 1.0, 1.0))
    norms = jnp.stack([degree_norm, 1.0 / degree_norm])
    both = mode_count * mode_count * total_lat < 2**25
    tables = legendre(norms, jnp.cos(colatitude), start, both)
    forward, inverse = fourier_tables(mode_count, total_lon)
    quad = 2.0 * math.pi / total_lon * (math.pi / total_lat) * jnp.sin(colatitude)
    weights = jnp.transpose(
        lax.dynamic_slice_in_dim(spec_weight, device_id * local, local, 2), (1, 2, 0)
    )
    offsets = jnp.arange(TAPS, dtype=jnp.int32) - REACH
    allowed = (jnp.abs(offsets)[None, None, :] <= support[:, :, None]).astype(F32)
    tap_coef = jnp.pad(disco_filter * allowed[None], ((0, 0), (REACH, REACH), (0, 0), (0, 0)))
    tap_coef = lax.dynamic_slice_in_dim(tap_coef, band_index * lat_rows, lat_rows + 2 * REACH, 1)
    taps = jnp.transpose(tap_coef, (1, 0, 2, 3)).reshape(lat_rows + 2 * REACH, -1)

    edges, tables = lax.optimization_barrier((edges, tables))
    first_rows, last_rows, west, east = edges
    sides = (
        shifted(last_rows, "lat", 1),
        shifted(first_rows, "lat", -1),
        shifted(east, "lon", 1),
        shifted(west, "lon", -1),
    )
    corners = corners_of(sides[0], sides[1], channels)
    received, sides = lax.optimization_barrier((received, sides))
    blocks = received.reshape(lon_count, lat_count, local * q_count, LANES)
    back = spectral(blocks, forward, inverse, tables, weights, quad, group)
    back, taps, corners = lax.optimization_barrier((back, taps, corners))
    returned = lax.all_to_all(
        back.reshape(devices, local * q_count, LANES), ("lon", "lat"), 0, 0, tiled=True
    )
    local_part = disco(taps, grad_pre, *sides, corners, disco_weight)
    return combine(returned, local_part, flip, group)


def solution(mesh):
    return jax.shard_map(
        shards,
        mesh=mesh,
        in_specs=(P("lat", "lon", None), P("lat", "lon", None), P(), P(), P(), P()),
        out_specs=P("lat", "lon", None),
        check_vma=False,
    )
```
